128 devices in a mesh: ctx: 16 (over x_lo, y, core), head: 8 (over z, x_hi).
Axes of the slice: x: 4 (x_hi: 2, x_lo: 2; x = x_hi * 2 + x_lo), y: 4, z: 4, core: 2. Of those that a mesh axis runs over, the one named last changes fastest.
Arguments:
- queries: bfloat16 [1024, 16384], P('ctx', 'head'), may hold values from -8 to 8, as said below
- key_cache: bfloat16 [16384, 1024], P('ctx', 'head'), may hold values from -8 to 8, as said below
- value_cache: bfloat16 [16384, 1024], P('ctx', 'head'), may hold values from -5 to 5
- out_weight: bfloat16 [16384, 16384], P('head', 'ctx'), may hold values from -0.046875 to 0.046875
Outputs:
- projected: bfloat16 [1024, 16384], P('head', 'ctx')
The draws below stay inside these ranges and needn't reach their ends.
Inputs may be any that keep to these rules, and one draw needn't show every extreme that they name: `queries`: entries of order one. `key_cache`: entries of order one.
All inputs are finite; a program needn't handle non-finite values.
Results may differ from the reference program's by a relative error of at most 0.012.
Values may be sent and summed in bfloat16 or wider, within the bound.
A program may use at most 320 MiB of HBM per device.

```python
import math
import jax
import jax.numpy as jnp
from jax import lax

D = 16384
QH = 128
KV = 8
HD = 128
GROUP = 16
TOK_DEV = 64
CACHE_DEV = 1024
CACHE_RUN = 64
TURN = 1024
CACHE = 16384
N_CTX = 16


def draw_queries(key, part):
    key = jax.random.fold_in(key, 1)
    base = 2.5 * jnp.clip(jax.random.normal(key, (TURN, QH * HD), jnp.float32), -3.2, 3.2)
    return base.astype(jnp.bfloat16)


def draw_key_cache(key, part):
    key = jax.random.fold_in(key, 2)
    base = jnp.clip(jax.random.normal(key, (CACHE, KV * HD), jnp.float32), -8.0, 8.0)
    return base.astype(jnp.bfloat16)


def level_of(key, extent, shards, low, largest):
    def one(position, shards_of):
        steps = jax.random.uniform(jax.random.fold_in(jax.random.fold_in(key, 6), position), (shards_of,), jnp.float32, low / len(shards), largest / len(shards))
        return jnp.repeat(jnp.exp(steps), extent[position] // shards_of).reshape((-1,) + (1,) * (len(extent) - position - 1))

    gain = one(*shards[0])
    for cut in shards[1:]:
        gain = gain * one(*cut)
    return gain


def bell_draw(key, dims, scale, limit, pieces=(), kind=jnp.bfloat16):
    entries = scale * jax.random.normal(key, dims, jnp.float32)
    if pieces:
        entries = entries * level_of(key, dims, pieces, -0.22, 0.18)
    return jnp.clip(entries, -limit, limit).astype(kind)


def setup_inputs(seed: int = 0) -> dict:
    key_list = jax.random.split(jax.random.key(seed), 5)
    return {
        "queries": draw_queries(jax.random.fold_in(key_list[4], 71), 0),
        "key_cache": draw_key_cache(jax.random.fold_in(key_list[4], 71), 0),
        "value_cache": bell_draw(key_list[2], (CACHE, KV * HD), 1.0, 5.0, ((0, 16), (1, 8))),
        "out_weight": bell_draw(key_list[3], (QH * HD, D), (QH * HD) ** -0.5, 0.046875, ((0, 8), (1, 16))),
    }


NEG = -1e+30

def positions_of(row_ids, per_device, devices, run_len):
    device = row_ids // per_device
    within = row_ids % per_device
    return (within // run_len * devices + device) * run_len + within % run_len

def attend_one(block, query_pos, head_keys, head_values, key_pos):
    scores = jnp.einsum('tgd,cd->tgc', block.astype(jnp.float32), head_keys.astype(jnp.float32), precision=lax.Precision.HIGHEST) * (1.0 / math.sqrt(HD))
    visible = key_pos[None, None, :] <= query_pos[:, None, None]
    scores = jnp.where(visible, scores, NEG)
    row_max = lax.optimization_barrier(jnp.max(scores, axis=-1, keepdims=True))
    weights = jnp.where(visible, jnp.exp(scores - row_max), 0.0)
    weight_sum = lax.optimization_barrier(jnp.sum(weights, axis=-1))
    rounded = weights.astype(jnp.bfloat16)
    summed = jnp.einsum('tgc,cd->tgd', rounded.astype(jnp.float32), head_values.astype(jnp.float32), precision=lax.Precision.HIGHEST)
    return (summed / weight_sum[..., None]).astype(jnp.bfloat16)

def reference(queries, key_cache, value_cache, out_weight):
    row_ids = jnp.arange(CACHE, dtype=jnp.int32)
    key_pos = positions_of(row_ids, CACHE_DEV, N_CTX, CACHE_RUN)
    blocks = TURN // TOK_DEV
    query_pos = (CACHE - TURN + jnp.arange(TURN, dtype=jnp.int32)).reshape(blocks, TOK_DEV)
    grouped = queries.reshape(blocks, TOK_DEV, KV, GROUP, HD).transpose(2, 0, 1, 3, 4)
    key_heads = key_cache.reshape(CACHE, KV, HD).transpose(1, 0, 2)
    value_heads = value_cache.reshape(CACHE, KV, HD).transpose(1, 0, 2)

    def per_head(item):
        head_query, head_keys, head_values = item

        def per_block(inner):
            block, positions = inner
            return attend_one(block, positions, head_keys, head_values, key_pos)
        return lax.map(per_block, (head_query, query_pos))
    attended = lax.map(per_head, (grouped, key_heads, value_heads))
    attended = attended.transpose(1, 2, 0, 3, 4).reshape(TURN, QH * HD)
    return jnp.dot(attended, out_weight, preferred_element_type=jnp.float32).astype(jnp.bfloat16)
```

```python
import math

import jax
import jax.numpy as jnp
from jax import lax
from jax.experimental import pallas as pl
from jax.experimental.pallas import tpu as pltpu
from jax.sharding import PartitionSpec as P

HD = 128
RUN = 64
NEG = -1e30
ROWS = 256
KEYS = 512
LOG2E = math.log2(math.e)
MESH = pl.DeviceIdType.MESH

S_KV = 0
S_Q = 14
S_O = 15
S_STAT = 16
S_ATT = 17
S_FAR = 34
S_NEAR = 38
S_SIDE = 42
S_COUNT = 43


def device_at(x, y, core):
    return x * 8 + y * 2 + core


def kernel(
    q_ref, k_ref, v_ref, w_hbm, out_ref,
    q_t, kv, acc, mrow, lrow, o_send, s_send, o_recv, s_recv, att, w,
    far, far_in, near, near_in, side, side_in, total, w_sem, send, recv,
):
    c, h = lax.axis_index("ctx"), lax.axis_index("head")
    x, y, core = c // 8, (c // 2) % 4, c % 2
    z, e = h // 2, h % 2
    scale = LOG2E / math.sqrt(HD)

    to_core = (device_at(x, y, 1 - core), h)
    to_up = (device_at(x, (y + 1) % 4, core), h)
    to_down = (device_at(x, (y + 3) % 4, core), h)
    to_x = (device_at(1 - x, y, core), h)
    to_zup = (c, ((z + 1) % 4) * 2 + e)
    to_zdown = (c, ((z + 3) % 4) * 2 + e)
    to_side = (c, z * 2 + 1 - e)
    partners = (to_core, to_up, to_down, to_x, to_zup, to_zdown, to_side)

    def remote(src, dst, number, where):
        return pltpu.make_async_remote_copy(
            src_ref=src, dst_ref=dst, send_sem=send.at[number], recv_sem=recv.at[number],
            device_id=where, device_id_type=MESH,
        )

    w_copy = pltpu.make_async_copy(w_hbm, w, w_sem)
    w_copy.start()
    barrier = pltpu.get_barrier_semaphore()
    for partner in partners:
        pl.semaphore_signal(barrier, inc=1, device_id=partner, device_id_type=MESH)

    for r in range(4):
        half, group = r // 2, r % 2
        heads = [
            q_ref[half * 32 : half * 32 + 32, (group * 8 + i) * HD : (group * 8 + i + 1) * HD]
            for i in range(8)
        ]
        block = jnp.concatenate(heads, axis=0).astype(jnp.float32)
        q_t[r] = block.T.astype(jnp.bfloat16)
    for half in range(2):
        kv[half, 0:KEYS] = k_ref[half * KEYS : (half + 1) * KEYS]
        for b in range(4):
            start = half * KEYS + b * HD
            piece = v_ref[start : start + HD].astype(jnp.float32)
            kv[half, KEYS + b * HD : KEYS + (b + 1) * HD] = piece.T.astype(jnp.bfloat16)
    for r in range(8):
        acc[r] = jnp.zeros((HD, ROWS), jnp.float32)
        mrow[r] = jnp.full((1, ROWS), NEG, jnp.float32)
        lrow[r] = jnp.zeros((1, ROWS), jnp.float32)

    pl.semaphore_wait(barrier, len(partners))

    def kv_copy(number, source, target, where):
        return remote(kv.at[source], kv.at[target], S_KV + number, where)

    own_up = [kv_copy(0 + i, i, 12 + i, to_up) for i in range(2)]
    own_down = [kv_copy(2 + i, i, 4 + i, to_down) for i in range(2)]
    own_core = [kv_copy(4 + i, i, 2 + i, to_core) for i in range(2)]
    pass_12 = kv_copy(6, 12, 14, to_core)
    pass_4 = kv_copy(7, 4, 6, to_core)
    pass_13 = kv_copy(8, 13, 15, to_core)
    pass_5 = kv_copy(9, 5, 7, to_core)
    on_up = kv_copy(10, 12, 8, to_up)
    on_down = kv_copy(11, 5, 9, to_down)
    pass_8 = kv_copy(12, 8, 10, to_core)
    pass_9 = kv_copy(13, 9, 11, to_core)
    q_copy = remote(q_t.at[0:4], q_t.at[4:8], S_Q, to_x)
    o_copy = remote(o_send, o_recv, S_O, to_x)
    s_copy = remote(s_send, s_recv, S_STAT, to_x)

    q_copy.start()
    for i in range(2):
        own_up[i].start()
        own_down[i].start()
        own_core[i].start()

    def finish_neighbour():
        row = lax.broadcasted_iota(jnp.int32, (8, ROWS), 0)
        for r in range(4):
            o_send[r] = (acc[4 + r] / lrow[4 + r]).astype(jnp.bfloat16)
            s_send[r] = jnp.where(row == 0, mrow[4 + r], lrow[4 + r])
        o_copy.start()
        s_copy.start()

    def unit(u, carry):
        @pl.when(u == 2)
        def _():
            own_core[0].wait_recv()
            own_core[1].wait_recv()

        @pl.when(u == 4)
        def _():
            q_copy.wait_recv()

        @pl.when(u == 8)
        def _():
            own_up[0].wait_recv()
            on_up.start()
            pass_12.start()
            own_down[0].wait_recv()
            pass_4.start()

        @pl.when(u == 10)
        def _():
            pass_12.wait_recv()
            pass_4.wait_recv()

        @pl.when(u == 16)
        def _():
            own_down[1].wait_recv()
            on_down.start()
            pass_5.start()
            own_up[1].wait_recv()
            pass_13.start()

        @pl.when(u == 18)
        def _():
            pass_13.wait_recv()
            pass_5.wait_recv()

        @pl.when(u == 24)
        def _():
            on_up.wait_recv()
            pass_8.start()
            on_down.wait_recv()
            pass_9.start()

        @pl.when(u == 26)
        def _():
            pass_8.wait_recv()
            pass_9.wait_recv()

        @pl.when(u == 28)
        def _():
            finish_neighbour()

        stage, v = u // 8, u % 8
        i = v % 4
        group = jnp.where(stage == 3, 1 - v // 4, v // 4)
        middle = 12 - 8 * (i % 2) + 2 * (i // 2) + stage - 1
        slot = jnp.where(stage == 0, i, jnp.where(stage == 3, 8 + i, middle))
        holder_core = jnp.where((slot // 2) % 2 == 1, 1 - core, core)
        holder = device_at(x, (y + slot // 4) % 4, holder_core)
        key_base = jnp.where(slot % 2 == 1, holder * RUN, -(1 << 20))
        asker = device_at(jnp.where(group == 1, 1 - x, x), y, core)
        key_rel = key_base - asker * RUN + lax.broadcasted_iota(jnp.int32, (RUN, ROWS), 0)
        token = lax.broadcasted_iota(jnp.int32, (RUN, ROWS), 1) % 32

        keys = kv[slot, 0:KEYS]
        values = jnp.concatenate(
            [kv[slot, KEYS + b * HD : KEYS + (b + 1) * HD] for b in range(4)], axis=1
        )

        def scores_of(r):
            return jnp.dot(keys, q_t[group * 4 + r], preferred_element_type=jnp.float32) * scale

        scores = scores_of(0)
        for r in range(4):
            row = group * 4 + r
            later = scores_of(r + 1) if r < 3 else None
            tail = jnp.where(key_rel <= token + (r // 2) * 32, scores[KEYS - RUN :], NEG)
            scores = jnp.concatenate([scores[: KEYS - RUN], tail], axis=0)
            old = mrow[row]
            new = jnp.maximum(old, jnp.max(scores, axis=0, keepdims=True))
            weights = jnp.exp2(scores - new)
            fade = jnp.exp2(old - new)
            mrow[row] = new
            lrow[row] = lrow[row] * fade + jnp.sum(weights, axis=0, keepdims=True)
            acc[row] = acc[row] * fade + jnp.dot(
                values, weights.astype(jnp.bfloat16), preferred_element_type=jnp.float32
            )
            scores = later
        return carry

    lax.fori_loop(0, 32, unit, 0)

    o_copy.wait_recv()
    s_copy.wait_recv()
    for r in range(4):
        half, group = r // 2, r % 2
        m_b, l_b = s_recv[r, 0:1], s_recv[r, 1:2]
        new = jnp.maximum(mrow[r], m_b)
        fade_a = jnp.exp2(mrow[r] - new)
        fade_b = jnp.exp2(m_b - new) * l_b
        summed = acc[r] * fade_a + o_recv[r].astype(jnp.float32) * fade_b
        done = (summed / (lrow[r] * fade_a + fade_b)).T.astype(jnp.bfloat16)
        for i in range(8):
            head = group * 8 + i
            att[0, 0, half * 32 : half * 32 + 32, head * HD : (head + 1) * HD] = done[
                i * 32 : i * 32 + 32
            ]

    def att_copy(number, source, target, where):
        return remote(att.at[source, 0], att.at[target, 0], S_ATT + number, where)

    def att_core(number, slot):
        return remote(att.at[slot, 0], att.at[slot, 1], S_ATT + number, to_core)

    def att_half(number, source, target, half, where):
        rows = pl.ds(half * 32, 32)
        return remote(
            att.at[source, 0, rows], att.at[target, 0, rows], S_ATT + number, where
        )

    a_core = [att_core(slot, slot) for slot in range(8)]
    a_x = att_copy(8, 0, 4, to_x)
    a_up = [att_copy(9, 0, 3, to_up), att_copy(10, 4, 7, to_up)]
    a_down = [att_copy(11, 0, 1, to_down), att_copy(12, 4, 5, to_down)]
    a_up2 = [att_half(13, 3, 2, 0, to_up), att_half(14, 7, 6, 0, to_up)]
    a_down2 = [att_half(15, 1, 2, 1, to_down), att_half(16, 5, 6, 1, to_down)]

    a_x.start()
    a_up[0].start()
    a_down[0].start()
    a_core[0].start()
    a_x.wait_recv()
    a_up[1].start()
    a_down[1].start()
    a_core[4].start()
    for plane in range(2):
        a_up[plane].wait_recv()
        a_up2[plane].start()
        a_core[plane * 4 + 3].start()
        a_down[plane].wait_recv()
        a_down2[plane].start()
        a_core[plane * 4 + 1].start()
    for plane in range(2):
        a_up2[plane].wait_recv()
        a_down2[plane].wait_recv()
        a_core[plane * 4 + 2].start()
    w_copy.wait()
    for slot in range(8):
        a_core[slot].wait_recv()

    cols = w.shape[1] // 2

    def project(distance, side_of, part):
        target = ((z + distance) % 4) * 2 + side_of
        slot = jnp.where(target // 4 == x, 0, 4) + (target % 4 - y + 4) % 4
        block = jnp.concatenate([att[slot, core], att[slot, 1 - core]], axis=0)
        return jnp.dot(
            block, w[:, part * cols : (part + 1) * cols], preferred_element_type=jnp.float32
        )

    def far_copy(way, s):
        return remote(
            far.at[way, s], far_in.at[way, s], S_FAR + way * 2 + s, (to_zup, to_zdown)[way]
        )

    def near_copy(way, s):
        return remote(
            near.at[way, s], near_in.at[way, s], S_NEAR + way * 2 + s, (to_zup, to_zdown)[way]
        )

    side_copy = remote(side, side_in, S_SIDE, to_side)

    def far_step(s, carry):
        for way in range(2):
            far[way, s] = project(2, s, way).astype(jnp.bfloat16)
            far_copy(way, s).start()
        return carry

    lax.fori_loop(0, 2, far_step, 0)
    for way in range(2):

        def near_step(s, carry):
            other = 1 - way
            near[way, s, :, other * cols : (other + 1) * cols] = project(
                1 + 2 * way, s, other
            ).astype(jnp.bfloat16)
            far_copy(way, s).wait_recv()
            near[way, s, :, way * cols : (way + 1) * cols] = (
                project(1 + 2 * way, s, way) + far_in[way, s].astype(jnp.float32)
            ).astype(jnp.bfloat16)
            near_copy(way, s).start()
            return carry

        lax.fori_loop(0, 2, near_step, 0)

    def last_step(turn, carry):
        s = jnp.where(turn == 0, 1 - e, e)
        for part in range(2):
            total[:, part * cols : (part + 1) * cols] = project(0, s, part)
        near_copy(0, s).wait_recv()
        near_copy(1, s).wait_recv()
        total[...] = (
            total[...] + near_in[0, s].astype(jnp.float32) + near_in[1, s].astype(jnp.float32)
        )

        @pl.when(turn == 0)
        def _():
            side[...] = total[...].astype(jnp.bfloat16)
            side_copy.start()

        return carry

    lax.fori_loop(0, 2, last_step, 0)
    side_copy.wait_recv()
    out_ref[...] = (total[...] + side_in[...].astype(jnp.float32)).astype(jnp.bfloat16)

    sent = own_up + own_down + own_core + [pass_12, pass_4, pass_13, pass_5, on_up, on_down]
    sent += [pass_8, pass_9, q_copy, o_copy, s_copy, a_x, side_copy]
    sent += a_core + a_up + a_down + a_up2 + a_down2
    sent += [far_copy(way, s) for way in range(2) for s in range(2)]
    sent += [near_copy(way, s) for way in range(2) for s in range(2)]
    for copy in sent:
        copy.wait_send()


def body(queries, key_cache, value_cache, out_weight):
    tokens, width = queries.shape
    cols = out_weight.shape[1]
    vmem = pl.BlockSpec(memory_space=pltpu.VMEM)
    bf16, f32 = jnp.bfloat16, jnp.float32
    return pl.pallas_call(
        kernel,
        out_shape=jax.ShapeDtypeStruct((2 * tokens, cols), bf16),
        in_specs=[vmem, vmem, vmem, pl.BlockSpec(memory_space=pl.ANY)],
        out_specs=vmem,
        scratch_shapes=[
            pltpu.VMEM((8, HD, ROWS), bf16),
            pltpu.VMEM((16, 2 * KEYS, HD), bf16),
            pltpu.VMEM((8, HD, ROWS), f32),
            pltpu.VMEM((8, 1, ROWS), f32),
            pltpu.VMEM((8, 1, ROWS), f32),
            pltpu.VMEM((4, HD, ROWS), bf16),
            pltpu.VMEM((4, 8, ROWS), f32),
            pltpu.VMEM((4, HD, ROWS), bf16),
            pltpu.VMEM((4, 8, ROWS), f32),
            pltpu.VMEM((8, 2, tokens, width), bf16),
            pltpu.VMEM(out_weight.shape, bf16),
            pltpu.VMEM((2, 2, 2 * tokens, cols // 2), bf16),
            pltpu.VMEM((2, 2, 2 * tokens, cols // 2), bf16),
            pltpu.VMEM((2, 2, 2 * tokens, cols), bf16),
            pltpu.VMEM((2, 2, 2 * tokens, cols), bf16),
            pltpu.VMEM((2 * tokens, cols), bf16),
            pltpu.VMEM((2 * tokens, cols), bf16),
            pltpu.VMEM((2 * tokens, cols), f32),
            pltpu.SemaphoreType.DMA,
            pltpu.SemaphoreType.DMA((S_COUNT,)),
            pltpu.SemaphoreType.DMA((S_COUNT,)),
        ],
        compiler_params=pltpu.CompilerParams(
            collective_id=0, has_side_effects=True, vmem_limit_bytes=56 * 1024 * 1024
        ),
        cost_estimate=pl.CostEstimate(
            flops=13_000_000_000, bytes_accessed=5_000_000, transcendentals=17_000_000
        ),
    )(queries, key_cache, value_cache, out_weight)


def solution(mesh):
    in_specs = (P("ctx", "head"), P("ctx", "head"), P("ctx", "head"), P("head", "ctx"))
    out_specs = P("head", "ctx")
    return jax.shard_map(body, mesh=mesh, in_specs=in_specs, out_specs=out_specs, check_vma=False)
```

```python
import math

import jax
import jax.numpy as jnp
from jax import lax
from jax.experimental import pallas as pl
from jax.experimental.pallas import tpu as pltpu
from jax.sharding import PartitionSpec as P

HD = 128
RUN = 64
NEG = -1e30
ROWS = 512
KEYS = 512
LOG2E = math.log2(math.e)
MESH = pl.DeviceIdType.MESH

S_KV = 0
S_Q = 14
S_O = 15
S_STAT = 16
S_ATT = 17
S_FAR = 34
S_NEAR = 38
S_SIDE = 42
S_COUNT = 43


def device_at(x, y, core):
    return x * 8 + y * 2 + core


def kernel(
    q_ref, k_ref, v_ref, w_hbm, out_ref,
    q_t, kv, s0, s1, p1, fade1, acc, mrow, lrow, o_send, s_send, o_recv, s_recv, att, w,
    far, far_in, near, near_in, side, side_in, total, w_sem, send, recv,
):
    c, h = lax.axis_index("ctx"), lax.axis_index("head")
    x, y, core = c // 8, (c // 2) % 4, c % 2
    z, e = h // 2, h % 2
    scale = LOG2E / math.sqrt(HD)

    to_core = (device_at(x, y, 1 - core), h)
    to_up = (device_at(x, (y + 1) % 4, core), h)
    to_down = (device_at(x, (y + 3) % 4, core), h)
    to_x = (device_at(1 - x, y, core), h)
    to_zup = (c, ((z + 1) % 4) * 2 + e)
    to_zdown = (c, ((z + 3) % 4) * 2 + e)
    to_side = (c, z * 2 + 1 - e)
    partners = (to_core, to_up, to_down, to_x, to_zup, to_zdown, to_side)

    def remote(src, dst, number, where):
        return pltpu.make_async_remote_copy(
            src_ref=src, dst_ref=dst, send_sem=send.at[number], recv_sem=recv.at[number],
            device_id=where, device_id_type=MESH,
        )

    w_copy = pltpu.make_async_copy(w_hbm, w, w_sem)
    w_copy.start()
    barrier = pltpu.get_barrier_semaphore()
    for partner in partners:
        pl.semaphore_signal(barrier, inc=1, device_id=partner, device_id_type=MESH)

    for r in range(2):
        heads = [q_ref[r * 32 : r * 32 + 32, i * HD : (i + 1) * HD] for i in range(16)]
        block = jnp.concatenate(heads, axis=0).astype(jnp.float32)
        q_t[r] = block.T.astype(jnp.bfloat16)
    for half in range(2):
        kv[half, 0:KEYS] = k_ref[half * KEYS : (half + 1) * KEYS]
        for b in range(4):
            start = half * KEYS + b * HD
            piece = v_ref[start : start + HD].astype(jnp.float32)
            kv[half, KEYS + b * HD : KEYS + (b + 1) * HD] = piece.T.astype(jnp.bfloat16)
    for r in range(4):
        acc[r] = jnp.zeros((HD, ROWS), jnp.float32)
        mrow[r] = jnp.full((1, ROWS), NEG, jnp.float32)
        lrow[r] = jnp.zeros((1, ROWS), jnp.float32)

    pl.semaphore_wait(barrier, len(partners))

    def kv_copy(number, source, target, where):
        return remote(kv.at[source], kv.at[target], S_KV + number, where)

    own_up = [kv_copy(0 + i, i, 12 + i, to_up) for i in range(2)]
    own_down = [kv_copy(2 + i, i, 4 + i, to_down) for i in range(2)]
    own_core = [kv_copy(4 + i, i, 2 + i, to_core) for i in range(2)]
    pass_12 = kv_copy(6, 12, 14, to_core)
    pass_4 = kv_copy(7, 4, 6, to_core)
    pass_13 = kv_copy(8, 13, 15, to_core)
    pass_5 = kv_copy(9, 5, 7, to_core)
    on_up = kv_copy(10, 12, 8, to_up)
    on_down = kv_copy(11, 5, 9, to_down)
    pass_8 = kv_copy(12, 8, 10, to_core)
    pass_9 = kv_copy(13, 9, 11, to_core)
    q_copy = remote(q_t.at[0:2], q_t.at[2:4], S_Q, to_x)
    o_copy = remote(o_send, o_recv, S_O, to_x)
    s_copy = remote(s_send, s_recv, S_STAT, to_x)

    q_copy.start()
    for i in range(2):
        own_up[i].start()
        own_down[i].start()
        own_core[i].start()

    def finish_neighbour():
        row = lax.broadcasted_iota(jnp.int32, (8, ROWS), 0)
        for r in range(2):
            o_send[r] = (acc[2 + r] / lrow[2 + r]).astype(jnp.bfloat16)
            s_send[r] = jnp.where(row == 0, mrow[2 + r], lrow[2 + r])
        o_copy.start()
        s_copy.start()

    def place(u):
        stage, v = u // 8, u % 8
        i = v % 4
        group = jnp.where(stage == 3, 1 - v // 4, v // 4)
        middle = 12 - 8 * (i % 2) + 2 * (i // 2) + stage - 1
        slot = jnp.where(stage == 0, i, jnp.where(stage == 3, 8 + i, middle))
        return slot, group

    def score(u, r, s_ref):
        slot, group = place(u)
        s_ref[...] = (
            jnp.dot(kv[slot, 0:KEYS], q_t[group * 2 + r], preferred_element_type=jnp.float32)
            * scale
        )

    def weigh(u, r, s_ref):
        slot, group = place(u)
        row = group * 2 + r
        holder_core = jnp.where((slot // 2) % 2 == 1, 1 - core, core)
        holder = device_at(x, (y + slot // 4) % 4, holder_core)
        key_base = jnp.where(slot % 2 == 1, holder * RUN, -(1 << 20))
        asker = device_at(jnp.where(group == 1, 1 - x, x), y, core)
        key_rel = key_base - asker * RUN + lax.broadcasted_iota(jnp.int32, (RUN, ROWS), 0)
        token = lax.broadcasted_iota(jnp.int32, (RUN, ROWS), 1) % 32
        tail = jnp.where(key_rel <= token + r * 32, s_ref[KEYS - RUN :], NEG)
        scores = jnp.concatenate([s_ref[0 : KEYS - RUN], tail], axis=0)
        old = mrow[row]
        new = jnp.maximum(old, jnp.max(scores, axis=0, keepdims=True))
        weights = jnp.exp2(scores - new)
        fade = jnp.exp2(old - new)
        mrow[row] = new
        lrow[row] = lrow[row] * fade + jnp.sum(weights, axis=0, keepdims=True)
        return weights.astype(jnp.bfloat16), fade

    def add_values(u, r, weights, fade):
        slot, group = place(u)
        row = group * 2 + r
        values = jnp.concatenate(
            [kv[slot, KEYS + b * HD : KEYS + (b + 1) * HD] for b in range(4)], axis=1
        )
        acc[row] = acc[row] * fade + jnp.dot(values, weights, preferred_element_type=jnp.float32)

    def unit(u, carry):
        @pl.when(u == 1)
        def _():
            own_core[0].wait_recv()
            own_core[1].wait_recv()

        @pl.when(u == 3)
        def _():
            q_copy.wait_recv()

        @pl.when(u == 7)
        def _():
            own_up[0].wait_recv()
            on_up.start()
            pass_12.start()
            own_down[0].wait_recv()
            pass_4.start()

        @pl.when(u == 9)
        def _():
            pass_12.wait_recv()
            pass_4.wait_recv()

        @pl.when(u == 15)
        def _():
            own_down[1].wait_recv()
            on_down.start()
            pass_5.start()
            own_up[1].wait_recv()
            pass_13.start()

        @pl.when(u == 17)
        def _():
            pass_13.wait_recv()
            pass_5.wait_recv()

        @pl.when(u == 23)
        def _():
            on_up.wait_recv()
            pass_8.start()
            on_down.wait_recv()
            pass_9.start()

        @pl.when(u == 25)
        def _():
            pass_8.wait_recv()
            pass_9.wait_recv()

        score(u, 1, s1)
        weights, fade = weigh(u, 0, s0)
        add_values(jnp.maximum(u - 1, 0), 1, p1[...], fade1[...])
        score(jnp.minimum(u + 1, 31), 0, s0)
        weights_1, fade_1 = weigh(u, 1, s1)
        add_values(u, 0, weights, fade)
        p1[...] = weights_1
        fade1[...] = fade_1

        @pl.when(u == 28)
        def _():
            finish_neighbour()

        return carry

    p1[...] = jnp.zeros_like(p1)
    fade1[...] = jnp.ones_like(fade1)
    score(0, 0, s0)
    lax.fori_loop(0, 32, unit, 0)
    add_values(31, 1, p1[...], fade1[...])

    o_copy.wait_recv()
    s_copy.wait_recv()
    for r in range(2):
        m_b, l_b = s_recv[r, 0:1], s_recv[r, 1:2]
        new = jnp.maximum(mrow[r], m_b)
        fade_a = jnp.exp2(mrow[r] - new)
        fade_b = jnp.exp2(m_b - new) * l_b
        summed = acc[r] * fade_a + o_recv[r].astype(jnp.float32) * fade_b
        done = (summed / (lrow[r] * fade_a + fade_b)).T.astype(jnp.bfloat16)
        for i in range(16):
            att[0, 0, r * 32 : r * 32 + 32, i * HD : (i + 1) * HD] = done[i * 32 : i * 32 + 32]

    def att_copy(number, source, target, where):
        return remote(att.at[source, 0], att.at[target, 0], S_ATT + number, where)

    def att_core(number, slot):
        return remote(att.at[slot, 0], att.at[slot, 1], S_ATT + number, to_core)

    def att_half(number, source, target, half, where):
        rows = pl.ds(half * 32, 32)
        return remote(
            att.at[source, 0, rows], att.at[target, 0, rows], S_ATT + number, where
        )

    a_core = [att_core(slot, slot) for slot in range(8)]
    a_x = att_copy(8, 0, 4, to_x)
    a_up = [att_copy(9, 0, 3, to_up), att_copy(10, 4, 7, to_up)]
    a_down = [att_copy(11, 0, 1, to_down), att_copy(12, 4, 5, to_down)]
    a_up2 = [att_half(13, 3, 2, 0, to_up), att_half(14, 7, 6, 0, to_up)]
    a_down2 = [att_half(15, 1, 2, 1, to_down), att_half(16, 5, 6, 1, to_down)]

    a_x.start()
    a_up[0].start()
    a_down[0].start()
    a_core[0].start()
    a_x.wait_recv()
    a_up[1].start()
    a_down[1].start()
    a_core[4].start()
    for plane in range(2):
        a_up[plane].wait_recv()
        a_up2[plane].start()
        a_core[plane * 4 + 3].start()
        a_down[plane].wait_recv()
        a_down2[plane].start()
        a_core[plane * 4 + 1].start()
    for plane in range(2):
        a_up2[plane].wait_recv()
        a_down2[plane].wait_recv()
        a_core[plane * 4 + 2].start()
    w_copy.wait()
    for slot in range(8):
        a_core[slot].wait_recv()

    cols = w.shape[1] // 2

    def project(distance, side_of, part):
        target = ((z + distance) % 4) * 2 + side_of
        slot = jnp.where(target // 4 == x, 0, 4) + (target % 4 - y + 4) % 4
        block = jnp.concatenate([att[slot, core], att[slot, 1 - core]], axis=0)
        return jnp.dot(
            block, w[:, part * cols : (part + 1) * cols], preferred_element_type=jnp.float32
        )

    def far_copy(way, s):
        return remote(
            far.at[way, s], far_in.at[way, s], S_FAR + way * 2 + s, (to_zup, to_zdown)[way]
        )

    def near_copy(way, s):
        return remote(
            near.at[way, s], near_in.at[way, s], S_NEAR + way * 2 + s, (to_zup, to_zdown)[way]
        )

    side_copy = remote(side, side_in, S_SIDE, to_side)

    def far_step(s, carry):
        for way in range(2):
            far[way, s] = project(2, s, way).astype(jnp.bfloat16)
            far_copy(way, s).start()
        return carry

    lax.fori_loop(0, 2, far_step, 0)
    for way in range(2):

        def near_step(s, carry):
            other = 1 - way
            near[way, s, :, other * cols : (other + 1) * cols] = project(
                1 + 2 * way, s, other
            ).astype(jnp.bfloat16)
            far_copy(way, s).wait_recv()
            near[way, s, :, way * cols : (way + 1) * cols] = (
                project(1 + 2 * way, s, way) + far_in[way, s].astype(jnp.float32)
            ).astype(jnp.bfloat16)
            near_copy(way, s).start()
            return carry

        lax.fori_loop(0, 2, near_step, 0)

    def last_step(turn, carry):
        s = jnp.where(turn == 0, 1 - e, e)
        for part in range(2):
            total[:, part * cols : (part + 1) * cols] = project(0, s, part)
        near_copy(0, s).wait_recv()
        near_copy(1, s).wait_recv()
        total[...] = (
            total[...] + near_in[0, s].astype(jnp.float32) + near_in[1, s].astype(jnp.float32)
        )

        @pl.when(turn == 0)
        def _():
            side[...] = total[...].astype(jnp.bfloat16)
            side_copy.start()

        return carry

    lax.fori_loop(0, 2, last_step, 0)
    side_copy.wait_recv()
    out_ref[...] = (total[...] + side_in[...].astype(jnp.float32)).astype(jnp.bfloat16)

    sent = own_up + own_down + own_core + [pass_12, pass_4, pass_13, pass_5, on_up, on_down]
    sent += [pass_8, pass_9, q_copy, o_copy, s_copy, a_x, side_copy]
    sent += a_core + a_up + a_down + a_up2 + a_down2
    sent += [far_copy(way, s) for way in range(2) for s in range(2)]
    sent += [near_copy(way, s) for way in range(2) for s in range(2)]
    for copy in sent:
        copy.wait_send()


def body(queries, key_cache, value_cache, out_weight):
    tokens, width = queries.shape
    cols = out_weight.shape[1]
    vmem = pl.BlockSpec(memory_space=pltpu.VMEM)
    bf16, f32 = jnp.bfloat16, jnp.float32
    return pl.pallas_call(
        kernel,
        out_shape=jax.ShapeDtypeStruct((2 * tokens, cols), bf16),
        in_specs=[vmem, vmem, vmem, pl.BlockSpec(memory_space=pl.ANY)],
        out_specs=vmem,
        scratch_shapes=[
            pltpu.VMEM((4, HD, ROWS), bf16),
            pltpu.VMEM((16, 2 * KEYS, HD), bf16),
            pltpu.VMEM((KEYS, ROWS), f32),
            pltpu.VMEM((KEYS, ROWS), f32),
            pltpu.VMEM((KEYS, ROWS), bf16),
            pltpu.VMEM((1, ROWS), f32),
            pltpu.VMEM((4, HD, ROWS), f32),
            pltpu.VMEM((4, 1, ROWS), f32),
            pltpu.VMEM((4, 1, ROWS), f32),
            pltpu.VMEM((2, HD, ROWS), bf16),
            pltpu.VMEM((2, 8, ROWS), f32),
            pltpu.VMEM((2, HD, ROWS), bf16),
            pltpu.VMEM((2, 8, ROWS), f32),
            pltpu.VMEM((8, 2, tokens, width), bf16),
            pltpu.VMEM(out_weight.shape, bf16),
            pltpu.VMEM((2, 2, 2 * tokens, cols // 2), bf16),
            pltpu.VMEM((2, 2, 2 * tokens, cols // 2), bf16),
            pltpu.VMEM((2, 2, 2 * tokens, cols), bf16),
            pltpu.VMEM((2, 2, 2 * tokens, cols), bf16),
            pltpu.VMEM((2 * tokens, cols), bf16),
            pltpu.VMEM((2 * tokens, cols), bf16),
            pltpu.VMEM((2 * tokens, cols), f32),
            pltpu.SemaphoreType.DMA,
            pltpu.SemaphoreType.DMA((S_COUNT,)),
            pltpu.SemaphoreType.DMA((S_COUNT,)),
        ],
        compiler_params=pltpu.CompilerParams(
            collective_id=0, has_side_effects=True, vmem_limit_bytes=56 * 1024 * 1024
        ),
        cost_estimate=pl.CostEstimate(
            flops=13_000_000_000, bytes_accessed=5_000_000, transcendentals=17_000_000
        ),
    )(queries, key_cache, value_cache, out_weight)


def solution(mesh):
    in_specs = (P("ctx", "head"), P("ctx", "head"), P("ctx", "head"), P("head", "ctx"))
    out_specs = P("head", "ctx")
    return jax.shard_map(body, mesh=mesh, in_specs=in_specs, out_specs=out_specs, check_vma=False)
```

```python
import math

import jax
import jax.numpy as jnp
from jax import lax
from jax.experimental import pallas as pl
from jax.experimental.pallas import tpu as pltpu
from jax.sharding import PartitionSpec as P

HD = 128
RUN = 64
NEG = -1e30
ROWS = 256
KEYS = 512
QUARTER = 16
LOG2E = math.log2(math.e)
MESH = pl.DeviceIdType.MESH

S_KV = 0
S_Q = 14
S_O = 16
S_STAT = 20
S_ATT = 24
S_FAR = 92
S_NEAR = 100
S_SIDE = 108
S_COUNT = 112


def device_at(x, y, core):
    return x * 8 + y * 2 + core


def kernel(
    q_hbm, k_hbm, v_hbm, w_hbm, out_ref,
    q_ref, v_ref, q_t, kv, s0, s1, p1, fade1, acc, mrow, lrow, o_send, s_send, o_recv, s_recv,
    att, w, prod, far, far_in, near, near_in, side, side_in, mine, fetched, send, recv,
):
    c, h = lax.axis_index("ctx"), lax.axis_index("head")
    x, y, core = c // 8, (c // 2) % 4, c % 2
    z, e = h // 2, h % 2
    scale = LOG2E / math.sqrt(HD)

    to_core = (device_at(x, y, 1 - core), h)
    to_up = (device_at(x, (y + 1) % 4, core), h)
    to_down = (device_at(x, (y + 3) % 4, core), h)
    to_x = (device_at(1 - x, y, core), h)
    to_zup = (c, ((z + 1) % 4) * 2 + e)
    to_zdown = (c, ((z + 3) % 4) * 2 + e)
    to_side = (c, z * 2 + 1 - e)
    partners = (to_core, to_up, to_down, to_x, to_zup, to_zdown, to_side)

    def remote(src, dst, number, where):
        return pltpu.make_async_remote_copy(
            src_ref=src, dst_ref=dst, send_sem=send.at[number], recv_sem=recv.at[number],
            device_id=where, device_id_type=MESH,
        )

    q_fetch = pltpu.make_async_copy(q_hbm, q_ref, fetched.at[0])
    v_fetch = pltpu.make_async_copy(v_hbm, v_ref, fetched.at[1])
    k_fetch = [
        pltpu.make_async_copy(
            k_hbm.at[pl.ds(i * KEYS, KEYS)], kv.at[i, pl.ds(0, KEYS)], fetched.at[2 + i]
        )
        for i in range(2)
    ]
    w_copy = pltpu.make_async_copy(w_hbm, w, fetched.at[4])
    for fetch in [q_fetch, v_fetch] + k_fetch:
        fetch.start()
    barrier = pltpu.get_barrier_semaphore()
    for partner in partners:
        pl.semaphore_signal(barrier, inc=1, device_id=partner, device_id_type=MESH)

    q_fetch.wait()
    for i in range(4):
        rows = slice(i * QUARTER, (i + 1) * QUARTER)
        heads = [q_ref[rows, j * HD : (j + 1) * HD] for j in range(16)]
        block = jnp.concatenate(heads, axis=0).astype(jnp.float32)
        q_t[i] = block.T.astype(jnp.bfloat16)
    v_fetch.wait()
    for half in range(2):
        for b in range(4):
            start = half * KEYS + b * HD
            piece = v_ref[start : start + HD].astype(jnp.float32)
            kv[half, KEYS + b * HD : KEYS + (b + 1) * HD] = piece.T.astype(jnp.bfloat16)
    for i in range(8):
        acc[i] = jnp.zeros((HD, ROWS), jnp.float32)
        mrow[i] = jnp.full((1, ROWS), NEG, jnp.float32)
        lrow[i] = jnp.zeros((1, ROWS), jnp.float32)

    for fetch in k_fetch:
        fetch.wait()
    w_copy.start()
    pl.semaphore_wait(barrier, len(partners))

    def kv_copy(number, source, target, where):
        return remote(kv.at[source], kv.at[target], S_KV + number, where)

    own_up = [kv_copy(0 + i, i, 12 + i, to_up) for i in range(2)]
    own_down = [kv_copy(2 + i, i, 4 + i, to_down) for i in range(2)]
    own_core = [kv_copy(4 + i, i, 2 + i, to_core) for i in range(2)]
    pass_12 = kv_copy(6, 12, 14, to_core)
    pass_4 = kv_copy(7, 4, 6, to_core)
    pass_13 = kv_copy(8, 13, 15, to_core)
    pass_5 = kv_copy(9, 5, 7, to_core)
    on_up = kv_copy(10, 12, 8, to_up)
    on_down = kv_copy(11, 5, 9, to_down)
    pass_8 = kv_copy(12, 8, 10, to_core)
    pass_9 = kv_copy(13, 9, 11, to_core)
    q_copy = [
        remote(q_t.at[pl.ds(2 * i, 2)], q_t.at[pl.ds(4 + 2 * i, 2)], S_Q + i, to_x)
        for i in range(2)
    ]
    o_copy = [remote(o_send.at[f], o_recv.at[f], S_O + f, to_x) for f in range(4)]
    s_copy = [remote(s_send.at[f], s_recv.at[f], S_STAT + f, to_x) for f in range(4)]

    own_up[0].start()
    own_down[0].start()
    for i in range(2):
        q_copy[i].start()
        own_core[i].start()

    def place(t):
        v = t % 8
        i = t % 4
        step = 12 - 8 * (i % 2) + 2 * (i // 2)
        late = jnp.where(v < 4, step + 1, 8 + i)
        slot = jnp.where(t < 16, i, jnp.where(t < 32, step, late))
        f = jnp.where(t < 32, t // 4 - 4, t // 8 - 4)
        one = jnp.where(t < 16, t // 4 * 2, f)
        two = jnp.where(t < 16, t // 4 * 2 + 1, f + 4)
        return slot, one, two

    def score(t, s_ref):
        slot, one, two = place(t)
        keys = kv[slot, 0:KEYS]
        for j, row in enumerate((one, two)):
            s_ref[:, j * ROWS : (j + 1) * ROWS] = (
                jnp.dot(keys, q_t[row], preferred_element_type=jnp.float32) * scale
            )

    def weigh(t, s_ref):
        slot, one, two = place(t)
        holder_core = jnp.where((slot // 2) % 2 == 1, 1 - core, core)
        holder = device_at(x, (y + slot // 4) % 4, holder_core)
        key_base = jnp.where(slot % 2 == 1, holder * RUN, -(1 << 20))
        token = lax.broadcasted_iota(jnp.int32, (RUN, ROWS), 1) % QUARTER
        key_token = lax.broadcasted_iota(jnp.int32, (RUN, ROWS), 0) - token
        rounded, fades = [], []
        for j, row in enumerate((one, two)):
            lanes = slice(j * ROWS, (j + 1) * ROWS)
            asker = device_at(jnp.where(row >= 4, 1 - x, x), y, core)
            limit = asker * RUN + (row % 4) * QUARTER - key_base
            tail = jnp.where(key_token <= limit, s_ref[KEYS - RUN :, lanes], NEG)
            scores = jnp.concatenate([s_ref[0 : KEYS - RUN, lanes], tail], axis=0)
            old = mrow[row]
            new = jnp.maximum(old, jnp.max(scores, axis=0, keepdims=True))
            weights = jnp.exp2(scores - new)
            fade = jnp.exp2(old - new)
            mrow[row] = new
            lrow[row] = lrow[row] * fade + jnp.sum(weights, axis=0, keepdims=True)
            rounded.append(weights.astype(jnp.bfloat16))
            fades.append(fade)
        return jnp.concatenate(rounded, axis=1), jnp.concatenate(fades, axis=1)

    def add_values(t, weights, fade):
        slot, one, two = place(t)
        values = jnp.concatenate(
            [kv[slot, KEYS + b * HD : KEYS + (b + 1) * HD] for b in range(4)], axis=1
        )
        for j, row in enumerate((one, two)):
            lanes = slice(j * ROWS, (j + 1) * ROWS)
            acc[row] = acc[row] * fade[:, lanes] + jnp.dot(
                values, weights[:, lanes], preferred_element_type=jnp.float32
            )

    def finish_neighbour(f):
        row = lax.broadcasted_iota(jnp.int32, (8, ROWS), 0)
        o_send[f] = (acc[4 + f] / lrow[4 + f]).astype(jnp.bfloat16)
        s_send[f] = jnp.where(row == 0, mrow[4 + f], lrow[4 + f])
        o_copy[f].start()
        s_copy[f].start()

    def combine(f):
        o_copy[f].wait_recv()
        s_copy[f].wait_recv()
        m_b, l_b = s_recv[f, 0:1], s_recv[f, 1:2]
        new = jnp.maximum(mrow[f], m_b)
        fade_a = jnp.exp2(mrow[f] - new)
        fade_b = jnp.exp2(m_b - new) * l_b
        summed = acc[f] * fade_a + o_recv[f].astype(jnp.float32) * fade_b
        done = (summed / (lrow[f] * fade_a + fade_b)).T.astype(jnp.bfloat16)
        for j in range(16):
            att[f, 0, :, j * HD : (j + 1) * HD] = done[j * QUARTER : (j + 1) * QUARTER]

    width = att.shape[3]

    def gather_copies(f):
        base = S_ATT + 17 * f

        def whole(number, source, target, where):
            return remote(att.at[f, source * 2], att.at[f, target * 2], base + number, where)

        def to_other_core(slot):
            return remote(att.at[f, slot * 2], att.at[f, slot * 2 + 1], base + slot, to_core)

        def part(number, source, target, piece, where):
            rows, lanes = pl.ds(0, QUARTER), pl.ds(piece * (width // 2), width // 2)
            return remote(
                att.at[f, source * 2, rows, lanes], att.at[f, target * 2, rows, lanes],
                base + number, where,
            )

        return dict(
            core=[to_other_core(slot) for slot in range(8)],
            x=[whole(8, 0, 4, to_x)],
            up=[whole(9, 0, 3, to_up), whole(10, 4, 7, to_up)],
            down=[whole(11, 0, 1, to_down), whole(12, 4, 5, to_down)],
            up2=[part(13, 3, 2, 0, to_up), part(14, 7, 6, 0, to_up)],
            down2=[part(15, 1, 2, 1, to_down), part(16, 5, 6, 1, to_down)],
        )

    gathers = [gather_copies(f) for f in range(4)]

    def gather_own(f):
        g = gathers[f]
        g["x"][0].start()
        g["up"][0].start()
        g["down"][0].start()
        g["core"][0].start()

    def gather_x(f):
        g = gathers[f]
        g["x"][0].wait_recv()
        g["up"][1].start()
        g["down"][1].start()
        g["core"][4].start()

    def gather_y(f, plane):
        g = gathers[f]
        g["up"][plane].wait_recv()
        g["up2"][plane].start()
        g["core"][plane * 4 + 3].start()
        g["down"][plane].wait_recv()
        g["down2"][plane].start()
        g["core"][plane * 4 + 1].start()

    def gather_y2(f, plane):
        g = gathers[f]
        g["up2"][plane].wait_recv()
        g["down2"][plane].wait_recv()
        g["core"][plane * 4 + 2].start()

    def gather_end(f):
        for slot in range(8):
            gathers[f]["core"][slot].wait_recv()

    cols = w.shape[1] // 2
    z_ways = (to_zup, to_zdown)
    far_copy = [
        [remote(far.at[f, i], far_in.at[f, i], S_FAR + f * 2 + i, z_ways[i]) for i in range(2)]
        for f in range(4)
    ]
    near_copy = [
        [remote(near.at[f, i], near_in.at[f, i], S_NEAR + f * 2 + i, z_ways[i]) for i in range(2)]
        for f in range(4)
    ]
    side_copy = [remote(side.at[f], side_in.at[f], S_SIDE + f, to_side) for f in range(4)]

    def product_of(f, distance, s, lanes):
        target = ((z + distance) % 4) * 2 + s
        slot = jnp.where(target // 4 == x, 0, 4) + (target % 4 - y + 4) % 4
        b = f % 2
        return jnp.concatenate(
            [prod[b, slot * 2 + core, :, lanes], prod[b, slot * 2 + 1 - core, :, lanes]], axis=0
        )

    span = 2 * QUARTER

    def reduce_far(f):
        block = att[f].reshape(16 * QUARTER, width)
        for way in range(2):
            lanes = slice(way * cols, (way + 1) * cols)
            prod[f % 2, :, :, lanes] = jnp.dot(
                block, w[:, lanes], preferred_element_type=jnp.float32
            ).reshape(16, QUARTER, cols)
            for s in range(2):
                far[f, way, s * span : (s + 1) * span] = product_of(f, 2, s, lanes).astype(
                    jnp.bfloat16
                )
            far_copy[f][way].start()

    def reduce_near(f):
        for way in range(2):
            other = slice((1 - way) * cols, (2 - way) * cols)
            lanes = slice(way * cols, (way + 1) * cols)
            far_copy[f][way].wait_recv()
            for s in range(2):
                rows = slice(s * span, (s + 1) * span)
                near[f, way, rows, other] = product_of(f, 1 + 2 * way, s, other).astype(
                    jnp.bfloat16
                )
                near[f, way, rows, lanes] = (
                    product_of(f, 1 + 2 * way, s, lanes) + far_in[f, way, rows].astype(jnp.float32)
                ).astype(jnp.bfloat16)
            near_copy[f][way].start()

    def reduce_last(f):
        near_copy[f][0].wait_recv()
        near_copy[f][1].wait_recv()

        def summed(s):
            rows = pl.ds(pl.multiple_of(s * span, span), span)
            return (
                product_of(f, 0, s, slice(0, 2 * cols))
                + near_in[f, 0, rows].astype(jnp.float32)
                + near_in[f, 1, rows].astype(jnp.float32)
            )

        side[f] = summed(1 - e).astype(jnp.bfloat16)
        side_copy[f].start()
        mine[f] = summed(e)

    def reduce_end(f):
        side_copy[f].wait_recv()
        done = (mine[f] + side_in[f].astype(jnp.float32)).astype(jnp.bfloat16)
        for i in range(2):
            start = i * RUN + f * QUARTER
            out_ref[start : start + QUARTER] = done[i * QUARTER : (i + 1) * QUARTER]

    def wait_all(*copies):
        for copy in copies:
            copy.wait_recv()

    def pass_on(arrived, *onward):
        arrived.wait_recv()
        for copy in onward:
            copy.start()

    def start_rest():
        wait_all(*own_core)
        own_up[1].start()
        own_down[1].start()

    before = [
        (0, start_rest),
        (3, lambda: wait_all(*q_copy)),
        (7, lambda: pass_on(own_up[0], on_up, pass_12)),
        (7, lambda: pass_on(own_down[0], pass_4)),
        (8, lambda: wait_all(pass_12, pass_4)),
        (13, lambda: pass_on(own_down[1], on_down, pass_5)),
        (13, lambda: pass_on(own_up[1], pass_13)),
        (16, lambda: wait_all(pass_13, pass_5)),
        (17, lambda: pass_on(on_up, pass_8)),
        (17, lambda: pass_on(on_down, pass_9)),
        (18, lambda: wait_all(pass_8, pass_9)),
        (28, w_copy.wait),
    ]
    after = [(20 + 4 * f, lambda f=f: finish_neighbour(f)) for f in range(4)]
    for f in range(4):
        after += [
            (22 + 4 * f, lambda f=f: combine(f)),
            (22 + 4 * f, lambda f=f: gather_own(f)),
            (24 + 4 * f, lambda f=f: gather_x(f)),
            (24 + 4 * f, lambda f=f: gather_y(f, 0)),
            (26 + 4 * f, lambda f=f: gather_y(f, 1)),
            (26 + 4 * f, lambda f=f: gather_y2(f, 0)),
            (28 + 4 * f, lambda f=f: gather_y2(f, 1)),
            (29 + 4 * f, lambda f=f: gather_end(f)),
            (29 + 4 * f, lambda f=f: reduce_far(f)),
            (31 + 4 * f, lambda f=f: reduce_near(f)),
            (33 + 4 * f, lambda f=f: reduce_last(f)),
            (35 + 4 * f, lambda f=f: reduce_end(f)),
        ]
    after.sort(key=lambda item: item[0])

    def run(events, u):
        for k in sorted({step for step, _ in events}):

            @pl.when(u == k)
            def _():
                for step, action in events:
                    if step == k:
                        action()

    def unit(u, carry):
        run(before, u)
        t = 2 * u
        score(t + 1, s1)
        weights, fade = weigh(t, s0)
        add_values(jnp.maximum(t - 1, 0), p1[...], fade1[...])
        score(jnp.minimum(t + 2, 63), s0)
        weights_1, fade_1 = weigh(t + 1, s1)
        add_values(t, weights, fade)
        p1[...] = weights_1
        fade1[...] = fade_1
        run([(step, action) for step, action in after if step < 32], u)
        return carry

    p1[...] = jnp.zeros_like(p1)
    fade1[...] = jnp.ones_like(fade1)
    score(0, s0)
    lax.fori_loop(0, 32, unit, 0)
    add_values(63, p1[...], fade1[...])
    for step, action in after:
        if step >= 32:
            action()

    sent = own_up + own_down + own_core + [pass_12, pass_4, pass_13, pass_5, on_up, on_down]
    sent += [pass_8, pass_9] + q_copy + o_copy + s_copy + side_copy
    for f in range(4):
        for copies in gathers[f].values():
            sent += copies
        sent += far_copy[f] + near_copy[f]
    for copy in sent:
        copy.wait_send()


def body(queries, key_cache, value_cache, out_weight):
    tokens, width = queries.shape
    cols = out_weight.shape[1]
    vmem, anywhere = pl.BlockSpec(memory_space=pltpu.VMEM), pl.BlockSpec(memory_space=pl.ANY)
    bf16, f32 = jnp.bfloat16, jnp.float32
    return pl.pallas_call(
        kernel,
        out_shape=jax.ShapeDtypeStruct((2 * tokens, cols), bf16),
        in_specs=[anywhere] * 4,
        out_specs=vmem,
        scratch_shapes=[
            pltpu.VMEM(queries.shape, bf16),
            pltpu.VMEM(value_cache.shape, bf16),
            pltpu.VMEM((8, HD, ROWS), bf16),
            pltpu.VMEM((16, 2 * KEYS, HD), bf16),
            pltpu.VMEM((KEYS, 2 * ROWS), f32),
            pltpu.VMEM((KEYS, 2 * ROWS), f32),
            pltpu.VMEM((KEYS, 2 * ROWS), bf16),
            pltpu.VMEM((1, 2 * ROWS), f32),
            pltpu.VMEM((8, HD, ROWS), f32),
            pltpu.VMEM((8, 1, ROWS), f32),
            pltpu.VMEM((8, 1, ROWS), f32),
            pltpu.VMEM((4, HD, ROWS), bf16),
            pltpu.VMEM((4, 8, ROWS), f32),
            pltpu.VMEM((4, HD, ROWS), bf16),
            pltpu.VMEM((4, 8, ROWS), f32),
            pltpu.VMEM((4, 16, QUARTER, width), bf16),
            pltpu.VMEM(out_weight.shape, bf16),
            pltpu.VMEM((2, 16, QUARTER, cols), f32),
            pltpu.VMEM((4, 2, tokens, cols // 2), bf16),
            pltpu.VMEM((4, 2, tokens, cols // 2), bf16),
            pltpu.VMEM((4, 2, tokens, cols), bf16),
            pltpu.VMEM((4, 2, tokens, cols), bf16),
            pltpu.VMEM((4, 2 * QUARTER, cols), bf16),
            pltpu.VMEM((4, 2 * QUARTER, cols), bf16),
            pltpu.VMEM((4, 2 * QUARTER, cols), f32),
            pltpu.SemaphoreType.DMA((5,)),
            pltpu.SemaphoreType.DMA((S_COUNT,)),
            pltpu.SemaphoreType.DMA((S_COUNT,)),
        ],
        compiler_params=pltpu.CompilerParams(
            collective_id=0, has_side_effects=True, vmem_limit_bytes=56 * 1024 * 1024
        ),
        cost_estimate=pl.CostEstimate(
            flops=13_000_000_000, bytes_accessed=5_000_000, transcendentals=17_000_000
        ),
    )(queries, key_cache, value_cache, out_weight)


def solution(mesh):
    in_specs = (P("ctx", "head"), P("ctx", "head"), P("ctx", "head"), P("head", "ctx"))
    out_specs = P("head", "ctx")
    return jax.shard_map(body, mesh=mesh, in_specs=in_specs, out_specs=out_specs, check_vma=False)
```

```python
import math

import jax
import jax.numpy as jnp
from jax import lax
from jax.experimental import pallas as pl
from jax.experimental.pallas import tpu as pltpu
from jax.sharding import PartitionSpec as P

HD = 128
RUN = 64
NEG = -1e30
ROWS = 512
HALF = 32
KEYS = 512
LOG2E = math.log2(math.e)
MESH = pl.DeviceIdType.MESH

S_KV = 0
S_Q = 14
S_O = 16
S_STAT = 18
S_ATT = 20
S_FAR = 54
S_PLAIN = 58
S_LATER = 62
S_SIDE = 66
S_COUNT = 68


def device_at(x, y, core):
    return x * 8 + y * 2 + core


def kernel(
    q_hbm, k_hbm, v_hbm, w_hbm, out_ref,
    q_ref, k_ref, q_s, kv, s0, s1, p1, fade1, acc, mrow, o_send, s_send, o_recv, s_recv,
    att, w, terms, far_in, plain_in, added, added_in, side, side_in, mine, fetched, send, recv,
):
    c, h = lax.axis_index("ctx"), lax.axis_index("head")
    x, y, core = c // 8, (c // 2) % 4, c % 2
    z, e = h // 2, h % 2
    scale = LOG2E / math.sqrt(HD)

    to_core = (device_at(x, y, 1 - core), h)
    to_up = (device_at(x, (y + 1) % 4, core), h)
    to_down = (device_at(x, (y + 3) % 4, core), h)
    to_x = (device_at(1 - x, y, core), h)
    z_ways = ((c, ((z + 1) % 4) * 2 + e), (c, ((z + 3) % 4) * 2 + e))
    to_side = (c, z * 2 + 1 - e)
    partners = (to_core, to_up, to_down, to_x, to_side) + z_ways

    def remote(src, dst, number, where):
        return pltpu.make_async_remote_copy(
            src_ref=src, dst_ref=dst, send_sem=send.at[number], recv_sem=recv.at[number],
            device_id=where, device_id_type=MESH,
        )

    q_fetch = pltpu.make_async_copy(q_hbm, q_ref, fetched.at[0])
    k_fetch = pltpu.make_async_copy(k_hbm, k_ref, fetched.at[1])
    v_fetch = [
        pltpu.make_async_copy(
            v_hbm.at[pl.ds(i * KEYS, KEYS)], kv.at[i, pl.ds(0, KEYS)], fetched.at[2 + i]
        )
        for i in range(2)
    ]
    w_copy = pltpu.make_async_copy(w_hbm, w, fetched.at[4])
    for fetch in [k_fetch, q_fetch] + v_fetch:
        fetch.start()
    barrier = pltpu.get_barrier_semaphore()
    for partner in partners:
        pl.semaphore_signal(barrier, inc=1, device_id=partner, device_id_type=MESH)

    k_fetch.wait()
    for half in range(2):
        for b in range(4):
            start = half * KEYS + b * HD
            piece = k_ref[start : start + HD].astype(jnp.float32)
            kv[half, KEYS + b * HD : KEYS + (b + 1) * HD] = piece.T.astype(jnp.bfloat16)
    q_fetch.wait()
    for r in range(2):
        for i in range(16):
            q_s[r, i * HALF : (i + 1) * HALF] = q_ref[
                r * HALF : (r + 1) * HALF, i * HD : (i + 1) * HD
            ]
    for fetch in v_fetch:
        fetch.wait()
    w_copy.start()
    pl.semaphore_wait(barrier, len(partners))

    def kv_copy(number, source, target, where):
        return remote(kv.at[source], kv.at[target], S_KV + number, where)

    own_up = [kv_copy(0 + i, i, 12 + i, to_up) for i in range(2)]
    own_down = [kv_copy(2 + i, i, 4 + i, to_down) for i in range(2)]
    own_core = [kv_copy(4 + i, i, 2 + i, to_core) for i in range(2)]
    pass_12 = kv_copy(6, 12, 14, to_core)
    pass_4 = kv_copy(7, 4, 6, to_core)
    pass_13 = kv_copy(8, 13, 15, to_core)
    pass_5 = kv_copy(9, 5, 7, to_core)
    on_up = kv_copy(10, 12, 8, to_up)
    on_down = kv_copy(11, 5, 9, to_down)
    pass_8 = kv_copy(12, 8, 10, to_core)
    pass_9 = kv_copy(13, 9, 11, to_core)
    q_copy = [remote(q_s.at[i], q_s.at[2 + i], S_Q + i, to_x) for i in range(2)]
    o_copy = [remote(o_send.at[f], o_recv.at[f], S_O + f, to_x) for f in range(2)]
    s_copy = [remote(s_send.at[f], s_recv.at[f], S_STAT + f, to_x) for f in range(2)]

    for i in range(2):
        own_core[i].start()
    q_copy[0].start()
    own_up[0].start()
    own_down[0].start()
    q_copy[1].start()
    for r in range(4):
        acc[r] = jnp.zeros((ROWS, 2 * HD), jnp.float32)
        mrow[r] = jnp.full((ROWS, HD), NEG, jnp.float32)

    def place(t):
        v = (t - 16) % 8
        f = (t - 16) // 8
        pair = jnp.where(t < 8, t // 2 % 2, jnp.where(t < 16, t // 4, 4 + v // 2))
        pair = jnp.where((t >= 16) & (v >= 4), 6 + v % 2, pair)
        row = jnp.where(t < 8, t // 4 * 2 + t % 2, jnp.where(t < 16, t % 4, v % 2 * 2 + f))
        row = jnp.where((t >= 16) & (v >= 4), (1 - (v - 4) // 2) * 2 + f, row)
        i = pair - 2
        middle = 12 + 2 * (i % 2) + i // 2
        one = jnp.where(pair < 2, 2 * pair, jnp.where(pair < 6, middle, 2 * pair - 4))
        two = jnp.where((pair >= 2) & (pair < 6), one - 8, one + 1)
        return one, two, row

    def score(t, s_ref):
        one, two, row = place(t)
        queries = q_s[row]
        for j, slot in enumerate((one, two)):
            keys = jnp.concatenate(
                [kv[slot, KEYS + b * HD : KEYS + (b + 1) * HD] for b in range(4)], axis=1
            )
            s_ref[:, j * KEYS : (j + 1) * KEYS] = (
                jnp.dot(queries, keys, preferred_element_type=jnp.float32) * scale
            )

    def weigh(t, s_ref):
        one, two, row = place(t)
        asker = device_at(jnp.where(row >= 2, 1 - x, x), y, core)
        token = lax.broadcasted_iota(jnp.int32, (ROWS, HD), 0) % HALF
        key_token = lax.broadcasted_iota(jnp.int32, (ROWS, HD), 1) - RUN
        pieces = []
        for j, slot in enumerate((one, two)):
            holder_core = jnp.where((slot // 2) % 2 == 1, 1 - core, core)
            holder = device_at(x, (y + slot // 4) % 4, holder_core)
            first = jnp.where(slot % 2 == 1, holder * RUN, -(1 << 20))
            limit = asker * RUN + (row % 2) * HALF - first
            end = (j + 1) * KEYS
            seen = (key_token < 0) | (key_token - token <= limit)
            pieces.append(s_ref[:, j * KEYS : end - HD])
            pieces.append(jnp.where(seen, s_ref[:, end - HD : end], NEG))
        scores = jnp.concatenate(pieces, axis=1)
        old = mrow[row]
        new = jnp.maximum(old, jnp.max(scores, axis=1, keepdims=True))
        weights = jnp.exp2(scores - jnp.concatenate([new] * (2 * KEYS // HD), axis=1))
        mrow[row] = new
        return weights.astype(jnp.bfloat16), jnp.exp2(old - new)

    def add_values(t, weights, fade):
        one, two, row = place(t)
        ones = jnp.ones((KEYS, HD), jnp.bfloat16)
        values = jnp.concatenate(
            [jnp.concatenate([kv[slot, 0:KEYS], ones], axis=1) for slot in (one, two)], axis=0
        )
        acc[row] = acc[row] * jnp.concatenate([fade, fade], axis=1) + jnp.dot(
            weights, values, preferred_element_type=jnp.float32
        )

    def normalised(row):
        total = acc[row, :, HD : 2 * HD]
        return acc[row, :, 0:HD] / total, mrow[row] + jnp.log(total) * LOG2E

    def finish_neighbour(f):
        value, level = normalised(2 + f)
        o_send[f] = value.astype(jnp.bfloat16)
        s_send[f] = level.T[0:8]
        o_copy[f].start()
        s_copy[f].start()

    def block_of(owner):
        start = owner * HALF
        return start if isinstance(start, int) else pl.multiple_of(start, HALF)

    def combine(f):
        value, level = normalised(f)
        o_copy[f].wait_recv()
        s_copy[f].wait_recv()
        other = jnp.broadcast_to(s_recv[f, 0:1], (HD, ROWS)).T
        top = jnp.maximum(level, other)
        part_a, part_b = jnp.exp2(level - top), jnp.exp2(other - top)
        done = (value * part_a + o_recv[f].astype(jnp.float32) * part_b) / (part_a + part_b)
        done = done.astype(jnp.bfloat16)
        for i in range(16):
            att[f, pl.ds(block_of(c), HALF), i * HD : (i + 1) * HD] = done[
                i * HALF : (i + 1) * HALF
            ]

    def gather_copy(f, number, dx, dy, where, part=None, from_core=None):
        owner = device_at(1 - x if dx else x, (y + dy) % 4, core if from_core is None else from_core)
        start, size = block_of(owner), HALF
        if part is not None:
            size = HALF // 2
            start = pl.multiple_of(start + part * size, size)
        block = att.at[f, pl.ds(start, size)]
        return remote(block, block, S_ATT + 17 * f + number, where)

    sent = own_up + own_down + own_core + [pass_12, pass_4, pass_13, pass_5, on_up, on_down]
    sent += [pass_8, pass_9] + q_copy + o_copy + s_copy

    def arrived(f, number, dx, dy, part=None, from_core=None):
        gather_copy(f, number, dx, dy, to_core, part, from_core).wait_recv()

    def gather_start(f, *args):
        gather_copy(f, *args).start()

    def gather_own(f):
        gather_start(f, 8, 0, 0, to_x)
        gather_start(f, 9, 0, 0, to_up)
        gather_start(f, 11, 0, 0, to_down)
        gather_start(f, 0, 0, 0, to_core)

    def gather_x(f):
        arrived(f, 8, 1, 0)
        gather_start(f, 10, 1, 0, to_up)
        gather_start(f, 12, 1, 0, to_down)
        gather_start(f, 4, 1, 0, to_core)

    def gather_y(f, plane):
        arrived(f, 9 + plane, plane, 3)
        gather_start(f, 13 + plane, plane, 3, to_up, 0)
        gather_start(f, 4 * plane + 3, plane, 3, to_core)
        arrived(f, 11 + plane, plane, 1)
        gather_start(f, 15 + plane, plane, 1, to_down, 1)
        gather_start(f, 4 * plane + 1, plane, 1, to_core)

    def gather_y2(f, plane):
        arrived(f, 13 + plane, plane, 2, 0)
        arrived(f, 15 + plane, plane, 2, 1)
        gather_start(f, 4 * plane + 2, plane, 2, to_core)

    def gather_end(f):
        for plane in range(2):
            for dy in range(4):
                arrived(f, 4 * plane + dy, plane, dy, None, 1 - core)

    def gather_sent(f):
        copies = [gather_copy(f, 8, 0, 0, to_x)]
        for plane in range(2):
            copies += [gather_copy(f, 4 * plane + dy, plane, dy, to_core) for dy in range(4)]
            copies += [gather_copy(f, 9 + plane, plane, 0, to_up)]
            copies += [gather_copy(f, 11 + plane, plane, 0, to_down)]
            copies += [gather_copy(f, 13 + plane, plane, 3, to_up, 0)]
            copies += [gather_copy(f, 15 + plane, plane, 1, to_down, 1)]
        return copies

    cols = w.shape[1] // 2
    rows = 4 * HALF

    def half(i):
        return pl.ds(i * cols, cols)

    def block(distance):
        return pl.ds(pl.multiple_of(((z + distance) % 4) * rows, rows), rows)

    far_copy = [
        [
            remote(terms.at[f, block(2), half(i)], far_in.at[f, i], S_FAR + 2 * f + i, z_ways[i])
            for i in range(2)
        ]
        for f in range(2)
    ]
    plain_copy = [
        [
            remote(
                terms.at[f, block(1 + 2 * i), half(1 - i)], plain_in.at[f, i],
                S_PLAIN + 2 * f + i, z_ways[i],
            )
            for i in range(2)
        ]
        for f in range(2)
    ]
    later_copy = [
        [
            remote(added.at[f, i], added_in.at[f, i], S_LATER + 2 * f + i, z_ways[i])
            for i in range(2)
        ]
        for f in range(2)
    ]
    side_copy = [remote(side.at[f], side_in.at[f], S_SIDE + f, to_side) for f in range(2)]

    def project(f):
        for i in range(2):
            terms[f, :, half(i)] = jnp.dot(
                att[f], w[:, half(i)], preferred_element_type=jnp.float32
            ).astype(jnp.bfloat16)
            far_copy[f][i].start()
        for i in range(2):
            plain_copy[f][i].start()

    def reduce_added(f):
        for i in range(2):
            far_copy[f][i].wait_recv()
            added[f, i] = (
                terms[f, block(1 + 2 * i), half(i)].astype(jnp.float32)
                + far_in[f, i].astype(jnp.float32)
            ).astype(jnp.bfloat16)
            later_copy[f][i].start()

    def reduce_last(f):
        for i in range(2):
            plain_copy[f][i].wait_recv()
        for i in range(2):
            later_copy[f][i].wait_recv()

        def summed(s, i):
            size = rows // 2
            part = pl.ds(pl.multiple_of(s * size, size), size)
            own = pl.ds(pl.multiple_of(z * rows + s * size, size), size)
            return (
                terms[f, own, half(i)].astype(jnp.float32)
                + added_in[f, i, part].astype(jnp.float32)
                + plain_in[f, 1 - i, part].astype(jnp.float32)
            )

        for i in range(2):
            side[f, :, half(i)] = summed(1 - e, i).astype(jnp.bfloat16)
        side_copy[f].start()
        for i in range(2):
            mine[f, :, half(i)] = summed(e, i)

    def reduce_end(f):
        side_copy[f].wait_recv()
        done = (mine[f] + side_in[f].astype(jnp.float32)).astype(jnp.bfloat16)
        for i in range(2):
            start = i * RUN + f * HALF
            out_ref[start : start + HALF] = done[i * HALF : (i + 1) * HALF]

    def wait_all(*copies):
        for copy in copies:
            copy.wait_recv()

    def pass_on(arrival, *onward):
        arrival.wait_recv()
        for copy in onward:
            copy.start()

    def start_rest():
        wait_all(*own_core)
        own_up[1].start()
        own_down[1].start()

    before = [
        (0, start_rest),
        (1, lambda: wait_all(q_copy[0])),
        (2, lambda: wait_all(q_copy[1])),
        (3, lambda: pass_on(own_up[0], on_up, pass_12)),
        (3, lambda: pass_on(own_down[0], pass_4)),
        (5, lambda: wait_all(pass_12, pass_4)),
        (7, lambda: pass_on(own_down[1], on_down, pass_5)),
        (7, lambda: pass_on(own_up[1], pass_13)),
        (8, lambda: wait_all(pass_13, pass_5)),
        (9, lambda: pass_on(on_up, pass_8)),
        (9, lambda: pass_on(on_down, pass_9)),
        (10, lambda: wait_all(pass_8, pass_9)),
    ]
    after = [
        (11, lambda: finish_neighbour(0)),
        (13, lambda: combine(0)),
        (13, lambda: gather_own(0)),
        (15, lambda: finish_neighbour(1)),
        (15, lambda: gather_x(0)),
    ]

    def run(events, u):
        for k in sorted({step for step, _ in events}):

            @pl.when(u == k)
            def _():
                for step, action in events:
                    if step == k:
                        action()

    def unit(u, carry):
        run(before, u)
        t = 2 * u
        score(t + 1, s1)
        weights, fade = weigh(t, s0)
        add_values(jnp.maximum(t - 1, 0), p1[...], fade1[...])
        score(jnp.minimum(t + 2, 31), s0)
        weights_1, fade_1 = weigh(t + 1, s1)
        add_values(t, weights, fade)
        p1[...] = weights_1
        fade1[...] = fade_1
        run(after, u)
        return carry

    p1[...] = jnp.zeros_like(p1)
    fade1[...] = jnp.ones_like(fade1)
    score(0, s0)
    lax.fori_loop(0, 16, unit, 0)
    gather_y(0, 0)
    add_values(31, p1[...], fade1[...])
    gather_y(0, 1)
    combine(1)
    gather_own(1)
    gather_y2(0, 0)
    gather_y2(0, 1)
    gather_x(1)
    w_copy.wait()
    gather_end(0)
    project(0)
    gather_y(1, 0)
    gather_y(1, 1)
    reduce_added(0)
    gather_y2(1, 0)
    gather_y2(1, 1)
    gather_end(1)
    project(1)
    reduce_last(0)
    reduce_added(1)
    reduce_end(0)
    reduce_last(1)
    reduce_end(1)

    sent += side_copy
    for f in range(2):
        sent += gather_sent(f) + far_copy[f] + plain_copy[f] + later_copy[f]
    for copy in sent:
        copy.wait_send()


def body(queries, key_cache, value_cache, out_weight):
    tokens, width = queries.shape
    cols = out_weight.shape[1]
    all_rows = tokens // 2 * lax.axis_size("ctx")
    vmem, anywhere = pl.BlockSpec(memory_space=pltpu.VMEM), pl.BlockSpec(memory_space=pl.ANY)
    bf16, f32 = jnp.bfloat16, jnp.float32
    piece = pltpu.VMEM((2, 2, 2 * tokens, cols // 2), bf16)
    return pl.pallas_call(
        kernel,
        out_shape=jax.ShapeDtypeStruct((2 * tokens, cols), bf16),
        in_specs=[anywhere] * 4,
        out_specs=vmem,
        scratch_shapes=[
            pltpu.VMEM(queries.shape, bf16),
            pltpu.VMEM(key_cache.shape, bf16),
            pltpu.VMEM((4, ROWS, HD), bf16),
            pltpu.VMEM((16, 2 * KEYS, HD), bf16),
            pltpu.VMEM((ROWS, 2 * KEYS), f32),
            pltpu.VMEM((ROWS, 2 * KEYS), f32),
            pltpu.VMEM((ROWS, 2 * KEYS), bf16),
            pltpu.VMEM((ROWS, HD), f32),
            pltpu.VMEM((4, ROWS, 2 * HD), f32),
            pltpu.VMEM((4, ROWS, HD), f32),
            pltpu.VMEM((2, ROWS, HD), bf16),
            pltpu.VMEM((2, 8, ROWS), f32),
            pltpu.VMEM((2, ROWS, HD), bf16),
            pltpu.VMEM((2, 8, ROWS), f32),
            pltpu.VMEM((2, all_rows, width), bf16),
            pltpu.VMEM(out_weight.shape, bf16),
            pltpu.VMEM((2, all_rows, cols), bf16),
            piece,
            piece,
            piece,
            piece,
            pltpu.VMEM((2, tokens, cols), bf16),
            pltpu.VMEM((2, tokens, cols), bf16),
            pltpu.VMEM((2, tokens, cols), f32),
            pltpu.SemaphoreType.DMA((5,)),
            pltpu.SemaphoreType.DMA((S_COUNT,)),
            pltpu.SemaphoreType.DMA((S_COUNT,)),
        ],
        compiler_params=pltpu.CompilerParams(
            collective_id=0, has_side_effects=True, vmem_limit_bytes=56 * 1024 * 1024
        ),
        cost_estimate=pl.CostEstimate(
            flops=13_000_000_000, bytes_accessed=5_000_000, transcendentals=17_000_000
        ),
    )(queries, key_cache, value_cache, out_weight)


def solution(mesh):
    in_specs = (P("ctx", "head"), P("ctx", "head"), P("ctx", "head"), P("head", "ctx"))
    out_specs = P("head", "ctx")
    return jax.shard_map(body, mesh=mesh, in_specs=in_specs, out_specs=out_specs, check_vma=False)
```

```python
import math

import jax
import jax.numpy as jnp
from jax import lax
from jax.experimental import pallas as pl
from jax.experimental.pallas import tpu as pltpu
from jax.sharding import PartitionSpec as P

HD = 128
RUN = 64
NEG = -1e30
ROWS = 512
HALF = 32
KEYS = 512
LOG2E = math.log2(math.e)
MESH = pl.DeviceIdType.MESH

S_KV = 0
S_Q = 14
S_O = 16
S_STAT = 18
S_ATT = 20
S_FAR = 54
S_PLAIN = 58
S_LATER = 62
S_SIDE = 66
S_COUNT = 68


def device_at(x, y, core):
    return x * 8 + y * 2 + core


def kernel(
    q_hbm, k_hbm, v_hbm, w_hbm, out_ref,
    q_ref, k_ref, q_s, kv, s0, s1, p1, fade1, acc, mrow, o_send, s_send, o_recv, s_recv,
    att, w, terms, far_in, plain_in, added, added_in, side, side_in, mine, fetched, send, recv,
):
    c, h = lax.axis_index("ctx"), lax.axis_index("head")
    x, y, core = c // 8, (c // 2) % 4, c % 2
    z, e = h // 2, h % 2
    scale = LOG2E / math.sqrt(HD)

    to_core = (device_at(x, y, 1 - core), h)
    to_up = (device_at(x, (y + 1) % 4, core), h)
    to_down = (device_at(x, (y + 3) % 4, core), h)
    to_x = (device_at(1 - x, y, core), h)
    z_ways = ((c, ((z + 1) % 4) * 2 + e), (c, ((z + 3) % 4) * 2 + e))
    to_side = (c, z * 2 + 1 - e)
    partners = (to_core, to_up, to_down, to_x, to_side) + z_ways

    def remote(src, dst, number, where):
        return pltpu.make_async_remote_copy(
            src_ref=src, dst_ref=dst, send_sem=send.at[number], recv_sem=recv.at[number],
            device_id=where, device_id_type=MESH,
        )

    q_fetch = pltpu.make_async_copy(q_hbm, q_ref, fetched.at[0])
    k_fetch = pltpu.make_async_copy(k_hbm, k_ref, fetched.at[1])
    v_fetch = [
        pltpu.make_async_copy(
            v_hbm.at[pl.ds(i * KEYS, KEYS)], kv.at[i, pl.ds(0, KEYS)], fetched.at[2 + i]
        )
        for i in range(2)
    ]
    w_copy = pltpu.make_async_copy(w_hbm, w, fetched.at[4])
    for fetch in [k_fetch, q_fetch] + v_fetch:
        fetch.start()
    barrier = pltpu.get_barrier_semaphore()
    for partner in partners:
        pl.semaphore_signal(barrier, inc=1, device_id=partner, device_id_type=MESH)

    k_fetch.wait()
    for half in range(2):
        for b in range(4):
            start = half * KEYS + b * HD
            piece = k_ref[start : start + HD].astype(jnp.float32)
            kv[half, KEYS + b * HD : KEYS + (b + 1) * HD] = piece.T.astype(jnp.bfloat16)
    q_fetch.wait()
    for r in range(2):
        for i in range(16):
            q_s[r, i * HALF : (i + 1) * HALF] = q_ref[
                r * HALF : (r + 1) * HALF, i * HD : (i + 1) * HD
            ]
    for fetch in v_fetch:
        fetch.wait()
    w_copy.start()
    pl.semaphore_wait(barrier, len(partners))

    def kv_copy(number, source, target, where):
        return remote(kv.at[source], kv.at[target], S_KV + number, where)

    own_up = [kv_copy(0 + i, i, 12 + i, to_up) for i in range(2)]
    own_down = [kv_copy(2 + i, i, 4 + i, to_down) for i in range(2)]
    own_core = [kv_copy(4 + i, i, 2 + i, to_core) for i in range(2)]
    pass_12 = kv_copy(6, 12, 14, to_core)
    pass_4 = kv_copy(7, 4, 6, to_core)
    pass_13 = kv_copy(8, 13, 15, to_core)
    pass_5 = kv_copy(9, 5, 7, to_core)
    on_up = kv_copy(10, 12, 8, to_up)
    on_down = kv_copy(11, 5, 9, to_down)
    pass_8 = kv_copy(12, 8, 10, to_core)
    pass_9 = kv_copy(13, 9, 11, to_core)
    q_copy = [remote(q_s.at[i], q_s.at[2 + i], S_Q + i, to_x) for i in range(2)]
    o_copy = [remote(o_send.at[f], o_recv.at[f], S_O + f, to_x) for f in range(2)]
    s_copy = [remote(s_send.at[f], s_recv.at[f], S_STAT + f, to_x) for f in range(2)]

    for i in range(2):
        own_core[i].start()
    q_copy[0].start()
    own_up[0].start()
    own_down[0].start()
    q_copy[1].start()
    for r in range(4):
        acc[r] = jnp.zeros((ROWS, 2 * HD), jnp.float32)
        mrow[r] = jnp.full((ROWS, HD), NEG, jnp.float32)

    def place(t):
        f, q = (t - 8) // 12, (t - 8) % 12
        pair = jnp.where(t < 8, t // 2 % 2, jnp.where(q < 8, 2 + q // 2, 6 + q % 2))
        late = jnp.where(q < 8, q % 2, 1 - (q - 8) // 2) * 2 + f
        row = jnp.where(t < 8, t // 4 * 2 + t % 2, late)
        i = pair - 2
        middle = 12 + 2 * (i % 2) + i // 2
        one = jnp.where(pair < 2, 2 * pair, jnp.where(pair < 6, middle, 2 * pair - 4))
        two = jnp.where((pair >= 2) & (pair < 6), one - 8, one + 1)
        return one, two, row

    def score(t, s_ref):
        one, two, row = place(t)
        queries = q_s[row]
        for j, slot in enumerate((one, two)):
            keys = jnp.concatenate(
                [kv[slot, KEYS + b * HD : KEYS + (b + 1) * HD] for b in range(4)], axis=1
            )
            s_ref[:, j * KEYS : (j + 1) * KEYS] = (
                jnp.dot(queries, keys, preferred_element_type=jnp.float32) * scale
            )

    def weigh(t, s_ref):
        one, two, row = place(t)
        asker = device_at(jnp.where(row >= 2, 1 - x, x), y, core)
        token = lax.broadcasted_iota(jnp.int32, (ROWS, HD), 0) % HALF
        key_token = lax.broadcasted_iota(jnp.int32, (ROWS, HD), 1) - RUN
        pieces = []
        for j, slot in enumerate((one, two)):
            holder_core = jnp.where((slot // 2) % 2 == 1, 1 - core, core)
            holder = device_at(x, (y + slot // 4) % 4, holder_core)
            first = jnp.where(slot % 2 == 1, holder * RUN, -(1 << 20))
            limit = asker * RUN + (row % 2) * HALF - first
            end = (j + 1) * KEYS
            seen = (key_token < 0) | (key_token - token <= limit)
            pieces.append(s_ref[:, j * KEYS : end - HD])
            pieces.append(jnp.where(seen, s_ref[:, end - HD : end], NEG))
        scores = jnp.concatenate(pieces, axis=1)
        old = mrow[row]
        new = jnp.maximum(old, jnp.max(scores, axis=1, keepdims=True))
        weights = jnp.exp2(scores - jnp.concatenate([new] * (2 * KEYS // HD), axis=1))
        mrow[row] = new
        return weights.astype(jnp.bfloat16), jnp.exp2(old - new)

    def add_values(t, weights, fade):
        one, two, row = place(t)
        ones = jnp.ones((KEYS, HD), jnp.bfloat16)
        values = jnp.concatenate(
            [jnp.concatenate([kv[slot, 0:KEYS], ones], axis=1) for slot in (one, two)], axis=0
        )
        acc[row] = acc[row] * jnp.concatenate([fade, fade], axis=1) + jnp.dot(
            weights, values, preferred_element_type=jnp.float32
        )

    def normalised(row):
        total = acc[row, :, HD : 2 * HD]
        return acc[row, :, 0:HD] / total, mrow[row] + jnp.log(total) * LOG2E

    def finish_neighbour(f):
        value, level = normalised(2 + f)
        o_send[f] = value.astype(jnp.bfloat16)
        s_send[f] = level.T[0:8]
        o_copy[f].start()
        s_copy[f].start()

    def block_of(owner):
        start = owner * HALF
        return start if isinstance(start, int) else pl.multiple_of(start, HALF)

    def combine(f):
        value, level = normalised(f)
        o_copy[f].wait_recv()
        s_copy[f].wait_recv()
        other = jnp.broadcast_to(s_recv[f, 0:1], (HD, ROWS)).T
        top = jnp.maximum(level, other)
        part_a, part_b = jnp.exp2(level - top), jnp.exp2(other - top)
        done = (value * part_a + o_recv[f].astype(jnp.float32) * part_b) / (part_a + part_b)
        done = done.astype(jnp.bfloat16)
        for i in range(16):
            att[f, pl.ds(block_of(c), HALF), i * HD : (i + 1) * HD] = done[
                i * HALF : (i + 1) * HALF
            ]

    def gather_copy(f, number, dx, dy, where, part=None, from_core=None):
        owner = device_at(1 - x if dx else x, (y + dy) % 4, core if from_core is None else from_core)
        start, size = block_of(owner), HALF
        if part is not None:
            size = HALF // 2
            start = pl.multiple_of(start + part * size, size)
        block = att.at[f, pl.ds(start, size)]
        return remote(block, block, S_ATT + 17 * f + number, where)

    sent = own_up + own_down + own_core + [pass_12, pass_4, pass_13, pass_5, on_up, on_down]
    sent += [pass_8, pass_9] + q_copy + o_copy + s_copy

    def arrived(f, number, dx, dy, part=None, from_core=None):
        gather_copy(f, number, dx, dy, to_core, part, from_core).wait_recv()

    def gather_start(f, *args):
        gather_copy(f, *args).start()

    def gather_own(f):
        gather_start(f, 8, 0, 0, to_x)
        gather_start(f, 9, 0, 0, to_up)
        gather_start(f, 11, 0, 0, to_down)
        gather_start(f, 0, 0, 0, to_core)

    def gather_x(f):
        arrived(f, 8, 1, 0)
        gather_start(f, 10, 1, 0, to_up)
        gather_start(f, 12, 1, 0, to_down)
        gather_start(f, 4, 1, 0, to_core)

    def gather_y(f, plane):
        arrived(f, 9 + plane, plane, 3)
        gather_start(f, 13 + plane, plane, 3, to_up, 0)
        gather_start(f, 4 * plane + 3, plane, 3, to_core)
        arrived(f, 11 + plane, plane, 1)
        gather_start(f, 15 + plane, plane, 1, to_down, 1)
        gather_start(f, 4 * plane + 1, plane, 1, to_core)

    def gather_y2(f, plane):
        arrived(f, 13 + plane, plane, 2, 0)
        arrived(f, 15 + plane, plane, 2, 1)
        gather_start(f, 4 * plane + 2, plane, 2, to_core)

    def gather_end(f):
        for plane in range(2):
            for dy in range(4):
                arrived(f, 4 * plane + dy, plane, dy, None, 1 - core)

    def gather_sent(f):
        copies = [gather_copy(f, 8, 0, 0, to_x)]
        for plane in range(2):
            copies += [gather_copy(f, 4 * plane + dy, plane, dy, to_core) for dy in range(4)]
            copies += [gather_copy(f, 9 + plane, plane, 0, to_up)]
            copies += [gather_copy(f, 11 + plane, plane, 0, to_down)]
            copies += [gather_copy(f, 13 + plane, plane, 3, to_up, 0)]
            copies += [gather_copy(f, 15 + plane, plane, 1, to_down, 1)]
        return copies

    cols = w.shape[1] // 2
    rows = 4 * HALF

    def half(i):
        return pl.ds(i * cols, cols)

    def block(distance):
        return pl.ds(pl.multiple_of(((z + distance) % 4) * rows, rows), rows)

    far_copy = [
        [
            remote(terms.at[f, block(2), half(i)], far_in.at[f, i], S_FAR + 2 * f + i, z_ways[i])
            for i in range(2)
        ]
        for f in range(2)
    ]
    plain_copy = [
        [
            remote(
                terms.at[f, block(1 + 2 * i), half(1 - i)], plain_in.at[f, i],
                S_PLAIN + 2 * f + i, z_ways[i],
            )
            for i in range(2)
        ]
        for f in range(2)
    ]
    later_copy = [
        [
            remote(added.at[f, i], added_in.at[f, i], S_LATER + 2 * f + i, z_ways[i])
            for i in range(2)
        ]
        for f in range(2)
    ]
    side_copy = [remote(side.at[f], side_in.at[f], S_SIDE + f, to_side) for f in range(2)]

    def project(f):
        for i in range(2):
            terms[f, :, half(i)] = jnp.dot(
                att[f], w[:, half(i)], preferred_element_type=jnp.float32
            ).astype(jnp.bfloat16)
            far_copy[f][i].start()
        for i in range(2):
            plain_copy[f][i].start()

    def reduce_added(f):
        for i in range(2):
            far_copy[f][i].wait_recv()
            added[f, i] = (
                terms[f, block(1 + 2 * i), half(i)].astype(jnp.float32)
                + far_in[f, i].astype(jnp.float32)
            ).astype(jnp.bfloat16)
            later_copy[f][i].start()

    def reduce_last(f):
        for i in range(2):
            plain_copy[f][i].wait_recv()
        for i in range(2):
            later_copy[f][i].wait_recv()

        def summed(s, i):
            size = rows // 2
            part = pl.ds(pl.multiple_of(s * size, size), size)
            own = pl.ds(pl.multiple_of(z * rows + s * size, size), size)
            return (
                terms[f, own, half(i)].astype(jnp.float32)
                + added_in[f, i, part].astype(jnp.float32)
                + plain_in[f, 1 - i, part].astype(jnp.float32)
            )

        for i in range(2):
            side[f, :, half(i)] = summed(1 - e, i).astype(jnp.bfloat16)
        side_copy[f].start()
        for i in range(2):
            mine[f, :, half(i)] = summed(e, i)

    def reduce_end(f):
        side_copy[f].wait_recv()
        done = (mine[f] + side_in[f].astype(jnp.float32)).astype(jnp.bfloat16)
        for i in range(2):
            start = i * RUN + f * HALF
            out_ref[start : start + HALF] = done[i * HALF : (i + 1) * HALF]

    def wait_all(*copies):
        for copy in copies:
            copy.wait_recv()

    def pass_on(arrival, *onward):
        arrival.wait_recv()
        for copy in onward:
            copy.start()

    def start_rest():
        wait_all(*own_core)
        own_up[1].start()
        own_down[1].start()

    before = [
        (0, start_rest),
        (1, lambda: wait_all(q_copy[0])),
        (2, lambda: wait_all(q_copy[1])),
        (3, lambda: pass_on(own_up[0], on_up, pass_12)),
        (3, lambda: pass_on(own_down[0], pass_4)),
        (4, lambda: wait_all(pass_12, pass_4)),
        (5, lambda: pass_on(own_down[1], on_down, pass_5)),
        (5, lambda: pass_on(own_up[1], pass_13)),
        (6, lambda: wait_all(pass_13, pass_5)),
        (7, lambda: pass_on(on_up, pass_8)),
        (7, lambda: pass_on(on_down, pass_9)),
        (8, lambda: wait_all(pass_8, pass_9)),
    ]
    after = [
        (9, lambda: finish_neighbour(0)),
        (11, lambda: combine(0)),
        (11, lambda: gather_own(0)),
        (12, lambda: gather_x(0)),
        (13, lambda: gather_y(0, 0)),
        (14, lambda: gather_y(0, 1)),
        (15, lambda: finish_neighbour(1)),
        (15, lambda: gather_y2(0, 0)),
    ]

    def run(events, u):
        for k in sorted({step for step, _ in events}):

            @pl.when(u == k)
            def _():
                for step, action in events:
                    if step == k:
                        action()

    def unit(u, carry):
        run(before, u)
        t = 2 * u
        score(t + 1, s1)
        weights, fade = weigh(t, s0)
        add_values(jnp.maximum(t - 1, 0), p1[...], fade1[...])
        score(jnp.minimum(t + 2, 31), s0)
        weights_1, fade_1 = weigh(t + 1, s1)
        add_values(t, weights, fade)
        p1[...] = weights_1
        fade1[...] = fade_1
        run(after, u)
        return carry

    p1[...] = jnp.zeros_like(p1)
    fade1[...] = jnp.ones_like(fade1)
    score(0, s0)
    lax.fori_loop(0, 16, unit, 0)
    add_values(31, p1[...], fade1[...])
    gather_y2(0, 1)
    w_copy.wait()
    gather_end(0)
    project(0)
    combine(1)
    gather_own(1)
    gather_x(1)
    reduce_added(0)
    gather_y(1, 0)
    gather_y(1, 1)
    gather_y2(1, 0)
    reduce_last(0)
    gather_y2(1, 1)
    gather_end(1)
    project(1)
    reduce_end(0)
    reduce_added(1)
    reduce_last(1)
    reduce_end(1)

    sent += side_copy
    for f in range(2):
        sent += gather_sent(f) + far_copy[f] + plain_copy[f] + later_copy[f]
    for copy in sent:
        copy.wait_send()


def body(queries, key_cache, value_cache, out_weight):
    tokens, width = queries.shape
    cols = out_weight.shape[1]
    all_rows = tokens // 2 * lax.axis_size("ctx")
    vmem, anywhere = pl.BlockSpec(memory_space=pltpu.VMEM), pl.BlockSpec(memory_space=pl.ANY)
    bf16, f32 = jnp.bfloat16, jnp.float32
    piece = pltpu.VMEM((2, 2, 2 * tokens, cols // 2), bf16)
    return pl.pallas_call(
        kernel,
        out_shape=jax.ShapeDtypeStruct((2 * tokens, cols), bf16),
        in_specs=[anywhere] * 4,
        out_specs=vmem,
        scratch_shapes=[
            pltpu.VMEM(queries.shape, bf16),
            pltpu.VMEM(key_cache.shape, bf16),
            pltpu.VMEM((4, ROWS, HD), bf16),
            pltpu.VMEM((16, 2 * KEYS, HD), bf16),
            pltpu.VMEM((ROWS, 2 * KEYS), f32),
            pltpu.VMEM((ROWS, 2 * KEYS), f32),
            pltpu.VMEM((ROWS, 2 * KEYS), bf16),
            pltpu.VMEM((ROWS, HD), f32),
            pltpu.VMEM((4, ROWS, 2 * HD), f32),
            pltpu.VMEM((4, ROWS, HD), f32),
            pltpu.VMEM((2, ROWS, HD), bf16),
            pltpu.VMEM((2, 8, ROWS), f32),
            pltpu.VMEM((2, ROWS, HD), bf16),
            pltpu.VMEM((2, 8, ROWS), f32),
            pltpu.VMEM((2, all_rows, width), bf16),
            pltpu.VMEM(out_weight.shape, bf16),
            pltpu.VMEM((2, all_rows, cols), bf16),
            piece,
            piece,
            piece,
            piece,
            pltpu.VMEM((2, tokens, cols), bf16),
            pltpu.VMEM((2, tokens, cols), bf16),
            pltpu.VMEM((2, tokens, cols), f32),
            pltpu.SemaphoreType.DMA((5,)),
            pltpu.SemaphoreType.DMA((S_COUNT,)),
            pltpu.SemaphoreType.DMA((S_COUNT,)),
        ],
        compiler_params=pltpu.CompilerParams(
            collective_id=0, has_side_effects=True, vmem_limit_bytes=56 * 1024 * 1024
        ),
        cost_estimate=pl.CostEstimate(
            flops=13_000_000_000, bytes_accessed=5_000_000, transcendentals=17_000_000
        ),
    )(queries, key_cache, value_cache, out_weight)


def solution(mesh):
    in_specs = (P("ctx", "head"), P("ctx", "head"), P("ctx", "head"), P("head", "ctx"))
    out_specs = P("head", "ctx")
    return jax.shard_map(body, mesh=mesh, in_specs=in_specs, out_specs=out_specs, check_vma=False)
```

```python
import math

import jax
import jax.numpy as jnp
from jax import lax
from jax.experimental import pallas as pl
from jax.experimental.pallas import tpu as pltpu
from jax.sharding import PartitionSpec as P

HD = 128
RUN = 64
NEG = -1e30
ROWS = 512
HALF = 32
KEYS = 512
LOG2E = math.log2(math.e)
MESH = pl.DeviceIdType.MESH

S_KV = 0
S_Q = 14
S_O = 16
S_STAT = 18
S_ATT = 20
S_FAR = 54
S_PLAIN = 58
S_LATER = 62
S_SIDE = 66
S_COUNT = 68


def device_at(x, y, core):
    return x * 8 + y * 2 + core


def kernel(
    q_hbm, k_hbm, v_hbm, w_hbm, out_ref,
    q_ref, k_ref, q_s, kv, s0, s1, p1, fade1, acc, mrow, o_send, s_send, o_recv, s_recv,
    att, w, terms, far_in, plain_in, added, added_in, side, side_in, mine, fetched, send, recv,
):
    c, h = lax.axis_index("ctx"), lax.axis_index("head")
    x, y, core = c // 8, (c // 2) % 4, c % 2
    z, e = h // 2, h % 2
    scale = LOG2E / math.sqrt(HD)

    to_core = (device_at(x, y, 1 - core), h)
    to_up = (device_at(x, (y + 1) % 4, core), h)
    to_down = (device_at(x, (y + 3) % 4, core), h)
    to_x = (device_at(1 - x, y, core), h)
    z_ways = ((c, ((z + 1) % 4) * 2 + e), (c, ((z + 3) % 4) * 2 + e))
    to_side = (c, z * 2 + 1 - e)
    partners = (to_core, to_up, to_down, to_x, to_side) + z_ways

    def remote(src, dst, number, where):
        return pltpu.make_async_remote_copy(
            src_ref=src, dst_ref=dst, send_sem=send.at[number], recv_sem=recv.at[number],
            device_id=where, device_id_type=MESH,
        )

    q_fetch = pltpu.make_async_copy(q_hbm, q_ref, fetched.at[0])
    k_fetch = pltpu.make_async_copy(k_hbm, k_ref, fetched.at[1])
    v_fetch = [
        pltpu.make_async_copy(
            v_hbm.at[pl.ds(i * KEYS, KEYS)], kv.at[i, pl.ds(0, KEYS)], fetched.at[2 + i]
        )
        for i in range(2)
    ]
    w_copy = pltpu.make_async_copy(w_hbm, w, fetched.at[4])
    for fetch in [k_fetch, q_fetch] + v_fetch:
        fetch.start()
    barrier = pltpu.get_barrier_semaphore()
    for partner in partners:
        pl.semaphore_signal(barrier, inc=1, device_id=partner, device_id_type=MESH)

    k_fetch.wait()
    for half in range(2):
        for b in range(4):
            start = half * KEYS + b * HD
            piece = k_ref[start : start + HD].astype(jnp.float32)
            kv[half, KEYS + b * HD : KEYS + (b + 1) * HD] = piece.T.astype(jnp.bfloat16)
    q_fetch.wait()
    for r in range(2):
        for i in range(16):
            q_s[r, i * HALF : (i + 1) * HALF] = q_ref[
                r * HALF : (r + 1) * HALF, i * HD : (i + 1) * HD
            ]
    for fetch in v_fetch:
        fetch.wait()
    w_copy.start()
    pl.semaphore_wait(barrier, len(partners))

    def kv_copy(number, source, target, where):
        return remote(kv.at[source], kv.at[target], S_KV + number, where)

    own_up = [kv_copy(0 + i, i, 12 + i, to_up) for i in range(2)]
    own_down = [kv_copy(2 + i, i, 4 + i, to_down) for i in range(2)]
    own_core = [kv_copy(4 + i, i, 2 + i, to_core) for i in range(2)]
    pass_12 = kv_copy(6, 12, 14, to_core)
    pass_4 = kv_copy(7, 4, 6, to_core)
    pass_13 = kv_copy(8, 13, 15, to_core)
    pass_5 = kv_copy(9, 5, 7, to_core)
    on_up = kv_copy(10, 12, 8, to_up)
    on_down = kv_copy(11, 5, 9, to_down)
    pass_8 = kv_copy(12, 8, 10, to_core)
    pass_9 = kv_copy(13, 9, 11, to_core)
    q_copy = [remote(q_s.at[i], q_s.at[2 + i], S_Q + i, to_x) for i in range(2)]
    o_copy = [remote(o_send.at[f], o_recv.at[f], S_O + f, to_x) for f in range(2)]
    s_copy = [remote(s_send.at[f], s_recv.at[f], S_STAT + f, to_x) for f in range(2)]

    for i in range(2):
        own_core[i].start()
    q_copy[0].start()
    own_up[0].start()
    own_down[0].start()
    q_copy[1].start()
    for r in range(4):
        acc[r] = jnp.zeros((ROWS, 2 * HD), jnp.float32)
        mrow[r] = jnp.full((ROWS, HD), NEG, jnp.float32)

    def place(t):
        pair = jnp.where(t < 8, t // 2 % 2, t // 4)
        row = jnp.where(t < 8, t // 4 * 2 + t % 2, jnp.where(t < 24, t % 4, (t + 2) % 4))
        i = pair - 2
        middle = 12 + 2 * (i % 2) + i // 2
        one = jnp.where(pair < 2, 2 * pair, jnp.where(pair < 6, middle, 2 * pair - 4))
        two = jnp.where((pair >= 2) & (pair < 6), one - 8, one + 1)
        return one, two, row

    def score(t, s_ref):
        one, two, row = place(t)
        queries = q_s[row]
        for j, slot in enumerate((one, two)):
            keys = jnp.concatenate(
                [kv[slot, KEYS + b * HD : KEYS + (b + 1) * HD] for b in range(4)], axis=1
            )
            s_ref[:, j * KEYS : (j + 1) * KEYS] = (
                jnp.dot(queries, keys, preferred_element_type=jnp.float32) * scale
            )

    def weigh(t, s_ref):
        one, two, row = place(t)
        asker = device_at(jnp.where(row >= 2, 1 - x, x), y, core)
        token = lax.broadcasted_iota(jnp.int32, (ROWS, HD), 0) % HALF
        key_token = lax.broadcasted_iota(jnp.int32, (ROWS, HD), 1) - RUN
        pieces = []
        for j, slot in enumerate((one, two)):
            holder_core = jnp.where((slot // 2) % 2 == 1, 1 - core, core)
            holder = device_at(x, (y + slot // 4) % 4, holder_core)
            first = jnp.where(slot % 2 == 1, holder * RUN, -(1 << 20))
            limit = asker * RUN + (row % 2) * HALF - first
            end = (j + 1) * KEYS
            seen = (key_token < 0) | (key_token - token <= limit)
            pieces.append(s_ref[:, j * KEYS : end - HD])
            pieces.append(jnp.where(seen, s_ref[:, end - HD : end], NEG))
        scores = jnp.concatenate(pieces, axis=1)
        old = mrow[row]
        new = jnp.maximum(old, jnp.max(scores, axis=1, keepdims=True))
        weights = jnp.exp2(scores - jnp.concatenate([new] * (2 * KEYS // HD), axis=1))
        mrow[row] = new
        return weights.astype(jnp.bfloat16), jnp.exp2(old - new)

    def add_values(t, weights, fade):
        one, two, row = place(t)
        ones = jnp.ones((KEYS, HD), jnp.bfloat16)
        values = jnp.concatenate(
            [jnp.concatenate([kv[slot, 0:KEYS], ones], axis=1) for slot in (one, two)], axis=0
        )
        acc[row] = acc[row] * jnp.concatenate([fade, fade], axis=1) + jnp.dot(
            weights, values, preferred_element_type=jnp.float32
        )

    def normalised(row):
        total = acc[row, :, HD : 2 * HD]
        return acc[row, :, 0:HD] / total, mrow[row] + jnp.log(total) * LOG2E

    def finish_neighbour(f):
        value, level = normalised(2 + f)
        o_send[f] = value.astype(jnp.bfloat16)
        s_send[f] = level.T[0:8]
        o_copy[f].start()
        s_copy[f].start()

    def block_of(owner):
        start = owner * HALF
        return start if isinstance(start, int) else pl.multiple_of(start, HALF)

    def combine(f):
        value, level = normalised(f)
        o_copy[f].wait_recv()
        s_copy[f].wait_recv()
        other = jnp.broadcast_to(s_recv[f, 0:1], (HD, ROWS)).T
        top = jnp.maximum(level, other)
        part_a, part_b = jnp.exp2(level - top), jnp.exp2(other - top)
        done = (value * part_a + o_recv[f].astype(jnp.float32) * part_b) / (part_a + part_b)
        done = done.astype(jnp.bfloat16)
        for i in range(16):
            att[f, pl.ds(block_of(c), HALF), i * HD : (i + 1) * HD] = done[
                i * HALF : (i + 1) * HALF
            ]

    def gather_copy(f, number, dx, dy, where, part=None, from_core=None):
        owner = device_at(1 - x if dx else x, (y + dy) % 4, core if from_core is None else from_core)
        start, size = block_of(owner), HALF
        if part is not None:
            size = HALF // 2
            start = pl.multiple_of(start + part * size, size)
        block = att.at[f, pl.ds(start, size)]
        return remote(block, block, S_ATT + 17 * f + number, where)

    sent = own_up + own_down + own_core + [pass_12, pass_4, pass_13, pass_5, on_up, on_down]
    sent += [pass_8, pass_9] + q_copy + o_copy + s_copy

    def arrived(f, number, dx, dy, part=None, from_core=None):
        gather_copy(f, number, dx, dy, to_core, part, from_core).wait_recv()

    def gather_start(f, *args):
        gather_copy(f, *args).start()

    def gather_own(f):
        gather_start(f, 8, 0, 0, to_x)
        gather_start(f, 9, 0, 0, to_up)
        gather_start(f, 11, 0, 0, to_down)
        gather_start(f, 0, 0, 0, to_core)

    def gather_x(f):
        arrived(f, 8, 1, 0)
        gather_start(f, 10, 1, 0, to_up)
        gather_start(f, 12, 1, 0, to_down)
        gather_start(f, 4, 1, 0, to_core)

    def gather_y(f, plane):
        arrived(f, 9 + plane, plane, 3)
        gather_start(f, 13 + plane, plane, 3, to_up, 0)
        gather_start(f, 4 * plane + 3, plane, 3, to_core)
        arrived(f, 11 + plane, plane, 1)
        gather_start(f, 15 + plane, plane, 1, to_down, 1)
        gather_start(f, 4 * plane + 1, plane, 1, to_core)

    def gather_y2(f, plane):
        arrived(f, 13 + plane, plane, 2, 0)
        arrived(f, 15 + plane, plane, 2, 1)
        gather_start(f, 4 * plane + 2, plane, 2, to_core)

    def gather_end(f):
        for plane in range(2):
            for dy in range(4):
                arrived(f, 4 * plane + dy, plane, dy, None, 1 - core)

    def gather_sent(f):
        copies = [gather_copy(f, 8, 0, 0, to_x)]
        for plane in range(2):
            copies += [gather_copy(f, 4 * plane + dy, plane, dy, to_core) for dy in range(4)]
            copies += [gather_copy(f, 9 + plane, plane, 0, to_up)]
            copies += [gather_copy(f, 11 + plane, plane, 0, to_down)]
            copies += [gather_copy(f, 13 + plane, plane, 3, to_up, 0)]
            copies += [gather_copy(f, 15 + plane, plane, 1, to_down, 1)]
        return copies

    cols = w.shape[1] // 2
    rows = 4 * HALF

    def half(i):
        return pl.ds(i * cols, cols)

    def block(distance):
        return pl.ds(pl.multiple_of(((z + distance) % 4) * rows, rows), rows)

    far_copy = [
        [
            remote(terms.at[f, block(2), half(i)], far_in.at[f, i], S_FAR + 2 * f + i, z_ways[i])
            for i in range(2)
        ]
        for f in range(2)
    ]
    plain_copy = [
        [
            remote(
                terms.at[f, block(1 + 2 * i), half(1 - i)], plain_in.at[f, i],
                S_PLAIN + 2 * f + i, z_ways[i],
            )
            for i in range(2)
        ]
        for f in range(2)
    ]
    later_copy = [
        [
            remote(added.at[f, i], added_in.at[f, i], S_LATER + 2 * f + i, z_ways[i])
            for i in range(2)
        ]
        for f in range(2)
    ]
    side_copy = [remote(side.at[f], side_in.at[f], S_SIDE + f, to_side) for f in range(2)]

    def project(f):
        for i in range(2):
            terms[f, :, half(i)] = jnp.dot(
                att[f], w[:, half(i)], preferred_element_type=jnp.float32
            ).astype(jnp.bfloat16)
            far_copy[f][i].start()
        for i in range(2):
            plain_copy[f][i].start()

    def reduce_added(f):
        for i in range(2):
            far_copy[f][i].wait_recv()
            added[f, i] = (
                terms[f, block(1 + 2 * i), half(i)].astype(jnp.float32)
                + far_in[f, i].astype(jnp.float32)
            ).astype(jnp.bfloat16)
            later_copy[f][i].start()

    def reduce_last(f):
        for i in range(2):
            plain_copy[f][i].wait_recv()
        for i in range(2):
            later_copy[f][i].wait_recv()

        def summed(s, i):
            size = rows // 2
            part = pl.ds(pl.multiple_of(s * size, size), size)
            own = pl.ds(pl.multiple_of(z * rows + s * size, size), size)
            return (
                terms[f, own, half(i)].astype(jnp.float32)
                + added_in[f, i, part].astype(jnp.float32)
                + plain_in[f, 1 - i, part].astype(jnp.float32)
            )

        for i in range(2):
            side[f, :, half(i)] = summed(1 - e, i).astype(jnp.bfloat16)
        side_copy[f].start()
        for i in range(2):
            mine[f, :, half(i)] = summed(e, i)

    def reduce_end(f):
        side_copy[f].wait_recv()
        done = (mine[f] + side_in[f].astype(jnp.float32)).astype(jnp.bfloat16)
        for i in range(2):
            start = i * RUN + f * HALF
            out_ref[start : start + HALF] = done[i * HALF : (i + 1) * HALF]

    def wait_all(*copies):
        for copy in copies:
            copy.wait_recv()

    def pass_on(arrival, *onward):
        arrival.wait_recv()
        for copy in onward:
            copy.start()

    def start_rest():
        wait_all(*own_core)
        own_up[1].start()
        own_down[1].start()

    before = [
        (0, start_rest),
        (1, lambda: wait_all(q_copy[0])),
        (2, lambda: wait_all(q_copy[1])),
        (3, lambda: pass_on(own_up[0], on_up, pass_12)),
        (3, lambda: pass_on(own_down[0], pass_4)),
        (5, lambda: wait_all(pass_12, pass_4)),
        (7, lambda: pass_on(own_down[1], on_down, pass_5)),
        (7, lambda: pass_on(own_up[1], pass_13)),
        (9, lambda: wait_all(pass_13, pass_5)),
        (11, lambda: pass_on(on_up, pass_8)),
        (11, lambda: pass_on(on_down, pass_9)),
        (13, lambda: wait_all(pass_8, pass_9)),
    ]
    after = [
        (14, lambda: finish_neighbour(0)),
        (15, lambda: finish_neighbour(1)),
    ]

    def run(events, u):
        for k in sorted({step for step, _ in events}):

            @pl.when(u == k)
            def _():
                for step, action in events:
                    if step == k:
                        action()

    def unit(u, carry):
        run(before, u)
        t = 2 * u
        score(t + 1, s1)
        weights, fade = weigh(t, s0)
        add_values(jnp.maximum(t - 1, 0), p1[...], fade1[...])
        score(jnp.minimum(t + 2, 31), s0)
        weights_1, fade_1 = weigh(t + 1, s1)
        add_values(t, weights, fade)
        p1[...] = weights_1
        fade1[...] = fade_1
        run(after, u)
        return carry

    p1[...] = jnp.zeros_like(p1)
    fade1[...] = jnp.ones_like(fade1)
    score(0, s0)
    lax.fori_loop(0, 16, unit, 0)
    combine(0)
    gather_own(0)
    add_values(31, p1[...], fade1[...])
    combine(1)
    gather_x(0)
    gather_y(0, 0)
    gather_own(1)
    gather_y(0, 1)
    gather_x(1)
    gather_y2(0, 0)
    gather_y(1, 0)
    gather_y2(0, 1)
    w_copy.wait()
    gather_end(0)
    project(0)
    gather_y(1, 1)
    gather_y2(1, 0)
    reduce_added(0)
    gather_y2(1, 1)
    gather_end(1)
    project(1)
    reduce_last(0)
    reduce_added(1)
    reduce_end(0)
    reduce_last(1)
    reduce_end(1)

    sent += side_copy
    for f in range(2):
        sent += gather_sent(f) + far_copy[f] + plain_copy[f] + later_copy[f]
    for copy in sent:
        copy.wait_send()


def body(queries, key_cache, value_cache, out_weight):
    tokens, width = queries.shape
    cols = out_weight.shape[1]
    all_rows = tokens // 2 * lax.axis_size("ctx")
    vmem, anywhere = pl.BlockSpec(memory_space=pltpu.VMEM), pl.BlockSpec(memory_space=pl.ANY)
    bf16, f32 = jnp.bfloat16, jnp.float32
    piece = pltpu.VMEM((2, 2, 2 * tokens, cols // 2), bf16)
    return pl.pallas_call(
        kernel,
        out_shape=jax.ShapeDtypeStruct((2 * tokens, cols), bf16),
        in_specs=[anywhere] * 4,
        out_specs=vmem,
        scratch_shapes=[
            pltpu.VMEM(queries.shape, bf16),
            pltpu.VMEM(key_cache.shape, bf16),
            pltpu.VMEM((4, ROWS, HD), bf16),
            pltpu.VMEM((16, 2 * KEYS, HD), bf16),
            pltpu.VMEM((ROWS, 2 * KEYS), f32),
            pltpu.VMEM((ROWS, 2 * KEYS), f32),
            pltpu.VMEM((ROWS, 2 * KEYS), bf16),
            pltpu.VMEM((ROWS, HD), f32),
            pltpu.VMEM((4, ROWS, 2 * HD), f32),
            pltpu.VMEM((4, ROWS, HD), f32),
            pltpu.VMEM((2, ROWS, HD), bf16),
            pltpu.VMEM((2, 8, ROWS), f32),
            pltpu.VMEM((2, ROWS, HD), bf16),
            pltpu.VMEM((2, 8, ROWS), f32),
            pltpu.VMEM((2, all_rows, width), bf16),
            pltpu.VMEM(out_weight.shape, bf16),
            pltpu.VMEM((2, all_rows, cols), bf16),
            piece,
            piece,
            piece,
            piece,
            pltpu.VMEM((2, tokens, cols), bf16),
            pltpu.VMEM((2, tokens, cols), bf16),
            pltpu.VMEM((2, tokens, cols), f32),
            pltpu.SemaphoreType.DMA((5,)),
            pltpu.SemaphoreType.DMA((S_COUNT,)),
            pltpu.SemaphoreType.DMA((S_COUNT,)),
        ],
        compiler_params=pltpu.CompilerParams(
            collective_id=0, has_side_effects=True, vmem_limit_bytes=56 * 1024 * 1024
        ),
        cost_estimate=pl.CostEstimate(
            flops=13_000_000_000, bytes_accessed=5_000_000, transcendentals=17_000_000
        ),
    )(queries, key_cache, value_cache, out_weight)


def solution(mesh):
    in_specs = (P("ctx", "head"), P("ctx", "head"), P("ctx", "head"), P("head", "ctx"))
    out_specs = P("head", "ctx")
    return jax.shard_map(body, mesh=mesh, in_specs=in_specs, out_specs=out_specs, check_vma=False)
```

```python
import math

import jax
import jax.numpy as jnp
from jax import lax
from jax.experimental import pallas as pl
from jax.experimental.pallas import tpu as pltpu
from jax.sharding import PartitionSpec as P

HD = 128
RUN = 64
NEG = -1e30
ROWS = 512
HALF = 32
KEYS = 512
LOG2E = math.log2(math.e)
MESH = pl.DeviceIdType.MESH

S_KV = 0
S_Q = 14
S_O = 16
S_STAT = 18
S_ATT = 20
S_FAR = 54
S_PLAIN = 58
S_LATER = 62
S_SIDE = 66
S_COUNT = 68


def device_at(x, y, core):
    return x * 8 + y * 2 + core


def kernel(
    q_hbm, k_hbm, v_hbm, w_hbm, out_ref,
    q_ref, k_ref, q_s, kv, s0, s1, p1, fade1, acc, mrow, o_send, s_send, o_recv, s_recv,
    att, w, terms, far_in, plain_in, added, added_in, side, side_in, mine, fetched, send, recv,
):
    c, h = lax.axis_index("ctx"), lax.axis_index("head")
    x, y, core = c // 8, (c // 2) % 4, c % 2
    z, e = h // 2, h % 2
    scale = LOG2E / math.sqrt(HD)

    to_core = (device_at(x, y, 1 - core), h)
    to_up = (device_at(x, (y + 1) % 4, core), h)
    to_down = (device_at(x, (y + 3) % 4, core), h)
    to_x = (device_at(1 - x, y, core), h)
    z_ways = ((c, ((z + 1) % 4) * 2 + e), (c, ((z + 3) % 4) * 2 + e))
    to_side = (c, z * 2 + 1 - e)
    partners = (to_core, to_up, to_down, to_x, to_side) + z_ways

    def remote(src, dst, number, where):
        return pltpu.make_async_remote_copy(
            src_ref=src, dst_ref=dst, send_sem=send.at[number], recv_sem=recv.at[number],
            device_id=where, device_id_type=MESH,
        )

    q_fetch = pltpu.make_async_copy(q_hbm, q_ref, fetched.at[0])
    k_fetch = pltpu.make_async_copy(k_hbm, k_ref, fetched.at[1])
    v_fetch = [
        pltpu.make_async_copy(
            v_hbm.at[pl.ds(i * KEYS, KEYS)], kv.at[i, pl.ds(0, KEYS)], fetched.at[2 + i]
        )
        for i in range(2)
    ]
    w_copy = pltpu.make_async_copy(w_hbm, w, fetched.at[4])
    for fetch in [k_fetch, q_fetch] + v_fetch:
        fetch.start()
    barrier = pltpu.get_barrier_semaphore()
    for partner in partners:
        pl.semaphore_signal(barrier, inc=1, device_id=partner, device_id_type=MESH)

    k_fetch.wait()
    for half in range(2):
        for b in range(4):
            start = half * KEYS + b * HD
            piece = k_ref[start : start + HD].astype(jnp.float32)
            kv[half, KEYS + b * HD : KEYS + (b + 1) * HD] = piece.T.astype(jnp.bfloat16)
    q_fetch.wait()
    for r in range(2):
        for i in range(16):
            q_s[r, i * HALF : (i + 1) * HALF] = q_ref[
                r * HALF : (r + 1) * HALF, i * HD : (i + 1) * HD
            ]
    for fetch in v_fetch:
        fetch.wait()
    w_copy.start()
    pl.semaphore_wait(barrier, len(partners))

    def kv_copy(number, source, target, where):
        return remote(kv.at[source], kv.at[target], S_KV + number, where)

    own_up = [kv_copy(0 + i, i, 12 + i, to_up) for i in range(2)]
    own_down = [kv_copy(2 + i, i, 4 + i, to_down) for i in range(2)]
    own_core = [kv_copy(4 + i, i, 2 + i, to_core) for i in range(2)]
    pass_12 = kv_copy(6, 12, 14, to_core)
    pass_4 = kv_copy(7, 4, 6, to_core)
    pass_13 = kv_copy(8, 13, 15, to_core)
    pass_5 = kv_copy(9, 5, 7, to_core)
    on_up = kv_copy(10, 12, 8, to_up)
    on_down = kv_copy(11, 5, 9, to_down)
    pass_8 = kv_copy(12, 8, 10, to_core)
    pass_9 = kv_copy(13, 9, 11, to_core)
    q_copy = [remote(q_s.at[i], q_s.at[2 + i], S_Q + i, to_x) for i in range(2)]
    o_copy = [remote(o_send.at[f], o_recv.at[f], S_O + f, to_x) for f in range(2)]
    s_copy = [remote(s_send.at[f], s_recv.at[f], S_STAT + f, to_x) for f in range(2)]

    for i in range(2):
        own_core[i].start()
    q_copy[0].start()
    own_up[0].start()
    own_down[0].start()
    q_copy[1].start()
    for r in range(4):
        acc[r] = jnp.zeros((ROWS, 2 * HD), jnp.float32)
        mrow[r] = jnp.full((ROWS, HD), NEG, jnp.float32)

    def place(t):
        v = t % 8
        early = jnp.where(v < 4, 4 + v // 2, 6 + v % 2)
        early_row = jnp.where(v < 4, v % 2, 1 - (v - 4) // 2) * 2
        pair = jnp.where(t < 8, t // 2 % 2, jnp.where(t < 16, t // 4, early))
        pair = jnp.where(t < 24, pair, 4 + t % 4)
        row = jnp.where(t < 8, t // 4 * 2 + t % 2, jnp.where(t < 16, t % 4, early_row))
        row = jnp.where(t < 24, row, (1 - v // 4) * 2 + 1)
        i = pair - 2
        middle = 12 + 2 * (i % 2) + i // 2
        one = jnp.where(pair < 2, 2 * pair, jnp.where(pair < 6, middle, 2 * pair - 4))
        two = jnp.where((pair >= 2) & (pair < 6), one - 8, one + 1)
        return one, two, row

    def score(t, s_ref):
        one, two, row = place(t)
        queries = q_s[row]
        for j, slot in enumerate((one, two)):
            keys = jnp.concatenate(
                [kv[slot, KEYS + b * HD : KEYS + (b + 1) * HD] for b in range(4)], axis=1
            )
            s_ref[:, j * KEYS : (j + 1) * KEYS] = (
                jnp.dot(queries, keys, preferred_element_type=jnp.float32) * scale
            )

    def weigh(t, s_ref):
        one, two, row = place(t)
        asker = device_at(jnp.where(row >= 2, 1 - x, x), y, core)
        token = lax.broadcasted_iota(jnp.int32, (ROWS, HD), 0) % HALF
        key_token = lax.broadcasted_iota(jnp.int32, (ROWS, HD), 1) - RUN
        pieces = []
        for j, slot in enumerate((one, two)):
            holder_core = jnp.where((slot // 2) % 2 == 1, 1 - core, core)
            holder = device_at(x, (y + slot // 4) % 4, holder_core)
            first = jnp.where(slot % 2 == 1, holder * RUN, -(1 << 20))
            limit = asker * RUN + (row % 2) * HALF - first
            end = (j + 1) * KEYS
            seen = (key_token < 0) | (key_token - token <= limit)
            pieces.append(s_ref[:, j * KEYS : end - HD])
            pieces.append(jnp.where(seen, s_ref[:, end - HD : end], NEG))
        scores = jnp.concatenate(pieces, axis=1)
        old = mrow[row]
        new = jnp.maximum(old, jnp.max(scores, axis=1, keepdims=True))
        weights = jnp.exp2(scores - jnp.concatenate([new] * (2 * KEYS // HD), axis=1))
        mrow[row] = new
        return weights.astype(jnp.bfloat16), jnp.exp2(old - new)

    def add_values(t, weights, fade):
        one, two, row = place(t)
        ones = jnp.ones((KEYS, HD), jnp.bfloat16)
        values = jnp.concatenate(
            [jnp.concatenate([kv[slot, 0:KEYS], ones], axis=1) for slot in (one, two)], axis=0
        )
        acc[row] = acc[row] * jnp.concatenate([fade, fade], axis=1) + jnp.dot(
            weights, values, preferred_element_type=jnp.float32
        )

    def normalised(row):
        total = acc[row, :, HD : 2 * HD]
        return acc[row, :, 0:HD] / total, mrow[row] + jnp.log(total) * LOG2E

    def finish_neighbour(f):
        value, level = normalised(2 + f)
        o_send[f] = value.astype(jnp.bfloat16)
        s_send[f] = level.T[0:8]
        o_copy[f].start()
        s_copy[f].start()

    def block_of(owner):
        start = owner * HALF
        return start if isinstance(start, int) else pl.multiple_of(start, HALF)

    def combine(f):
        value, level = normalised(f)
        o_copy[f].wait_recv()
        s_copy[f].wait_recv()
        other = jnp.broadcast_to(s_recv[f, 0:1], (HD, ROWS)).T
        top = jnp.maximum(level, other)
        part_a, part_b = jnp.exp2(level - top), jnp.exp2(other - top)
        done = (value * part_a + o_recv[f].astype(jnp.float32) * part_b) / (part_a + part_b)
        done = done.astype(jnp.bfloat16)
        for i in range(16):
            att[f, pl.ds(block_of(c), HALF), i * HD : (i + 1) * HD] = done[
                i * HALF : (i + 1) * HALF
            ]

    def gather_copy(f, number, dx, dy, where, part=None, from_core=None):
        owner = device_at(1 - x if dx else x, (y + dy) % 4, core if from_core is None else from_core)
        start, size = block_of(owner), HALF
        if part is not None:
            size = HALF // 2
            start = pl.multiple_of(start + part * size, size)
        block = att.at[f, pl.ds(start, size)]
        return remote(block, block, S_ATT + 17 * f + number, where)

    sent = own_up + own_down + own_core + [pass_12, pass_4, pass_13, pass_5, on_up, on_down]
    sent += [pass_8, pass_9] + q_copy + o_copy + s_copy

    def arrived(f, number, dx, dy, part=None, from_core=None):
        gather_copy(f, number, dx, dy, to_core, part, from_core).wait_recv()

    def gather_start(f, *args):
        gather_copy(f, *args).start()

    def gather_own(f):
        gather_start(f, 8, 0, 0, to_x)
        gather_start(f, 9, 0, 0, to_up)
        gather_start(f, 11, 0, 0, to_down)
        gather_start(f, 0, 0, 0, to_core)

    def gather_x(f):
        arrived(f, 8, 1, 0)
        gather_start(f, 10, 1, 0, to_up)
        gather_start(f, 12, 1, 0, to_down)
        gather_start(f, 4, 1, 0, to_core)

    def gather_y(f, plane):
        arrived(f, 9 + plane, plane, 3)
        gather_start(f, 13 + plane, plane, 3, to_up, 0)
        gather_start(f, 4 * plane + 3, plane, 3, to_core)
        arrived(f, 11 + plane, plane, 1)
        gather_start(f, 15 + plane, plane, 1, to_down, 1)
        gather_start(f, 4 * plane + 1, plane, 1, to_core)

    def gather_y2(f, plane):
        arrived(f, 13 + plane, plane, 2, 0)
        arrived(f, 15 + plane, plane, 2, 1)
        gather_start(f, 4 * plane + 2, plane, 2, to_core)

    def gather_end(f):
        for plane in range(2):
            for dy in range(4):
                arrived(f, 4 * plane + dy, plane, dy, None, 1 - core)

    def gather_sent(f):
        copies = [gather_copy(f, 8, 0, 0, to_x)]
        for plane in range(2):
            copies += [gather_copy(f, 4 * plane + dy, plane, dy, to_core) for dy in range(4)]
            copies += [gather_copy(f, 9 + plane, plane, 0, to_up)]
            copies += [gather_copy(f, 11 + plane, plane, 0, to_down)]
            copies += [gather_copy(f, 13 + plane, plane, 3, to_up, 0)]
            copies += [gather_copy(f, 15 + plane, plane, 1, to_down, 1)]
        return copies

    cols = w.shape[1] // 2
    rows = 4 * HALF

    def half(i):
        return pl.ds(i * cols, cols)

    def block(distance):
        return pl.ds(pl.multiple_of(((z + distance) % 4) * rows, rows), rows)

    far_copy = [
        [
            remote(terms.at[f, block(2), half(i)], far_in.at[f, i], S_FAR + 2 * f + i, z_ways[i])
            for i in range(2)
        ]
        for f in range(2)
    ]
    plain_copy = [
        [
            remote(
                terms.at[f, block(1 + 2 * i), half(1 - i)], plain_in.at[f, i],
                S_PLAIN + 2 * f + i, z_ways[i],
            )
            for i in range(2)
        ]
        for f in range(2)
    ]
    later_copy = [
        [
            remote(added.at[f, i], added_in.at[f, i], S_LATER + 2 * f + i, z_ways[i])
            for i in range(2)
        ]
        for f in range(2)
    ]
    side_copy = [remote(side.at[f], side_in.at[f], S_SIDE + f, to_side) for f in range(2)]

    def project(f, part):
        lanes = slice(part * (cols // 2), (part + 1) * (cols // 2))
        terms[f, :, lanes] = jnp.dot(
            att[f], w[:, lanes], preferred_element_type=jnp.float32
        ).astype(jnp.bfloat16)
        if part % 2 == 1:
            i = part // 2
            far_copy[f][i].start()
            plain_copy[f][1 - i].start()

    def reduce_added(f):
        for i in range(2):
            far_copy[f][i].wait_recv()
            added[f, i] = (
                terms[f, block(1 + 2 * i), half(i)].astype(jnp.float32)
                + far_in[f, i].astype(jnp.float32)
            ).astype(jnp.bfloat16)
            later_copy[f][i].start()

    def reduce_last(f):
        for i in range(2):
            plain_copy[f][i].wait_recv()
        for i in range(2):
            later_copy[f][i].wait_recv()

        def summed(s, i):
            size = rows // 2
            part = pl.ds(pl.multiple_of(s * size, size), size)
            own = pl.ds(pl.multiple_of(z * rows + s * size, size), size)
            return (
                terms[f, own, half(i)].astype(jnp.float32)
                + added_in[f, i, part].astype(jnp.float32)
                + plain_in[f, 1 - i, part].astype(jnp.float32)
            )

        for i in range(2):
            side[f, :, half(i)] = summed(1 - e, i).astype(jnp.bfloat16)
        side_copy[f].start()
        for i in range(2):
            mine[f, :, half(i)] = summed(e, i)

    def reduce_end(f):
        side_copy[f].wait_recv()
        done = (mine[f] + side_in[f].astype(jnp.float32)).astype(jnp.bfloat16)
        for i in range(2):
            start = i * RUN + f * HALF
            out_ref[start : start + HALF] = done[i * HALF : (i + 1) * HALF]

    def wait_all(*copies):
        for copy in copies:
            copy.wait_recv()

    def pass_on(arrival, *onward):
        arrival.wait_recv()
        for copy in onward:
            copy.start()

    def start_rest():
        wait_all(*own_core)
        own_up[1].start()
        own_down[1].start()

    before = [
        (0, start_rest),
        (1, lambda: wait_all(q_copy[0])),
        (2, lambda: wait_all(q_copy[1])),
        (3, lambda: pass_on(own_up[0], on_up, pass_12)),
        (3, lambda: pass_on(own_down[0], pass_4)),
        (5, lambda: wait_all(pass_12, pass_4)),
        (7, lambda: pass_on(own_down[1], on_down, pass_5)),
        (7, lambda: pass_on(own_up[1], pass_13)),
        (8, lambda: wait_all(pass_13, pass_5)),
        (9, lambda: pass_on(on_up, pass_8)),
        (9, lambda: pass_on(on_down, pass_9)),
        (10, lambda: wait_all(pass_8, pass_9)),
    ]
    after = [
        (11, lambda: finish_neighbour(0)),
        (13, lambda: combine(0)),
        (13, lambda: gather_own(0)),
        (14, lambda: finish_neighbour(1)),
        (15, lambda: gather_x(0)),
    ]

    def run(events, u):
        for k in sorted({step for step, _ in events}):

            @pl.when(u == k)
            def _():
                for step, action in events:
                    if step == k:
                        action()

    def unit(u, carry):
        run(before, u)
        t = 2 * u
        score(t + 1, s1)
        weights, fade = weigh(t, s0)
        add_values(jnp.maximum(t - 1, 0), p1[...], fade1[...])
        score(jnp.minimum(t + 2, 31), s0)
        weights_1, fade_1 = weigh(t + 1, s1)
        add_values(t, weights, fade)
        p1[...] = weights_1
        fade1[...] = fade_1
        run(after, u)
        return carry

    p1[...] = jnp.zeros_like(p1)
    fade1[...] = jnp.ones_like(fade1)
    score(0, s0)
    lax.fori_loop(0, 16, unit, 0)
    add_values(31, p1[...], fade1[...])
    combine(1)
    gather_own(1)
    gather_y(0, 0)
    gather_y(0, 1)
    gather_x(1)
    gather_y2(0, 0)
    gather_y(1, 0)
    gather_y2(0, 1)
    w_copy.wait()
    gather_end(0)
    project(0, 0)
    gather_y(1, 1)
    project(0, 1)
    gather_y2(1, 0)
    project(0, 2)
    gather_y2(1, 1)
    project(0, 3)
    gather_end(1)
    project(1, 0)
    project(1, 1)
    reduce_added(0)
    project(1, 2)
    project(1, 3)
    reduce_last(0)
    reduce_added(1)
    reduce_end(0)
    reduce_last(1)
    reduce_end(1)

    sent += side_copy
    for f in range(2):
        sent += gather_sent(f) + far_copy[f] + plain_copy[f] + later_copy[f]
    for copy in sent:
        copy.wait_send()


def body(queries, key_cache, value_cache, out_weight):
    tokens, width = queries.shape
    cols = out_weight.shape[1]
    all_rows = tokens // 2 * lax.axis_size("ctx")
    vmem, anywhere = pl.BlockSpec(memory_space=pltpu.VMEM), pl.BlockSpec(memory_space=pl.ANY)
    bf16, f32 = jnp.bfloat16, jnp.float32
    piece = pltpu.VMEM((2, 2, 2 * tokens, cols // 2), bf16)
    return pl.pallas_call(
        kernel,
        out_shape=jax.ShapeDtypeStruct((2 * tokens, cols), bf16),
        in_specs=[anywhere] * 4,
        out_specs=vmem,
        scratch_shapes=[
            pltpu.VMEM(queries.shape, bf16),
            pltpu.VMEM(key_cache.shape, bf16),
            pltpu.VMEM((4, ROWS, HD), bf16),
            pltpu.VMEM((16, 2 * KEYS, HD), bf16),
            pltpu.VMEM((ROWS, 2 * KEYS), f32),
            pltpu.VMEM((ROWS, 2 * KEYS), f32),
            pltpu.VMEM((ROWS, 2 * KEYS), bf16),
            pltpu.VMEM((ROWS, HD), f32),
            pltpu.VMEM((4, ROWS, 2 * HD), f32),
            pltpu.VMEM((4, ROWS, HD), f32),
            pltpu.VMEM((2, ROWS, HD), bf16),
            pltpu.VMEM((2, 8, ROWS), f32),
            pltpu.VMEM((2, ROWS, HD), bf16),
            pltpu.VMEM((2, 8, ROWS), f32),
            pltpu.VMEM((2, all_rows, width), bf16),
            pltpu.VMEM(out_weight.shape, bf16),
            pltpu.VMEM((2, all_rows, cols), bf16),
            piece,
            piece,
            piece,
            piece,
            pltpu.VMEM((2, tokens, cols), bf16),
            pltpu.VMEM((2, tokens, cols), bf16),
            pltpu.VMEM((2, tokens, cols), f32),
            pltpu.SemaphoreType.DMA((5,)),
            pltpu.SemaphoreType.DMA((S_COUNT,)),
            pltpu.SemaphoreType.DMA((S_COUNT,)),
        ],
        compiler_params=pltpu.CompilerParams(
            collective_id=0, has_side_effects=True, vmem_limit_bytes=56 * 1024 * 1024
        ),
        cost_estimate=pl.CostEstimate(
            flops=13_000_000_000, bytes_accessed=5_000_000, transcendentals=17_000_000
        ),
    )(queries, key_cache, value_cache, out_weight)


def solution(mesh):
    in_specs = (P("ctx", "head"), P("ctx", "head"), P("ctx", "head"), P("head", "ctx"))
    out_specs = P("head", "ctx")
    return jax.shard_map(body, mesh=mesh, in_specs=in_specs, out_specs=out_specs, check_vma=False)
```

```python
import math

import jax
import jax.numpy as jnp
from jax import lax
from jax.experimental import pallas as pl
from jax.experimental.pallas import tpu as pltpu
from jax.sharding import PartitionSpec as P

HD = 128
RUN = 64
NEG = -1e30
ROWS = 512
HALF = 32
KEYS = 512
LOG2E = math.log2(math.e)
MESH = pl.DeviceIdType.MESH

S_KV = 0
S_Q = 14
S_O = 16
S_STAT = 18
S_ATT = 20
S_COUNT = 54


def device_at(x, y, core):
    return x * 8 + y * 2 + core


def attend_kernel(
    q_hbm, k_hbm, v_hbm, att,
    q_ref, k_ref, q_s, kv, s0, s1, p1, fade1, acc, mrow, o_send, s_send, o_recv, s_recv,
    own, fetched, send, recv,
):
    c, h = lax.axis_index("ctx"), lax.axis_index("head")
    x, y, core = c // 8, (c // 2) % 4, c % 2
    scale = LOG2E / math.sqrt(HD)

    to_core = (device_at(x, y, 1 - core), h)
    to_up = (device_at(x, (y + 1) % 4, core), h)
    to_down = (device_at(x, (y + 3) % 4, core), h)
    to_x = (device_at(1 - x, y, core), h)
    partners = (to_core, to_up, to_down, to_x)

    def remote(src, dst, number, where):
        return pltpu.make_async_remote_copy(
            src_ref=src, dst_ref=dst, send_sem=send.at[number], recv_sem=recv.at[number],
            device_id=where, device_id_type=MESH,
        )

    q_fetch = pltpu.make_async_copy(q_hbm, q_ref, fetched.at[0])
    k_fetch = pltpu.make_async_copy(k_hbm, k_ref, fetched.at[1])
    v_fetch = [
        pltpu.make_async_copy(
            v_hbm.at[pl.ds(i * KEYS, KEYS)], kv.at[i, pl.ds(0, KEYS)], fetched.at[2 + i]
        )
        for i in range(2)
    ]
    for fetch in [k_fetch, q_fetch] + v_fetch:
        fetch.start()
    barrier = pltpu.get_barrier_semaphore()
    for partner in partners:
        pl.semaphore_signal(barrier, inc=1, device_id=partner, device_id_type=MESH)

    k_fetch.wait()
    for half in range(2):
        for b in range(4):
            start = half * KEYS + b * HD
            piece = k_ref[start : start + HD].astype(jnp.float32)
            kv[half, KEYS + b * HD : KEYS + (b + 1) * HD] = piece.T.astype(jnp.bfloat16)
    q_fetch.wait()
    for r in range(2):
        for i in range(16):
            q_s[r, i * HALF : (i + 1) * HALF] = q_ref[
                r * HALF : (r + 1) * HALF, i * HD : (i + 1) * HD
            ]
    for fetch in v_fetch:
        fetch.wait()
    pl.semaphore_wait(barrier, len(partners))

    def kv_copy(number, source, target, where):
        return remote(kv.at[source], kv.at[target], S_KV + number, where)

    own_up = [kv_copy(0 + i, i, 12 + i, to_up) for i in range(2)]
    own_down = [kv_copy(2 + i, i, 4 + i, to_down) for i in range(2)]
    own_core = [kv_copy(4 + i, i, 2 + i, to_core) for i in range(2)]
    pass_12 = kv_copy(6, 12, 14, to_core)
    pass_4 = kv_copy(7, 4, 6, to_core)
    pass_13 = kv_copy(8, 13, 15, to_core)
    pass_5 = kv_copy(9, 5, 7, to_core)
    on_up = kv_copy(10, 12, 8, to_up)
    on_down = kv_copy(11, 5, 9, to_down)
    pass_8 = kv_copy(12, 8, 10, to_core)
    pass_9 = kv_copy(13, 9, 11, to_core)
    q_copy = [remote(q_s.at[i], q_s.at[2 + i], S_Q + i, to_x) for i in range(2)]
    o_copy = [remote(o_send.at[f], o_recv.at[f], S_O + f, to_x) for f in range(2)]
    s_copy = [remote(s_send.at[f], s_recv.at[f], S_STAT + f, to_x) for f in range(2)]

    for i in range(2):
        own_core[i].start()
    q_copy[0].start()
    own_up[0].start()
    own_down[0].start()
    q_copy[1].start()
    for r in range(4):
        acc[r] = jnp.zeros((ROWS, 2 * HD), jnp.float32)
        mrow[r] = jnp.full((ROWS, HD), NEG, jnp.float32)

    def place(t):
        v = t % 8
        early = jnp.where(v < 4, 4 + v // 2, 6 + v % 2)
        early_row = jnp.where(v < 4, v % 2, 1 - (v - 4) // 2) * 2
        pair = jnp.where(t < 8, t // 2 % 2, jnp.where(t < 16, t // 4, early))
        pair = jnp.where(t < 24, pair, 4 + t % 4)
        row = jnp.where(t < 8, t // 4 * 2 + t % 2, jnp.where(t < 16, t % 4, early_row))
        row = jnp.where(t < 24, row, (1 - v // 4) * 2 + 1)
        i = pair - 2
        middle = 12 + 2 * (i % 2) + i // 2
        one = jnp.where(pair < 2, 2 * pair, jnp.where(pair < 6, middle, 2 * pair - 4))
        two = jnp.where((pair >= 2) & (pair < 6), one - 8, one + 1)
        return one, two, row

    def score(t, s_ref):
        one, two, row = place(t)
        queries = q_s[row]
        for j, slot in enumerate((one, two)):
            keys = jnp.concatenate(
                [kv[slot, KEYS + b * HD : KEYS + (b + 1) * HD] for b in range(4)], axis=1
            )
            s_ref[:, j * KEYS : (j + 1) * KEYS] = (
                jnp.dot(queries, keys, preferred_element_type=jnp.float32) * scale
            )

    def weigh(t, s_ref):
        one, two, row = place(t)
        asker = device_at(jnp.where(row >= 2, 1 - x, x), y, core)
        token = lax.broadcasted_iota(jnp.int32, (ROWS, HD), 0) % HALF
        key_token = lax.broadcasted_iota(jnp.int32, (ROWS, HD), 1) - RUN
        pieces = []
        for j, slot in enumerate((one, two)):
            holder_core = jnp.where((slot // 2) % 2 == 1, 1 - core, core)
            holder = device_at(x, (y + slot // 4) % 4, holder_core)
            first = jnp.where(slot % 2 == 1, holder * RUN, -(1 << 20))
            limit = asker * RUN + (row % 2) * HALF - first
            end = (j + 1) * KEYS
            seen = (key_token < 0) | (key_token - token <= limit)
            pieces.append(s_ref[:, j * KEYS : end - HD])
            pieces.append(jnp.where(seen, s_ref[:, end - HD : end], NEG))
        scores = jnp.concatenate(pieces, axis=1)
        old = mrow[row]
        new = jnp.maximum(old, jnp.max(scores, axis=1, keepdims=True))
        weights = jnp.exp2(scores - jnp.concatenate([new] * (2 * KEYS // HD), axis=1))
        mrow[row] = new
        return weights.astype(jnp.bfloat16), jnp.exp2(old - new)

    def add_values(t, weights, fade):
        one, two, row = place(t)
        ones = jnp.ones((KEYS, HD), jnp.bfloat16)
        values = jnp.concatenate(
            [jnp.concatenate([kv[slot, 0:KEYS], ones], axis=1) for slot in (one, two)], axis=0
        )
        acc[row] = acc[row] * jnp.concatenate([fade, fade], axis=1) + jnp.dot(
            weights, values, preferred_element_type=jnp.float32
        )

    def normalised(row):
        total = acc[row, :, HD : 2 * HD]
        return acc[row, :, 0:HD] / total, mrow[row] + jnp.log(total) * LOG2E

    def finish_neighbour(f):
        value, level = normalised(2 + f)
        o_send[f] = value.astype(jnp.bfloat16)
        s_send[f] = level.T[0:8]
        o_copy[f].start()
        s_copy[f].start()

    def block_of(owner):
        start = owner * HALF
        return start if isinstance(start, int) else pl.multiple_of(start, HALF)

    keep = [
        pltpu.make_async_copy(own.at[f], att.at[f, pl.ds(block_of(c), HALF)], fetched.at[4 + f])
        for f in range(2)
    ]

    def combine(f):
        value, level = normalised(f)
        o_copy[f].wait_recv()
        s_copy[f].wait_recv()
        other = jnp.broadcast_to(s_recv[f, 0:1], (HD, ROWS)).T
        top = jnp.maximum(level, other)
        part_a, part_b = jnp.exp2(level - top), jnp.exp2(other - top)
        done = (value * part_a + o_recv[f].astype(jnp.float32) * part_b) / (part_a + part_b)
        done = done.astype(jnp.bfloat16)
        for i in range(16):
            own[f, :, i * HD : (i + 1) * HD] = done[i * HALF : (i + 1) * HALF]
        keep[f].start()

    def gather_copy(f, number, dx, dy, where, part=None, from_core=None):
        owner = device_at(1 - x if dx else x, (y + dy) % 4, core if from_core is None else from_core)
        start, size = block_of(owner), HALF
        if part is not None:
            size = HALF // 2
            start = pl.multiple_of(start + part * size, size)
        block = att.at[f, pl.ds(start, size)]
        mine = dx == 0 and dy == 0 and from_core is None
        return remote(own.at[f] if mine else block, block, S_ATT + 17 * f + number, where)

    sent = own_up + own_down + own_core + [pass_12, pass_4, pass_13, pass_5, on_up, on_down]
    sent += [pass_8, pass_9] + q_copy + o_copy + s_copy

    def arrived(f, number, dx, dy, part=None, from_core=None):
        gather_copy(f, number, dx, dy, to_core, part, from_core).wait_recv()

    def gather_start(f, *args):
        gather_copy(f, *args).start()

    def gather_own(f):
        gather_start(f, 8, 0, 0, to_x)
        gather_start(f, 9, 0, 0, to_up)
        gather_start(f, 11, 0, 0, to_down)
        gather_start(f, 0, 0, 0, to_core)

    def gather_x(f):
        arrived(f, 8, 1, 0)
        gather_start(f, 10, 1, 0, to_up)
        gather_start(f, 12, 1, 0, to_down)
        gather_start(f, 4, 1, 0, to_core)

    def gather_y(f, plane):
        arrived(f, 9 + plane, plane, 3)
        gather_start(f, 13 + plane, plane, 3, to_up, 0)
        gather_start(f, 4 * plane + 3, plane, 3, to_core)
        arrived(f, 11 + plane, plane, 1)
        gather_start(f, 15 + plane, plane, 1, to_down, 1)
        gather_start(f, 4 * plane + 1, plane, 1, to_core)

    def gather_y2(f, plane):
        arrived(f, 13 + plane, plane, 2, 0)
        arrived(f, 15 + plane, plane, 2, 1)
        gather_start(f, 4 * plane + 2, plane, 2, to_core)

    def gather_end(f):
        for plane in range(2):
            for dy in range(4):
                arrived(f, 4 * plane + dy, plane, dy, None, 1 - core)

    def gather_sent(f):
        copies = [gather_copy(f, 8, 0, 0, to_x)]
        for plane in range(2):
            copies += [gather_copy(f, 4 * plane + dy, plane, dy, to_core) for dy in range(4)]
            copies += [gather_copy(f, 9 + plane, plane, 0, to_up)]
            copies += [gather_copy(f, 11 + plane, plane, 0, to_down)]
            copies += [gather_copy(f, 13 + plane, plane, 3, to_up, 0)]
            copies += [gather_copy(f, 15 + plane, plane, 1, to_down, 1)]
        return copies

    def wait_all(*copies):
        for copy in copies:
            copy.wait_recv()

    def pass_on(arrival, *onward):
        arrival.wait_recv()
        for copy in onward:
            copy.start()

    def start_rest():
        wait_all(*own_core)
        own_up[1].start()
        own_down[1].start()

    before = [
        (0, start_rest),
        (1, lambda: wait_all(q_copy[0])),
        (2, lambda: wait_all(q_copy[1])),
        (3, lambda: pass_on(own_up[0], on_up, pass_12)),
        (3, lambda: pass_on(own_down[0], pass_4)),
        (5, lambda: wait_all(pass_12, pass_4)),
        (7, lambda: pass_on(own_down[1], on_down, pass_5)),
        (7, lambda: pass_on(own_up[1], pass_13)),
        (8, lambda: wait_all(pass_13, pass_5)),
        (9, lambda: pass_on(on_up, pass_8)),
        (9, lambda: pass_on(on_down, pass_9)),
        (10, lambda: wait_all(pass_8, pass_9)),
    ]
    after = [
        (11, lambda: finish_neighbour(0)),
        (13, lambda: combine(0)),
        (13, lambda: gather_own(0)),
        (14, lambda: finish_neighbour(1)),
        (15, lambda: gather_x(0)),
    ]

    def run(events, u):
        for k in sorted({step for step, _ in events}):

            @pl.when(u == k)
            def _():
                for step, action in events:
                    if step == k:
                        action()

    def unit(u, carry):
        run(before, u)
        t = 2 * u
        score(t + 1, s1)
        weights, fade = weigh(t, s0)
        add_values(jnp.maximum(t - 1, 0), p1[...], fade1[...])
        score(jnp.minimum(t + 2, 31), s0)
        weights_1, fade_1 = weigh(t + 1, s1)
        add_values(t, weights, fade)
        p1[...] = weights_1
        fade1[...] = fade_1
        run(after, u)
        return carry

    p1[...] = jnp.zeros_like(p1)
    fade1[...] = jnp.ones_like(fade1)
    score(0, s0)
    lax.fori_loop(0, 16, unit, 0)
    add_values(31, p1[...], fade1[...])
    combine(1)
    gather_own(1)
    gather_y(0, 0)
    gather_y(0, 1)
    gather_x(1)
    gather_y2(0, 0)
    gather_y(1, 0)
    gather_y2(0, 1)
    gather_y(1, 1)
    gather_y2(1, 0)
    gather_y2(1, 1)
    gather_end(0)
    gather_end(1)

    for f in range(2):
        keep[f].wait()
        sent += gather_sent(f)
    for copy in sent:
        copy.wait_send()


def reduce_kernel(terms, out_ref, far_in, plain_in, added, added_in, side, side_in, send, recv):
    c, h = lax.axis_index("ctx"), lax.axis_index("head")
    z, e = h // 2, h % 2
    cols = out_ref.shape[1] // 2
    size = 2 * HALF
    ways = ((c, ((z + 1) % 4) * 2 + e), (c, ((z + 3) % 4) * 2 + e))
    to_side = (c, z * 2 + 1 - e)

    barrier = pltpu.get_barrier_semaphore()
    for partner in ways + (to_side,):
        pl.semaphore_signal(barrier, inc=1, device_id=partner, device_id_type=MESH)
    pl.semaphore_wait(barrier, 3)

    def copy_of(number, source, target, where):
        return pltpu.make_async_remote_copy(
            src_ref=source, dst_ref=target, send_sem=send.at[number], recv_sem=recv.at[number],
            device_id=where, device_id_type=MESH,
        )

    def half(i):
        return pl.ds(i * cols, cols)

    def block(distance, g):
        side_of = e if g == 1 else 1 - e
        return pl.ds(pl.multiple_of((((z + distance) % 4) * 2 + side_of) * size, size), size)

    both = pl.ds(0, 2)
    far = [
        [
            copy_of(2 * g + i, terms.at[both, block(2, g), half(i)], far_in.at[g, i], ways[i])
            for i in range(2)
        ]
        for g in range(2)
    ]
    plain = [
        [
            copy_of(
                4 + 2 * g + i, terms.at[both, block(1 + 2 * i, g), half(1 - i)],
                plain_in.at[g, i], ways[i],
            )
            for i in range(2)
        ]
        for g in range(2)
    ]
    later = [
        [copy_of(8 + 2 * g + i, added.at[g, i], added_in.at[g, i], ways[i]) for i in range(2)]
        for g in range(2)
    ]
    across = copy_of(12, side, side_in, to_side)

    def add_on(g):
        for i in range(2):
            far[g][i].wait_recv()
            added[g, i] = (
                terms[:, block(1 + 2 * i, g), half(i)].astype(jnp.float32)
                + far_in[g, i].astype(jnp.float32)
            ).astype(jnp.bfloat16)
            later[g][i].start()

    def summed(g, i):
        return (
            terms[:, block(0, g), half(i)].astype(jnp.float32)
            + added_in[g, i].astype(jnp.float32)
            + plain_in[g, 1 - i].astype(jnp.float32)
        )

    def wait_sums(g):
        for i in range(2):
            plain[g][i].wait_recv()
        for i in range(2):
            later[g][i].wait_recv()

    for copies in far + plain[:1]:
        for copy in copies:
            copy.start()
    add_on(0)
    for copy in plain[1]:
        copy.start()
    add_on(1)
    wait_sums(0)
    for i in range(2):
        side[:, :, half(i)] = summed(0, i).astype(jnp.bfloat16)
    across.start()
    wait_sums(1)
    across.wait_recv()
    for i in range(2):
        done = (summed(1, i) + side_in[:, :, half(i)].astype(jnp.float32)).astype(jnp.bfloat16)
        for f in range(2):
            for k in range(2):
                start = k * RUN + f * HALF
                out_ref[start : start + HALF, half(i)] = done[f, k * HALF : (k + 1) * HALF]
    for copies in far + plain + later:
        for copy in copies:
            copy.wait_send()
    across.wait_send()


def params(number, mib):
    return pltpu.CompilerParams(
        collective_id=number, has_side_effects=True, vmem_limit_bytes=mib * 1024 * 1024
    )


def body(queries, key_cache, value_cache, out_weight):
    tokens, width = queries.shape
    cols = out_weight.shape[1]
    all_rows = tokens // 2 * lax.axis_size("ctx")
    vmem, anywhere = pl.BlockSpec(memory_space=pltpu.VMEM), pl.BlockSpec(memory_space=pl.ANY)
    bf16, f32 = jnp.bfloat16, jnp.float32
    attended = pl.pallas_call(
        attend_kernel,
        out_shape=jax.ShapeDtypeStruct((2, all_rows, width), bf16),
        in_specs=[anywhere] * 3,
        out_specs=anywhere,
        scratch_shapes=[
            pltpu.VMEM(queries.shape, bf16),
            pltpu.VMEM(key_cache.shape, bf16),
            pltpu.VMEM((4, ROWS, HD), bf16),
            pltpu.VMEM((16, 2 * KEYS, HD), bf16),
            pltpu.VMEM((ROWS, 2 * KEYS), f32),
            pltpu.VMEM((ROWS, 2 * KEYS), f32),
            pltpu.VMEM((ROWS, 2 * KEYS), bf16),
            pltpu.VMEM((ROWS, HD), f32),
            pltpu.VMEM((4, ROWS, 2 * HD), f32),
            pltpu.VMEM((4, ROWS, HD), f32),
            pltpu.VMEM((2, ROWS, HD), bf16),
            pltpu.VMEM((2, 8, ROWS), f32),
            pltpu.VMEM((2, ROWS, HD), bf16),
            pltpu.VMEM((2, 8, ROWS), f32),
            pltpu.VMEM((2, tokens // 2, width), bf16),
            pltpu.SemaphoreType.DMA((6,)),
            pltpu.SemaphoreType.DMA((S_COUNT,)),
            pltpu.SemaphoreType.DMA((S_COUNT,)),
        ],
        compiler_params=params(0, 58),
        cost_estimate=pl.CostEstimate(
            flops=8_600_000_000, bytes_accessed=5_000_000, transcendentals=17_000_000
        ),
    )(queries, key_cache, value_cache)
    terms = jnp.dot(
        attended.reshape(2 * all_rows, width), out_weight, preferred_element_type=f32
    ).astype(bf16)
    piece = pltpu.VMEM((2, 2, 2, tokens, cols // 2), bf16)
    return pl.pallas_call(
        reduce_kernel,
        out_shape=jax.ShapeDtypeStruct((2 * tokens, cols), bf16),
        in_specs=[vmem],
        out_specs=vmem,
        scratch_shapes=[
            piece,
            piece,
            piece,
            piece,
            pltpu.VMEM((2, tokens, cols), bf16),
            pltpu.VMEM((2, tokens, cols), bf16),
            pltpu.SemaphoreType.DMA((13,)),
            pltpu.SemaphoreType.DMA((13,)),
        ],
        compiler_params=params(1, 16),
    )(terms.reshape(2, all_rows, cols))


def solution(mesh):
    in_specs = (P("ctx", "head"), P("ctx", "head"), P("ctx", "head"), P("head", "ctx"))
    out_specs = P("head", "ctx")
    return jax.shard_map(body, mesh=mesh, in_specs=in_specs, out_specs=out_specs, check_vma=False)
```

```python
import math

import jax
import jax.numpy as jnp
from jax import lax
from jax.experimental import pallas as pl
from jax.experimental.pallas import tpu as pltpu
from jax.sharding import PartitionSpec as P

HD = 128
RUN = 64
NEG = -1e30
ROWS = 512
HALF = 32
KEYS = 512
LOG2E = math.log2(math.e)
MESH = pl.DeviceIdType.MESH

S_KV = 0
S_Q = 14
S_O = 16
S_STAT = 18
S_ATT = 20
S_FAR = 54
S_PLAIN = 58
S_LATER = 62
S_SIDE = 66
S_COUNT = 68


def device_at(x, y, core):
    return x * 8 + y * 2 + core


def kernel(
    q_hbm, k_hbm, v_hbm, w_hbm, out_ref,
    q_ref, k_ref, q_s, kv, keys, values, s0, s1, p1, fade1, acc, mrow, o_send, s_send, o_recv, s_recv,
    att, w, terms, far_in, plain_in, added, added_in, side, side_in, mine, fetched, send, recv,
):
    c, h = lax.axis_index("ctx"), lax.axis_index("head")
    x, y, core = c // 8, (c // 2) % 4, c % 2
    z, e = h // 2, h % 2
    scale = LOG2E / math.sqrt(HD)

    to_core = (device_at(x, y, 1 - core), h)
    to_up = (device_at(x, (y + 1) % 4, core), h)
    to_down = (device_at(x, (y + 3) % 4, core), h)
    to_x = (device_at(1 - x, y, core), h)
    z_ways = ((c, ((z + 1) % 4) * 2 + e), (c, ((z + 3) % 4) * 2 + e))
    to_side = (c, z * 2 + 1 - e)
    partners = (to_core, to_up, to_down, to_x, to_side) + z_ways

    def remote(src, dst, number, where):
        return pltpu.make_async_remote_copy(
            src_ref=src, dst_ref=dst, send_sem=send.at[number], recv_sem=recv.at[number],
            device_id=where, device_id_type=MESH,
        )

    q_fetch = pltpu.make_async_copy(q_hbm, q_ref, fetched.at[0])
    k_fetch = pltpu.make_async_copy(k_hbm, k_ref, fetched.at[1])
    v_fetch = [
        pltpu.make_async_copy(
            v_hbm.at[pl.ds(i * KEYS, KEYS)], kv.at[i, pl.ds(0, KEYS)], fetched.at[2 + i]
        )
        for i in range(2)
    ]
    w_copy = pltpu.make_async_copy(w_hbm, w, fetched.at[4])
    for fetch in [k_fetch, q_fetch] + v_fetch:
        fetch.start()
    barrier = pltpu.get_barrier_semaphore()
    for partner in partners:
        pl.semaphore_signal(barrier, inc=1, device_id=partner, device_id_type=MESH)

    k_fetch.wait()
    for half in range(2):
        for b in range(4):
            start = half * KEYS + b * HD
            piece = k_ref[start : start + HD].astype(jnp.float32)
            kv[half, KEYS + b * HD : KEYS + (b + 1) * HD] = piece.T.astype(jnp.bfloat16)
    q_fetch.wait()
    for r in range(2):
        for i in range(16):
            q_s[r, i * HALF : (i + 1) * HALF] = q_ref[
                r * HALF : (r + 1) * HALF, i * HD : (i + 1) * HD
            ]
    for fetch in v_fetch:
        fetch.wait()
    w_copy.start()
    pl.semaphore_wait(barrier, len(partners))

    def kv_copy(number, source, target, where):
        return remote(kv.at[source], kv.at[target], S_KV + number, where)

    own_up = [kv_copy(0 + i, i, 12 + i, to_up) for i in range(2)]
    own_down = [kv_copy(2 + i, i, 4 + i, to_down) for i in range(2)]
    own_core = [kv_copy(4 + i, i, 2 + i, to_core) for i in range(2)]
    pass_12 = kv_copy(6, 12, 14, to_core)
    pass_4 = kv_copy(7, 4, 6, to_core)
    pass_13 = kv_copy(8, 13, 15, to_core)
    pass_5 = kv_copy(9, 5, 7, to_core)
    on_up = kv_copy(10, 12, 8, to_up)
    on_down = kv_copy(11, 5, 9, to_down)
    pass_8 = kv_copy(12, 8, 10, to_core)
    pass_9 = kv_copy(13, 9, 11, to_core)
    q_copy = [remote(q_s.at[i], q_s.at[2 + i], S_Q + i, to_x) for i in range(2)]
    o_copy = [remote(o_send.at[f], o_recv.at[f], S_O + f, to_x) for f in range(2)]
    s_copy = [remote(s_send.at[f], s_recv.at[f], S_STAT + f, to_x) for f in range(2)]

    for i in range(2):
        own_core[i].start()
    q_copy[0].start()
    own_up[0].start()
    own_down[0].start()
    q_copy[1].start()
    for r in range(4):
        acc[r] = jnp.zeros((ROWS, 2 * HD), jnp.float32)
        mrow[r] = jnp.full((ROWS, HD), NEG, jnp.float32)

    def slots_of(pair):
        i = pair - 2
        middle = 12 + 2 * (i % 2) + i // 2
        one = jnp.where(pair < 2, 2 * pair, jnp.where(pair < 6, middle, 2 * pair - 4))
        two = jnp.where((pair >= 2) & (pair < 6), one - 8, one + 1)
        return one, two

    def stage(pair, where):
        for j, slot in enumerate(slots_of(pair)):
            for b in range(4):
                start = j * KEYS + b * HD
                keys[where, :, start : start + HD] = kv[slot, KEYS + b * HD : KEYS + (b + 1) * HD]
            values[where, j * KEYS : (j + 1) * KEYS, 0:HD] = kv[slot, 0:KEYS]

    def score(row, where, s_ref):
        s_ref[...] = (
            jnp.dot(q_s[row], keys[where], preferred_element_type=jnp.float32) * scale
        )

    def weigh(pair, row, s_ref):
        asker = device_at(1 - x if row >= 2 else x, y, core)
        token = lax.broadcasted_iota(jnp.int32, (ROWS, HD), 0) % HALF
        key_token = lax.broadcasted_iota(jnp.int32, (ROWS, HD), 1) - RUN
        pieces = []
        for j, slot in enumerate(slots_of(pair)):
            holder_core = jnp.where((slot // 2) % 2 == 1, 1 - core, core)
            holder = device_at(x, (y + slot // 4) % 4, holder_core)
            first = jnp.where(slot % 2 == 1, holder * RUN, -(1 << 20))
            limit = asker * RUN + (row % 2) * HALF - first
            end = (j + 1) * KEYS
            seen = (key_token < 0) | (key_token - token <= limit)
            pieces.append(s_ref[:, j * KEYS : end - HD])
            pieces.append(jnp.where(seen, s_ref[:, end - HD : end], NEG))
        scores = jnp.concatenate(pieces, axis=1)
        old = mrow[row]
        new = jnp.maximum(old, jnp.max(scores, axis=1, keepdims=True))
        weights = jnp.exp2(scores - jnp.concatenate([new] * (2 * KEYS // HD), axis=1))
        mrow[row] = new
        return weights.astype(jnp.bfloat16), jnp.exp2(old - new)

    def add_values(row, where, weights, fade):
        acc[row] = acc[row] * jnp.concatenate([fade, fade], axis=1) + jnp.dot(
            weights, values[where], preferred_element_type=jnp.float32
        )

    def normalised(row):
        total = acc[row, :, HD : 2 * HD]
        return acc[row, :, 0:HD] / total, mrow[row] + jnp.log(total) * LOG2E

    def finish_neighbour(f):
        value, level = normalised(2 + f)
        o_send[f] = value.astype(jnp.bfloat16)
        s_send[f] = level.T[0:8]
        o_copy[f].start()
        s_copy[f].start()

    def block_of(owner):
        start = owner * HALF
        return start if isinstance(start, int) else pl.multiple_of(start, HALF)

    def combine(f):
        value, level = normalised(f)
        o_copy[f].wait_recv()
        s_copy[f].wait_recv()
        other = jnp.broadcast_to(s_recv[f, 0:1], (HD, ROWS)).T
        top = jnp.maximum(level, other)
        part_a, part_b = jnp.exp2(level - top), jnp.exp2(other - top)
        done = (value * part_a + o_recv[f].astype(jnp.float32) * part_b) / (part_a + part_b)
        done = done.astype(jnp.bfloat16)
        for i in range(16):
            att[f, pl.ds(block_of(c), HALF), i * HD : (i + 1) * HD] = done[
                i * HALF : (i + 1) * HALF
            ]

    def gather_copy(f, number, dx, dy, where, part=None, from_core=None):
        owner = device_at(1 - x if dx else x, (y + dy) % 4, core if from_core is None else from_core)
        start, size = block_of(owner), HALF
        if part is not None:
            size = HALF // 2
            start = pl.multiple_of(start + part * size, size)
        block = att.at[f, pl.ds(start, size)]
        return remote(block, block, S_ATT + 17 * f + number, where)

    sent = own_up + own_down + own_core + [pass_12, pass_4, pass_13, pass_5, on_up, on_down]
    sent += [pass_8, pass_9] + q_copy + o_copy + s_copy

    def arrived(f, number, dx, dy, part=None, from_core=None):
        gather_copy(f, number, dx, dy, to_core, part, from_core).wait_recv()

    def gather_start(f, *args):
        gather_copy(f, *args).start()

    def gather_own(f):
        gather_start(f, 8, 0, 0, to_x)
        gather_start(f, 9, 0, 0, to_up)
        gather_start(f, 11, 0, 0, to_down)
        gather_start(f, 0, 0, 0, to_core)

    def gather_x(f):
        arrived(f, 8, 1, 0)
        gather_start(f, 10, 1, 0, to_up)
        gather_start(f, 12, 1, 0, to_down)
        gather_start(f, 4, 1, 0, to_core)

    def gather_y(f, plane):
        arrived(f, 9 + plane, plane, 3)
        gather_start(f, 13 + plane, plane, 3, to_up, 0)
        gather_start(f, 4 * plane + 3, plane, 3, to_core)
        arrived(f, 11 + plane, plane, 1)
        gather_start(f, 15 + plane, plane, 1, to_down, 1)
        gather_start(f, 4 * plane + 1, plane, 1, to_core)

    def gather_y2(f, plane):
        arrived(f, 13 + plane, plane, 2, 0)
        arrived(f, 15 + plane, plane, 2, 1)
        gather_start(f, 4 * plane + 2, plane, 2, to_core)

    def gather_end(f):
        for plane in range(2):
            for dy in range(4):
                arrived(f, 4 * plane + dy, plane, dy, None, 1 - core)

    def gather_sent(f):
        copies = [gather_copy(f, 8, 0, 0, to_x)]
        for plane in range(2):
            copies += [gather_copy(f, 4 * plane + dy, plane, dy, to_core) for dy in range(4)]
            copies += [gather_copy(f, 9 + plane, plane, 0, to_up)]
            copies += [gather_copy(f, 11 + plane, plane, 0, to_down)]
            copies += [gather_copy(f, 13 + plane, plane, 3, to_up, 0)]
            copies += [gather_copy(f, 15 + plane, plane, 1, to_down, 1)]
        return copies

    cols = w.shape[1] // 2
    rows = 4 * HALF

    def half(i):
        return pl.ds(i * cols, cols)

    def block(distance):
        return pl.ds(pl.multiple_of(((z + distance) % 4) * rows, rows), rows)

    far_copy = [
        [
            remote(terms.at[f, block(2), half(i)], far_in.at[f, i], S_FAR + 2 * f + i, z_ways[i])
            for i in range(2)
        ]
        for f in range(2)
    ]
    plain_copy = [
        [
            remote(
                terms.at[f, block(1 + 2 * i), half(1 - i)], plain_in.at[f, i],
                S_PLAIN + 2 * f + i, z_ways[i],
            )
            for i in range(2)
        ]
        for f in range(2)
    ]
    later_copy = [
        [
            remote(added.at[f, i], added_in.at[f, i], S_LATER + 2 * f + i, z_ways[i])
            for i in range(2)
        ]
        for f in range(2)
    ]
    side_copy = [remote(side.at[f], side_in.at[f], S_SIDE + f, to_side) for f in range(2)]

    def project(f):
        for i in range(2):
            terms[f, :, half(i)] = jnp.dot(
                att[f], w[:, half(i)], preferred_element_type=jnp.float32
            ).astype(jnp.bfloat16)
            far_copy[f][i].start()
        for i in range(2):
            plain_copy[f][i].start()

    def reduce_added(f):
        for i in range(2):
            far_copy[f][i].wait_recv()
            added[f, i] = (
                terms[f, block(1 + 2 * i), half(i)].astype(jnp.float32)
                + far_in[f, i].astype(jnp.float32)
            ).astype(jnp.bfloat16)
            later_copy[f][i].start()

    def reduce_last(f):
        for i in range(2):
            plain_copy[f][i].wait_recv()
        for i in range(2):
            later_copy[f][i].wait_recv()

        def summed(s, i):
            size = rows // 2
            part = pl.ds(pl.multiple_of(s * size, size), size)
            own = pl.ds(pl.multiple_of(z * rows + s * size, size), size)
            return (
                terms[f, own, half(i)].astype(jnp.float32)
                + added_in[f, i, part].astype(jnp.float32)
                + plain_in[f, 1 - i, part].astype(jnp.float32)
            )

        for i in range(2):
            side[f, :, half(i)] = summed(1 - e, i).astype(jnp.bfloat16)
        side_copy[f].start()
        for i in range(2):
            mine[f, :, half(i)] = summed(e, i)

    def reduce_end(f):
        side_copy[f].wait_recv()
        done = (mine[f] + side_in[f].astype(jnp.float32)).astype(jnp.bfloat16)
        for i in range(2):
            start = i * RUN + f * HALF
            out_ref[start : start + HALF] = done[i * HALF : (i + 1) * HALF]

    def wait_all(*copies):
        for copy in copies:
            copy.wait_recv()

    def pass_on(arrival, *onward):
        arrival.wait_recv()
        for copy in onward:
            copy.start()

    def start_rest():
        wait_all(*own_core)
        own_up[1].start()
        own_down[1].start()

    amid = [
        (0, start_rest),
        (1, lambda: pass_on(own_up[0], on_up, pass_12)),
        (1, lambda: pass_on(own_down[0], pass_4)),
        (2, lambda: wait_all(pass_12, pass_4)),
        (3, lambda: pass_on(own_down[1], on_down, pass_5)),
        (3, lambda: pass_on(own_up[1], pass_13)),
        (4, lambda: wait_all(pass_13, pass_5)),
        (5, lambda: pass_on(on_up, pass_8)),
        (5, lambda: pass_on(on_down, pass_9)),
        (6, lambda: wait_all(pass_8, pass_9)),
        (7, lambda: finish_neighbour(0)),
    ]

    def run(events, u):
        for k in sorted({step for step, _ in events}):

            @pl.when(u == k)
            def _():
                for step, action in events:
                    if step == k:
                        action()

    def two_pairs(step, carry):
        for now in range(2):
            pair, then = 2 * step + now, 1 - now
            score(3, now, s1)
            weights_a, fade_a = weigh(pair, 2, s0)
            add_values(1, then, p1[...], fade1[...])
            score(0, now, s0)
            weights_b, fade_b = weigh(pair, 3, s1)
            add_values(2, now, weights_a, fade_a)
            run([(k, action) for k, action in amid if k % 2 == now], pair)
            stage(jnp.minimum(pair + 1, 7), then)
            score(1, now, s1)
            weights_c, fade_c = weigh(pair, 0, s0)
            add_values(3, now, weights_b, fade_b)
            score(2, then, s0)
            weights_d, fade_d = weigh(pair, 1, s1)
            add_values(0, now, weights_c, fade_c)
            p1[...] = weights_d
            fade1[...] = fade_d
        return carry

    p1[...] = jnp.zeros_like(p1)
    fade1[...] = jnp.ones_like(fade1)
    for i in range(2):
        values[i, :, 0:HD] = jnp.zeros((2 * KEYS, HD), jnp.bfloat16)
        values[i, :, HD : 2 * HD] = jnp.ones((2 * KEYS, HD), jnp.bfloat16)
    stage(0, 0)
    wait_all(*q_copy)
    score(2, 0, s0)
    lax.fori_loop(0, 4, two_pairs, 0)
    finish_neighbour(1)
    add_values(1, 1, p1[...], fade1[...])
    combine(0)
    gather_own(0)
    combine(1)
    gather_x(0)
    gather_y(0, 0)
    gather_own(1)
    gather_y(0, 1)
    gather_x(1)
    gather_y2(0, 0)
    gather_y(1, 0)
    gather_y2(0, 1)
    w_copy.wait()
    gather_end(0)
    project(0)
    gather_y(1, 1)
    gather_y2(1, 0)
    reduce_added(0)
    gather_y2(1, 1)
    gather_end(1)
    project(1)
    reduce_last(0)
    reduce_added(1)
    reduce_end(0)
    reduce_last(1)
    reduce_end(1)

    sent += side_copy
    for f in range(2):
        sent += gather_sent(f) + far_copy[f] + plain_copy[f] + later_copy[f]
    for copy in sent:
        copy.wait_send()


def body(queries, key_cache, value_cache, out_weight):
    tokens, width = queries.shape
    cols = out_weight.shape[1]
    all_rows = tokens // 2 * lax.axis_size("ctx")
    vmem, anywhere = pl.BlockSpec(memory_space=pltpu.VMEM), pl.BlockSpec(memory_space=pl.ANY)
    bf16, f32 = jnp.bfloat16, jnp.float32
    piece = pltpu.VMEM((2, 2, 2 * tokens, cols // 2), bf16)
    return pl.pallas_call(
        kernel,
        out_shape=jax.ShapeDtypeStruct((2 * tokens, cols), bf16),
        in_specs=[anywhere] * 4,
        out_specs=vmem,
        scratch_shapes=[
            pltpu.VMEM(queries.shape, bf16),
            pltpu.VMEM(key_cache.shape, bf16),
            pltpu.VMEM((4, ROWS, HD), bf16),
            pltpu.VMEM((16, 2 * KEYS, HD), bf16),
            pltpu.VMEM((2, HD, 2 * KEYS), bf16),
            pltpu.VMEM((2, 2 * KEYS, 2 * HD), bf16),
            pltpu.VMEM((ROWS, 2 * KEYS), f32),
            pltpu.VMEM((ROWS, 2 * KEYS), f32),
            pltpu.VMEM((ROWS, 2 * KEYS), bf16),
            pltpu.VMEM((ROWS, HD), f32),
            pltpu.VMEM((4, ROWS, 2 * HD), f32),
            pltpu.VMEM((4, ROWS, HD), f32),
            pltpu.VMEM((2, ROWS, HD), bf16),
            pltpu.VMEM((2, 8, ROWS), f32),
            pltpu.VMEM((2, ROWS, HD), bf16),
            pltpu.VMEM((2, 8, ROWS), f32),
            pltpu.VMEM((2, all_rows, width), bf16),
            pltpu.VMEM(out_weight.shape, bf16),
            pltpu.VMEM((2, all_rows, cols), bf16),
            piece,
            piece,
            piece,
            piece,
            pltpu.VMEM((2, tokens, cols), bf16),
            pltpu.VMEM((2, tokens, cols), bf16),
            pltpu.VMEM((2, tokens, cols), f32),
            pltpu.SemaphoreType.DMA((5,)),
            pltpu.SemaphoreType.DMA((S_COUNT,)),
            pltpu.SemaphoreType.DMA((S_COUNT,)),
        ],
        compiler_params=pltpu.CompilerParams(
            collective_id=0, has_side_effects=True, vmem_limit_bytes=56 * 1024 * 1024
        ),
        cost_estimate=pl.CostEstimate(
            flops=13_000_000_000, bytes_accessed=5_000_000, transcendentals=17_000_000
        ),
    )(queries, key_cache, value_cache, out_weight)


def solution(mesh):
    in_specs = (P("ctx", "head"), P("ctx", "head"), P("ctx", "head"), P("head", "ctx"))
    out_specs = P("head", "ctx")
    return jax.shard_map(body, mesh=mesh, in_specs=in_specs, out_specs=out_specs, check_vma=False)
```

```python
import math

import jax
import jax.numpy as jnp
from jax import lax
from jax.experimental import pallas as pl
from jax.experimental.pallas import tpu as pltpu
from jax.sharding import PartitionSpec as P

HD = 128
RUN = 64
NEG = -1e30
ROWS = 512
HALF = 32
KEYS = 512
LOG2E = math.log2(math.e)
MESH = pl.DeviceIdType.MESH

S_KV = 0
S_Q = 14
S_O = 16
S_STAT = 18
S_ATT = 20
S_FAR = 54
S_PLAIN = 62
S_LATER = 70
S_SIDE = 78
S_COUNT = 80


def device_at(x, y, core):
    return x * 8 + y * 2 + core


def kernel(
    q_hbm, k_hbm, v_hbm, w_hbm, out_ref,
    q_ref, k_ref, q_s, kv, s0, s1, p1, fade1, acc, mrow, o_send, s_send, o_recv, s_recv,
    att, w, terms, far_in, plain_in, added, added_in, side, side_in, fetched, send, recv,
):
    c, h = lax.axis_index("ctx"), lax.axis_index("head")
    x, y, core = c // 8, (c // 2) % 4, c % 2
    z, e = h // 2, h % 2
    scale = LOG2E / math.sqrt(HD)

    to_core = (device_at(x, y, 1 - core), h)
    to_up = (device_at(x, (y + 1) % 4, core), h)
    to_down = (device_at(x, (y + 3) % 4, core), h)
    to_x = (device_at(1 - x, y, core), h)
    z_ways = ((c, ((z + 1) % 4) * 2 + e), (c, ((z + 3) % 4) * 2 + e))
    to_side = (c, z * 2 + 1 - e)
    partners = (to_core, to_up, to_down, to_x, to_side) + z_ways

    def remote(src, dst, number, where):
        return pltpu.make_async_remote_copy(
            src_ref=src, dst_ref=dst, send_sem=send.at[number], recv_sem=recv.at[number],
            device_id=where, device_id_type=MESH,
        )

    q_fetch = pltpu.make_async_copy(q_hbm, q_ref, fetched.at[0])
    k_fetch = pltpu.make_async_copy(k_hbm, k_ref, fetched.at[1])
    v_fetch = [
        pltpu.make_async_copy(
            v_hbm.at[pl.ds(i * KEYS, KEYS)], kv.at[i, pl.ds(0, KEYS)], fetched.at[2 + i]
        )
        for i in range(2)
    ]
    w_copy = pltpu.make_async_copy(w_hbm, w, fetched.at[4])
    for fetch in [k_fetch, q_fetch] + v_fetch:
        fetch.start()
    barrier = pltpu.get_barrier_semaphore()
    for partner in partners:
        pl.semaphore_signal(barrier, inc=1, device_id=partner, device_id_type=MESH)

    k_fetch.wait()
    for half in range(2):
        for b in range(4):
            start = half * KEYS + b * HD
            piece = k_ref[start : start + HD].astype(jnp.float32)
            kv[half, KEYS + b * HD : KEYS + (b + 1) * HD] = piece.T.astype(jnp.bfloat16)
    q_fetch.wait()
    for r in range(2):
        for i in range(16):
            q_s[r, i * HALF : (i + 1) * HALF] = q_ref[
                r * HALF : (r + 1) * HALF, i * HD : (i + 1) * HD
            ]
    for fetch in v_fetch:
        fetch.wait()
    w_copy.start()
    pl.semaphore_wait(barrier, len(partners))

    def kv_copy(number, source, target, where):
        return remote(kv.at[source], kv.at[target], S_KV + number, where)

    own_up = [kv_copy(0 + i, i, 12 + i, to_up) for i in range(2)]
    own_down = [kv_copy(2 + i, i, 4 + i, to_down) for i in range(2)]
    own_core = [kv_copy(4 + i, i, 2 + i, to_core) for i in range(2)]
    pass_12 = kv_copy(6, 12, 14, to_core)
    pass_4 = kv_copy(7, 4, 6, to_core)
    pass_13 = kv_copy(8, 13, 15, to_core)
    pass_5 = kv_copy(9, 5, 7, to_core)
    on_up = kv_copy(10, 12, 8, to_up)
    on_down = kv_copy(11, 5, 9, to_down)
    pass_8 = kv_copy(12, 8, 10, to_core)
    pass_9 = kv_copy(13, 9, 11, to_core)
    q_copy = [remote(q_s.at[i], q_s.at[2 + i], S_Q + i, to_x) for i in range(2)]
    o_copy = [remote(o_send.at[f], o_recv.at[f], S_O + f, to_x) for f in range(2)]
    s_copy = [remote(s_send.at[f], s_recv.at[f], S_STAT + f, to_x) for f in range(2)]

    for i in range(2):
        own_core[i].start()
    q_copy[0].start()
    own_up[0].start()
    own_down[0].start()
    q_copy[1].start()
    for r in range(4):
        acc[r] = jnp.zeros((ROWS, 2 * HD), jnp.float32)
        mrow[r] = jnp.full((ROWS, HD), NEG, jnp.float32)

    def place(t):
        q = (t - 8) % 12
        early = jnp.where(q < 8, 2 + q // 2, 6 + q % 2)
        early_row = jnp.where(q < 8, q % 2, 1 - (q - 8) // 2) * 2
        pair = jnp.where(t < 8, t // 2 % 2, jnp.where(t < 20, early, 2 + q % 6))
        row = jnp.where(t < 8, t // 4 * 2 + t % 2, early_row)
        row = jnp.where(t < 20, row, (1 - q // 6) * 2 + 1)
        i = pair - 2
        middle = 12 + 2 * (i % 2) + i // 2
        one = jnp.where(pair < 2, 2 * pair, jnp.where(pair < 6, middle, 2 * pair - 4))
        two = jnp.where((pair >= 2) & (pair < 6), one - 8, one + 1)
        return one, two, row

    def score(t, s_ref):
        one, two, row = place(t)
        queries = q_s[row]
        for j, slot in enumerate((one, two)):
            keys = jnp.concatenate(
                [kv[slot, KEYS + b * HD : KEYS + (b + 1) * HD] for b in range(4)], axis=1
            )
            s_ref[:, j * KEYS : (j + 1) * KEYS] = (
                jnp.dot(queries, keys, preferred_element_type=jnp.float32) * scale
            )

    def weigh(t, s_ref):
        one, two, row = place(t)
        asker = device_at(jnp.where(row >= 2, 1 - x, x), y, core)
        token = lax.broadcasted_iota(jnp.int32, (ROWS, HD), 0) % HALF
        key_token = lax.broadcasted_iota(jnp.int32, (ROWS, HD), 1) - RUN
        pieces = []
        for j, slot in enumerate((one, two)):
            holder_core = jnp.where((slot // 2) % 2 == 1, 1 - core, core)
            holder = device_at(x, (y + slot // 4) % 4, holder_core)
            first = jnp.where(slot % 2 == 1, holder * RUN, -(1 << 20))
            limit = asker * RUN + (row % 2) * HALF - first
            end = (j + 1) * KEYS
            seen = (key_token < 0) | (key_token - token <= limit)
            pieces.append(s_ref[:, j * KEYS : end - HD])
            pieces.append(jnp.where(seen, s_ref[:, end - HD : end], NEG))
        scores = jnp.concatenate(pieces, axis=1)
        old = mrow[row]
        new = jnp.maximum(old, jnp.max(scores, axis=1, keepdims=True))
        weights = jnp.exp2(scores - jnp.concatenate([new] * (2 * KEYS // HD), axis=1))
        mrow[row] = new
        return weights.astype(jnp.bfloat16), jnp.exp2(old - new)

    def add_values(t, weights, fade):
        one, two, row = place(t)
        ones = jnp.ones((KEYS, HD), jnp.bfloat16)
        values = jnp.concatenate(
            [jnp.concatenate([kv[slot, 0:KEYS], ones], axis=1) for slot in (one, two)], axis=0
        )
        acc[row] = acc[row] * jnp.concatenate([fade, fade], axis=1) + jnp.dot(
            weights, values, preferred_element_type=jnp.float32
        )

    def normalised(row):
        total = acc[row, :, HD : 2 * HD]
        return acc[row, :, 0:HD] / total, mrow[row] + jnp.log(total) * LOG2E

    def finish_neighbour(f):
        value, level = normalised(2 + f)
        o_send[f] = value.astype(jnp.bfloat16)
        s_send[f] = level.T[0:8]
        o_copy[f].start()
        s_copy[f].start()

    def block_of(owner):
        start = owner * HALF
        return start if isinstance(start, int) else pl.multiple_of(start, HALF)

    def combine(f):
        value, level = normalised(f)
        o_copy[f].wait_recv()
        s_copy[f].wait_recv()
        other = jnp.broadcast_to(s_recv[f, 0:1], (HD, ROWS)).T
        top = jnp.maximum(level, other)
        part_a, part_b = jnp.exp2(level - top), jnp.exp2(other - top)
        done = (value * part_a + o_recv[f].astype(jnp.float32) * part_b) / (part_a + part_b)
        done = done.astype(jnp.bfloat16)
        for i in range(16):
            att[f, pl.ds(block_of(c), HALF), i * HD : (i + 1) * HD] = done[
                i * HALF : (i + 1) * HALF
            ]

    def gather_copy(f, number, dx, dy, where, part=None, from_core=None):
        owner = device_at(1 - x if dx else x, (y + dy) % 4, core if from_core is None else from_core)
        start, size = block_of(owner), HALF
        if part is not None:
            size = HALF // 2
            start = pl.multiple_of(start + part * size, size)
        block = att.at[f, pl.ds(start, size)]
        return remote(block, block, S_ATT + 17 * f + number, where)

    sent = own_up + own_down + own_core + [pass_12, pass_4, pass_13, pass_5, on_up, on_down]
    sent += [pass_8, pass_9] + q_copy + o_copy + s_copy

    def arrived(f, number, dx, dy, part=None, from_core=None):
        gather_copy(f, number, dx, dy, to_core, part, from_core).wait_recv()

    def gather_start(f, *args):
        gather_copy(f, *args).start()

    def gather_own(f):
        gather_start(f, 8, 0, 0, to_x)
        gather_start(f, 9, 0, 0, to_up)
        gather_start(f, 11, 0, 0, to_down)
        gather_start(f, 0, 0, 0, to_core)

    def gather_x(f):
        arrived(f, 8, 1, 0)
        gather_start(f, 10, 1, 0, to_up)
        gather_start(f, 12, 1, 0, to_down)
        gather_start(f, 4, 1, 0, to_core)

    def gather_y(f, plane):
        arrived(f, 9 + plane, plane, 3)
        gather_start(f, 13 + plane, plane, 3, to_up, 0)
        gather_start(f, 4 * plane + 3, plane, 3, to_core)
        arrived(f, 11 + plane, plane, 1)
        gather_start(f, 15 + plane, plane, 1, to_down, 1)
        gather_start(f, 4 * plane + 1, plane, 1, to_core)

    def gather_y2(f, plane):
        arrived(f, 13 + plane, plane, 2, 0)
        arrived(f, 15 + plane, plane, 2, 1)
        gather_start(f, 4 * plane + 2, plane, 2, to_core)

    def gather_end(f):
        for plane in range(2):
            for dy in range(4):
                arrived(f, 4 * plane + dy, plane, dy, None, 1 - core)

    def gather_sent(f):
        copies = [gather_copy(f, 8, 0, 0, to_x)]
        for plane in range(2):
            copies += [gather_copy(f, 4 * plane + dy, plane, dy, to_core) for dy in range(4)]
            copies += [gather_copy(f, 9 + plane, plane, 0, to_up)]
            copies += [gather_copy(f, 11 + plane, plane, 0, to_down)]
            copies += [gather_copy(f, 13 + plane, plane, 3, to_up, 0)]
            copies += [gather_copy(f, 15 + plane, plane, 1, to_down, 1)]
        return copies

    cols = w.shape[1] // 2
    span = 2 * HALF

    def half(i):
        return pl.ds(i * cols, cols)

    def block(distance, g):
        side_of = e if g == 1 else 1 - e
        start = (((z + distance) % 4) * 2 + side_of) * span
        return pl.ds(pl.multiple_of(start, span), span)

    def z_copies(number, source_of, target):
        return [
            [
                [
                    remote(
                        source_of(f, g, i), target.at[f, g, i], number + 4 * f + 2 * g + i,
                        z_ways[i],
                    )
                    for i in range(2)
                ]
                for g in range(2)
            ]
            for f in range(2)
        ]

    far_copy = z_copies(S_FAR, lambda f, g, i: terms.at[f, block(2, g), half(i)], far_in)
    plain_copy = z_copies(
        S_PLAIN, lambda f, g, i: terms.at[f, block(1 + 2 * i, g), half(1 - i)], plain_in
    )
    later_copy = z_copies(S_LATER, lambda f, g, i: added.at[f, g, i], added_in)
    side_copy = [remote(side.at[f], side_in.at[f], S_SIDE + f, to_side) for f in range(2)]

    def project(f, i):
        terms[f, :, half(i)] = jnp.dot(
            att[f], w[:, half(i)], preferred_element_type=jnp.float32
        ).astype(jnp.bfloat16)
        for g in range(2):
            far_copy[f][g][i].start()
        if i == 1:
            for j in range(2):
                plain_copy[f][0][j].start()

    def add_on(f, g):
        for i in range(2):
            far_copy[f][g][i].wait_recv()
            added[f, g, i] = (
                terms[f, block(1 + 2 * i, g), half(i)].astype(jnp.float32)
                + far_in[f, g, i].astype(jnp.float32)
            ).astype(jnp.bfloat16)
            later_copy[f][g][i].start()

    def reduce_added(f):
        add_on(f, 0)
        for i in range(2):
            plain_copy[f][1][i].start()
        add_on(f, 1)

    def summed(f, g, i):
        return (
            terms[f, block(0, g), half(i)].astype(jnp.float32)
            + added_in[f, g, i].astype(jnp.float32)
            + plain_in[f, g, 1 - i].astype(jnp.float32)
        )

    def wait_sums(f, g):
        for i in range(2):
            plain_copy[f][g][i].wait_recv()
            later_copy[f][g][i].wait_recv()

    def reduce_last(f):
        wait_sums(f, 0)
        for i in range(2):
            side[f, :, half(i)] = summed(f, 0, i).astype(jnp.bfloat16)
        side_copy[f].start()

    def reduce_end(f):
        wait_sums(f, 1)
        side_copy[f].wait_recv()
        for i in range(2):
            done = (summed(f, 1, i) + side_in[f, :, half(i)].astype(jnp.float32)).astype(
                jnp.bfloat16
            )
            for k in range(2):
                start = k * RUN + f * HALF
                out_ref[start : start + HALF, half(i)] = done[k * HALF : (k + 1) * HALF]

    def wait_all(*copies):
        for copy in copies:
            copy.wait_recv()

    def pass_on(arrival, *onward):
        arrival.wait_recv()
        for copy in onward:
            copy.start()

    def start_rest():
        wait_all(*own_core)
        own_up[1].start()
        own_down[1].start()

    before = [
        (0, start_rest),
        (1, lambda: wait_all(q_copy[0])),
        (2, lambda: wait_all(q_copy[1])),
        (3, lambda: pass_on(own_up[0], on_up, pass_12)),
        (3, lambda: pass_on(own_down[0], pass_4)),
        (4, lambda: wait_all(pass_12, pass_4)),
        (5, lambda: pass_on(own_down[1], on_down, pass_5)),
        (5, lambda: pass_on(own_up[1], pass_13)),
        (6, lambda: wait_all(pass_13, pass_5)),
        (7, lambda: pass_on(on_up, pass_8)),
        (7, lambda: pass_on(on_down, pass_9)),
        (8, lambda: wait_all(pass_8, pass_9)),
    ]
    after = [
        (9, lambda: finish_neighbour(0)),
        (11, lambda: combine(0)),
        (11, lambda: gather_own(0)),
        (12, lambda: gather_x(0)),
        (13, lambda: finish_neighbour(1)),
        (13, lambda: gather_y(0, 0)),
        (14, lambda: gather_y(0, 1)),
        (15, lambda: gather_y2(0, 0)),
    ]

    def run(events, u):
        for k in sorted({step for step, _ in events}):

            @pl.when(u == k)
            def _():
                for step, action in events:
                    if step == k:
                        action()

    def unit(u, carry):
        run(before, u)
        t = 2 * u
        score(t + 1, s1)
        weights, fade = weigh(t, s0)
        add_values(jnp.maximum(t - 1, 0), p1[...], fade1[...])
        score(jnp.minimum(t + 2, 31), s0)
        weights_1, fade_1 = weigh(t + 1, s1)
        add_values(t, weights, fade)
        p1[...] = weights_1
        fade1[...] = fade_1
        run(after, u)
        return carry

    p1[...] = jnp.zeros_like(p1)
    fade1[...] = jnp.ones_like(fade1)
    score(0, s0)
    lax.fori_loop(0, 16, unit, 0)
    add_values(31, p1[...], fade1[...])
    combine(1)
    gather_own(1)
    gather_y2(0, 1)
    w_copy.wait()
    gather_end(0)
    project(0, 0)
    gather_x(1)
    gather_y(1, 0)
    project(0, 1)
    gather_y(1, 1)
    gather_y2(1, 0)
    reduce_added(0)
    gather_y2(1, 1)
    gather_end(1)
    project(1, 0)
    project(1, 1)
    reduce_last(0)
    reduce_added(1)
    reduce_end(0)
    reduce_last(1)
    reduce_end(1)

    sent += side_copy
    for f in range(2):
        sent += gather_sent(f)
        for copies in far_copy[f] + plain_copy[f] + later_copy[f]:
            sent += copies
    for copy in sent:
        copy.wait_send()


def body(queries, key_cache, value_cache, out_weight):
    tokens, width = queries.shape
    cols = out_weight.shape[1]
    all_rows = tokens // 2 * lax.axis_size("ctx")
    vmem, anywhere = pl.BlockSpec(memory_space=pltpu.VMEM), pl.BlockSpec(memory_space=pl.ANY)
    bf16, f32 = jnp.bfloat16, jnp.float32
    piece = pltpu.VMEM((2, 2, 2, tokens, cols // 2), bf16)
    return pl.pallas_call(
        kernel,
        out_shape=jax.ShapeDtypeStruct((2 * tokens, cols), bf16),
        in_specs=[anywhere] * 4,
        out_specs=vmem,
        scratch_shapes=[
            pltpu.VMEM(queries.shape, bf16),
            pltpu.VMEM(key_cache.shape, bf16),
            pltpu.VMEM((4, ROWS, HD), bf16),
            pltpu.VMEM((16, 2 * KEYS, HD), bf16),
            pltpu.VMEM((ROWS, 2 * KEYS), f32),
            pltpu.VMEM((ROWS, 2 * KEYS), f32),
            pltpu.VMEM((ROWS, 2 * KEYS), bf16),
            pltpu.VMEM((ROWS, HD), f32),
            pltpu.VMEM((4, ROWS, 2 * HD), f32),
            pltpu.VMEM((4, ROWS, HD), f32),
            pltpu.VMEM((2, ROWS, HD), bf16),
            pltpu.VMEM((2, 8, ROWS), f32),
            pltpu.VMEM((2, ROWS, HD), bf16),
            pltpu.VMEM((2, 8, ROWS), f32),
            pltpu.VMEM((2, all_rows, width), bf16),
            pltpu.VMEM(out_weight.shape, bf16),
            pltpu.VMEM((2, all_rows, cols), bf16),
            piece,
            piece,
            piece,
            piece,
            pltpu.VMEM((2, tokens, cols), bf16),
            pltpu.VMEM((2, tokens, cols), bf16),
            pltpu.SemaphoreType.DMA((5,)),
            pltpu.SemaphoreType.DMA((S_COUNT,)),
            pltpu.SemaphoreType.DMA((S_COUNT,)),
        ],
        compiler_params=pltpu.CompilerParams(
            collective_id=0, has_side_effects=True, vmem_limit_bytes=56 * 1024 * 1024
        ),
        cost_estimate=pl.CostEstimate(
            flops=13_000_000_000, bytes_accessed=5_000_000, transcendentals=17_000_000
        ),
    )(queries, key_cache, value_cache, out_weight)


def solution(mesh):
    in_specs = (P("ctx", "head"), P("ctx", "head"), P("ctx", "head"), P("head", "ctx"))
    out_specs = P("head", "ctx")
    return jax.shard_map(body, mesh=mesh, in_specs=in_specs, out_specs=out_specs, check_vma=False)
```

```python
import math

import jax
import jax.numpy as jnp
from jax import lax
from jax.experimental import pallas as pl
from jax.experimental.pallas import tpu as pltpu
from jax.sharding import PartitionSpec as P

HD = 128
RUN = 64
NEG = -1e30
ROWS = 512
HALF = 32
KEYS = 512

MESH = pl.DeviceIdType.MESH

S_KV = 0
S_Q = 14
S_O = 16
S_STAT = 18
S_ATT = 20
S_FAR = 54
S_PLAIN = 62
S_LATER = 70
S_SIDE = 78
S_COUNT = 80


def device_at(x, y, core):
    return x * 8 + y * 2 + core


def kernel(
    q_hbm, k_hbm, v_hbm, w_hbm, out_ref,
    q_ref, k_ref, q_s, kv, s0, s1, p1, fade1, acc, mrow, o_send, s_send, o_recv, s_recv,
    att, w, terms, far_in, plain_in, added, added_in, side, side_in, fetched, send, recv,
):
    c, h = lax.axis_index("ctx"), lax.axis_index("head")
    x, y, core = c // 8, (c // 2) % 4, c % 2
    z, e = h // 2, h % 2
    scale = 1.0 / math.sqrt(HD)

    to_core = (device_at(x, y, 1 - core), h)
    to_up = (device_at(x, (y + 1) % 4, core), h)
    to_down = (device_at(x, (y + 3) % 4, core), h)
    to_x = (device_at(1 - x, y, core), h)
    z_ways = ((c, ((z + 1) % 4) * 2 + e), (c, ((z + 3) % 4) * 2 + e))
    to_side = (c, z * 2 + 1 - e)
    partners = (to_core, to_up, to_down, to_x, to_side) + z_ways

    def remote(src, dst, number, where):
        return pltpu.make_async_remote_copy(
            src_ref=src, dst_ref=dst, send_sem=send.at[number], recv_sem=recv.at[number],
            device_id=where, device_id_type=MESH,
        )

    q_fetch = pltpu.make_async_copy(q_hbm, q_ref, fetched.at[0])
    k_fetch = pltpu.make_async_copy(k_hbm, k_ref, fetched.at[1])
    v_fetch = [
        pltpu.make_async_copy(
            v_hbm.at[pl.ds(i * KEYS, KEYS)], kv.at[i, pl.ds(0, KEYS)], fetched.at[2 + i]
        )
        for i in range(2)
    ]
    w_copy = pltpu.make_async_copy(w_hbm, w, fetched.at[4])
    for fetch in [k_fetch, q_fetch] + v_fetch:
        fetch.start()
    barrier = pltpu.get_barrier_semaphore()
    for partner in partners:
        pl.semaphore_signal(barrier, inc=1, device_id=partner, device_id_type=MESH)

    k_fetch.wait()
    for half in range(2):
        for b in range(4):
            start = half * KEYS + b * HD
            piece = k_ref[start : start + HD].astype(jnp.float32)
            kv[half, KEYS + b * HD : KEYS + (b + 1) * HD] = piece.T.astype(jnp.bfloat16)
    q_fetch.wait()
    for r in range(2):
        for i in range(16):
            q_s[r, i * HALF : (i + 1) * HALF] = q_ref[
                r * HALF : (r + 1) * HALF, i * HD : (i + 1) * HD
            ]
    for fetch in v_fetch:
        fetch.wait()
    w_copy.start()
    pl.semaphore_wait(barrier, len(partners))

    def kv_copy(number, source, target, where):
        return remote(kv.at[source], kv.at[target], S_KV + number, where)

    own_up = [kv_copy(0 + i, i, 12 + i, to_up) for i in range(2)]
    own_down = [kv_copy(2 + i, i, 4 + i, to_down) for i in range(2)]
    own_core = [kv_copy(4 + i, i, 2 + i, to_core) for i in range(2)]
    pass_12 = kv_copy(6, 12, 14, to_core)
    pass_4 = kv_copy(7, 4, 6, to_core)
    pass_13 = kv_copy(8, 13, 15, to_core)
    pass_5 = kv_copy(9, 5, 7, to_core)
    on_up = kv_copy(10, 12, 8, to_up)
    on_down = kv_copy(11, 5, 9, to_down)
    pass_8 = kv_copy(12, 8, 10, to_core)
    pass_9 = kv_copy(13, 9, 11, to_core)
    q_copy = [remote(q_s.at[i], q_s.at[2 + i], S_Q + i, to_x) for i in range(2)]
    o_copy = [remote(o_send.at[f], o_recv.at[f], S_O + f, to_x) for f in range(2)]
    s_copy = [remote(s_send.at[f], s_recv.at[f], S_STAT + f, to_x) for f in range(2)]

    for i in range(2):
        own_core[i].start()
    q_copy[0].start()
    own_up[0].start()
    own_down[0].start()
    q_copy[1].start()
    for r in range(4):
        acc[r] = jnp.zeros((ROWS, 2 * HD), jnp.float32)
        mrow[r] = jnp.full((ROWS, HD), NEG, jnp.float32)

    def place(t):
        q = (t - 8) % 12
        early = jnp.where(q < 8, 2 + q // 2, 6 + q % 2)
        early_row = jnp.where(q < 8, q % 2, 1 - (q - 8) // 2) * 2
        pair = jnp.where(t < 8, t // 2 % 2, jnp.where(t < 20, early, 2 + q % 6))
        row = jnp.where(t < 8, t // 4 * 2 + t % 2, early_row)
        row = jnp.where(t < 20, row, (1 - q // 6) * 2 + 1)
        i = pair - 2
        middle = 12 + 2 * (i % 2) + i // 2
        one = jnp.where(pair < 2, 2 * pair, jnp.where(pair < 6, middle, 2 * pair - 4))
        two = jnp.where((pair >= 2) & (pair < 6), one - 8, one + 1)
        return one, two, row

    def score(t, s_ref):
        one, two, row = place(t)
        queries = q_s[row]
        for j, slot in enumerate((one, two)):
            keys = jnp.concatenate(
                [kv[slot, KEYS + b * HD : KEYS + (b + 1) * HD] for b in range(4)], axis=1
            )
            s_ref[:, j * KEYS : (j + 1) * KEYS] = (
                jnp.dot(queries, keys, preferred_element_type=jnp.float32) * scale
            )

    def weigh(t, s_ref):
        one, two, row = place(t)
        asker = device_at(jnp.where(row >= 2, 1 - x, x), y, core)
        token = lax.broadcasted_iota(jnp.int32, (ROWS, HD), 0) % HALF
        key_token = lax.broadcasted_iota(jnp.int32, (ROWS, HD), 1) - RUN
        pieces = []
        for j, slot in enumerate((one, two)):
            holder_core = jnp.where((slot // 2) % 2 == 1, 1 - core, core)
            holder = device_at(x, (y + slot // 4) % 4, holder_core)
            first = jnp.where(slot % 2 == 1, holder * RUN, -(1 << 20))
            limit = asker * RUN + (row % 2) * HALF - first
            end = (j + 1) * KEYS
            seen = (key_token < 0) | (key_token - token <= limit)
            pieces.append(s_ref[:, j * KEYS : end - HD])
            pieces.append(jnp.where(seen, s_ref[:, end - HD : end], NEG))
        scores = jnp.concatenate(pieces, axis=1)
        old = mrow[row]
        new = jnp.maximum(old, jnp.max(scores, axis=1, keepdims=True))
        weights = jnp.exp(scores - jnp.concatenate([new] * (2 * KEYS // HD), axis=1))
        mrow[row] = new
        return weights.astype(jnp.bfloat16), jnp.exp(old - new)

    def add_values(t, weights, fade):
        one, two, row = place(t)
        ones = jnp.ones((KEYS, HD), jnp.bfloat16)
        values = jnp.concatenate(
            [jnp.concatenate([kv[slot, 0:KEYS], ones], axis=1) for slot in (one, two)], axis=0
        )
        acc[row] = acc[row] * jnp.concatenate([fade, fade], axis=1) + jnp.dot(
            weights, values, preferred_element_type=jnp.float32
        )

    def normalised(row):
        total = acc[row, :, HD : 2 * HD]
        return acc[row, :, 0:HD] / total, mrow[row] + jnp.log(total)

    def finish_neighbour(f):
        value, level = normalised(2 + f)
        o_send[f] = value.astype(jnp.bfloat16)
        s_send[f] = level.T[0:8]
        o_copy[f].start()
        s_copy[f].start()

    def block_of(owner):
        start = owner * HALF
        return start if isinstance(start, int) else pl.multiple_of(start, HALF)

    def combine(f):
        value, level = normalised(f)
        o_copy[f].wait_recv()
        s_copy[f].wait_recv()
        other = jnp.broadcast_to(s_recv[f, 0:1], (HD, ROWS)).T
        top = jnp.maximum(level, other)
        part_a, part_b = jnp.exp(level - top), jnp.exp(other - top)
        done = (value * part_a + o_recv[f].astype(jnp.float32) * part_b) / (part_a + part_b)
        done = done.astype(jnp.bfloat16)
        for i in range(16):
            att[f, pl.ds(block_of(c), HALF), i * HD : (i + 1) * HD] = done[
                i * HALF : (i + 1) * HALF
            ]

    def gather_copy(f, number, dx, dy, where, part=None, from_core=None):
        owner = device_at(1 - x if dx else x, (y + dy) % 4, core if from_core is None else from_core)
        start, size = block_of(owner), HALF
        if part is not None:
            size = HALF // 2
            start = pl.multiple_of(start + part * size, size)
        block = att.at[f, pl.ds(start, size)]
        return remote(block, block, S_ATT + 17 * f + number, where)

    sent = own_up + own_down + own_core + [pass_12, pass_4, pass_13, pass_5, on_up, on_down]
    sent += [pass_8, pass_9] + q_copy + o_copy + s_copy

    def arrived(f, number, dx, dy, part=None, from_core=None):
        gather_copy(f, number, dx, dy, to_core, part, from_core).wait_recv()

    def gather_start(f, *args):
        gather_copy(f, *args).start()

    def gather_own(f):
        gather_start(f, 8, 0, 0, to_x)
        gather_start(f, 9, 0, 0, to_up)
        gather_start(f, 11, 0, 0, to_down)
        gather_start(f, 0, 0, 0, to_core)

    def gather_x(f):
        arrived(f, 8, 1, 0)
        gather_start(f, 10, 1, 0, to_up)
        gather_start(f, 12, 1, 0, to_down)
        gather_start(f, 4, 1, 0, to_core)

    def gather_y(f, plane):
        arrived(f, 9 + plane, plane, 3)
        gather_start(f, 13 + plane, plane, 3, to_up, 0)
        gather_start(f, 4 * plane + 3, plane, 3, to_core)
        arrived(f, 11 + plane, plane, 1)
        gather_start(f, 15 + plane, plane, 1, to_down, 1)
        gather_start(f, 4 * plane + 1, plane, 1, to_core)

    def gather_y2(f, plane):
        arrived(f, 13 + plane, plane, 2, 0)
        arrived(f, 15 + plane, plane, 2, 1)
        gather_start(f, 4 * plane + 2, plane, 2, to_core)

    def gather_end(f):
        for plane in range(2):
            for dy in range(4):
                arrived(f, 4 * plane + dy, plane, dy, None, 1 - core)

    def gather_sent(f):
        copies = [gather_copy(f, 8, 0, 0, to_x)]
        for plane in range(2):
            copies += [gather_copy(f, 4 * plane + dy, plane, dy, to_core) for dy in range(4)]
            copies += [gather_copy(f, 9 + plane, plane, 0, to_up)]
            copies += [gather_copy(f, 11 + plane, plane, 0, to_down)]
            copies += [gather_copy(f, 13 + plane, plane, 3, to_up, 0)]
            copies += [gather_copy(f, 15 + plane, plane, 1, to_down, 1)]
        return copies

    cols = w.shape[1] // 2
    span = 2 * HALF

    def half(i):
        return pl.ds(i * cols, cols)

    def block(distance, g):
        side_of = e if g == 1 else 1 - e
        start = (((z + distance) % 4) * 2 + side_of) * span
        return pl.ds(pl.multiple_of(start, span), span)

    def z_copies(number, source_of, target):
        return [
            [
                [
                    remote(
                        source_of(f, g, i), target.at[f, g, i], number + 4 * f + 2 * g + i,
                        z_ways[i],
                    )
                    for i in range(2)
                ]
                for g in range(2)
            ]
            for f in range(2)
        ]

    far_copy = z_copies(S_FAR, lambda f, g, i: terms.at[f, block(2, g), half(i)], far_in)
    plain_copy = z_copies(
        S_PLAIN, lambda f, g, i: terms.at[f, block(1 + 2 * i, g), half(1 - i)], plain_in
    )
    later_copy = z_copies(S_LATER, lambda f, g, i: added.at[f, g, i], added_in)
    side_copy = [remote(side.at[f], side_in.at[f], S_SIDE + f, to_side) for f in range(2)]

    def project(f, i):
        terms[f, :, half(i)] = jnp.dot(
            att[f], w[:, half(i)], preferred_element_type=jnp.float32
        ).astype(jnp.bfloat16)
        for g in range(2):
            far_copy[f][g][i].start()
        if i == 1:
            for j in range(2):
                plain_copy[f][0][j].start()

    def add_on(f, g):
        for i in range(2):
            far_copy[f][g][i].wait_recv()
            added[f, g, i] = (
                terms[f, block(1 + 2 * i, g), half(i)].astype(jnp.float32)
                + far_in[f, g, i].astype(jnp.float32)
            ).astype(jnp.bfloat16)
            later_copy[f][g][i].start()

    def reduce_added(f):
        add_on(f, 0)
        for i in range(2):
            plain_copy[f][1][i].start()
        add_on(f, 1)

    def summed(f, g, i):
        return (
            terms[f, block(0, g), half(i)].astype(jnp.float32)
            + added_in[f, g, i].astype(jnp.float32)
            + plain_in[f, g, 1 - i].astype(jnp.float32)
        )

    def wait_sums(f, g):
        for i in range(2):
            plain_copy[f][g][i].wait_recv()
            later_copy[f][g][i].wait_recv()

    def reduce_last(f):
        wait_sums(f, 0)
        for i in range(2):
            side[f, :, half(i)] = summed(f, 0, i).astype(jnp.bfloat16)
        side_copy[f].start()

    def reduce_end(f):
        wait_sums(f, 1)
        side_copy[f].wait_recv()
        for i in range(2):
            done = (summed(f, 1, i) + side_in[f, :, half(i)].astype(jnp.float32)).astype(
                jnp.bfloat16
            )
            for k in range(2):
                start = k * RUN + f * HALF
                out_ref[start : start + HALF, half(i)] = done[k * HALF : (k + 1) * HALF]

    def wait_all(*copies):
        for copy in copies:
            copy.wait_recv()

    def pass_on(arrival, *onward):
        arrival.wait_recv()
        for copy in onward:
            copy.start()

    def start_rest():
        wait_all(*own_core)
        own_up[1].start()
        own_down[1].start()

    before = [
        (0, start_rest),
        (1, lambda: wait_all(q_copy[0])),
        (2, lambda: wait_all(q_copy[1])),
        (3, lambda: pass_on(own_up[0], on_up, pass_12)),
        (3, lambda: pass_on(own_down[0], pass_4)),
        (4, lambda: wait_all(pass_12, pass_4)),
        (5, lambda: pass_on(own_down[1], on_down, pass_5)),
        (5, lambda: pass_on(own_up[1], pass_13)),
        (6, lambda: wait_all(pass_13, pass_5)),
        (7, lambda: pass_on(on_up, pass_8)),
        (7, lambda: pass_on(on_down, pass_9)),
        (8, lambda: wait_all(pass_8, pass_9)),
    ]
    after = [
        (9, lambda: finish_neighbour(0)),
        (11, lambda: combine(0)),
        (11, lambda: gather_own(0)),
        (12, lambda: gather_x(0)),
        (13, lambda: finish_neighbour(1)),
        (13, lambda: gather_y(0, 0)),
        (14, lambda: gather_y(0, 1)),
        (15, lambda: gather_y2(0, 0)),
    ]

    def run(events, u):
        for k in sorted({step for step, _ in events}):

            @pl.when(u == k)
            def _():
                for step, action in events:
                    if step == k:
                        action()

    def unit(u, carry):
        run(before, u)
        t = 2 * u
        score(t + 1, s1)
        weights, fade = weigh(t, s0)
        add_values(jnp.maximum(t - 1, 0), p1[...], fade1[...])
        score(jnp.minimum(t + 2, 31), s0)
        weights_1, fade_1 = weigh(t + 1, s1)
        add_values(t, weights, fade)
        p1[...] = weights_1
        fade1[...] = fade_1
        run(after, u)
        return carry

    p1[...] = jnp.zeros_like(p1)
    fade1[...] = jnp.ones_like(fade1)
    score(0, s0)
    lax.fori_loop(0, 16, unit, 0)
    add_values(31, p1[...], fade1[...])
    combine(1)
    gather_own(1)
    gather_y2(0, 1)
    w_copy.wait()
    gather_end(0)
    project(0, 0)
    gather_x(1)
    gather_y(1, 0)
    project(0, 1)
    gather_y(1, 1)
    gather_y2(1, 0)
    reduce_added(0)
    gather_y2(1, 1)
    gather_end(1)
    project(1, 0)
    project(1, 1)
    reduce_last(0)
    reduce_added(1)
    reduce_end(0)
    reduce_last(1)
    reduce_end(1)

    sent += side_copy
    for f in range(2):
        sent += gather_sent(f)
        for copies in far_copy[f] + plain_copy[f] + later_copy[f]:
            sent += copies
    for copy in sent:
        copy.wait_send()


def body(queries, key_cache, value_cache, out_weight):
    tokens, width = queries.shape
    cols = out_weight.shape[1]
    all_rows = tokens // 2 * lax.axis_size("ctx")
    vmem, anywhere = pl.BlockSpec(memory_space=pltpu.VMEM), pl.BlockSpec(memory_space=pl.ANY)
    bf16, f32 = jnp.bfloat16, jnp.float32
    piece = pltpu.VMEM((2, 2, 2, tokens, cols // 2), bf16)
    return pl.pallas_call(
        kernel,
        out_shape=jax.ShapeDtypeStruct((2 * tokens, cols), bf16),
        in_specs=[anywhere] * 4,
        out_specs=vmem,
        scratch_shapes=[
            pltpu.VMEM(queries.shape, bf16),
            pltpu.VMEM(key_cache.shape, bf16),
            pltpu.VMEM((4, ROWS, HD), bf16),
            pltpu.VMEM((16, 2 * KEYS, HD), bf16),
            pltpu.VMEM((ROWS, 2 * KEYS), f32),
            pltpu.VMEM((ROWS, 2 * KEYS), f32),
            pltpu.VMEM((ROWS, 2 * KEYS), bf16),
            pltpu.VMEM((ROWS, HD), f32),
            pltpu.VMEM((4, ROWS, 2 * HD), f32),
            pltpu.VMEM((4, ROWS, HD), f32),
            pltpu.VMEM((2, ROWS, HD), bf16),
            pltpu.VMEM((2, 8, ROWS), f32),
            pltpu.VMEM((2, ROWS, HD), bf16),
            pltpu.VMEM((2, 8, ROWS), f32),
            pltpu.VMEM((2, all_rows, width), bf16),
            pltpu.VMEM(out_weight.shape, bf16),
            pltpu.VMEM((2, all_rows, cols), bf16),
            piece,
            piece,
            piece,
            piece,
            pltpu.VMEM((2, tokens, cols), bf16),
            pltpu.VMEM((2, tokens, cols), bf16),
            pltpu.SemaphoreType.DMA((5,)),
            pltpu.SemaphoreType.DMA((S_COUNT,)),
            pltpu.SemaphoreType.DMA((S_COUNT,)),
        ],
        compiler_params=pltpu.CompilerParams(
            collective_id=0, has_side_effects=True, vmem_limit_bytes=56 * 1024 * 1024
        ),
        cost_estimate=pl.CostEstimate(
            flops=13_000_000_000, bytes_accessed=5_000_000, transcendentals=17_000_000
        ),
    )(queries, key_cache, value_cache, out_weight)


def solution(mesh):
    in_specs = (P("ctx", "head"), P("ctx", "head"), P("ctx", "head"), P("head", "ctx"))
    out_specs = P("head", "ctx")
    return jax.shard_map(body, mesh=mesh, in_specs=in_specs, out_specs=out_specs, check_vma=False)
```

```python
import math

import jax
import jax.numpy as jnp
from jax import lax
from jax.experimental import pallas as pl
from jax.experimental.pallas import tpu as pltpu
from jax.sharding import PartitionSpec as P

HD = 128
RUN = 64
NEG = -1e30
ROWS = 512
HALF = 32
KEYS = 512
LOG2E = math.log2(math.e)
MESH = pl.DeviceIdType.MESH

S_KV = 0
S_Q = 14
S_O = 16
S_STAT = 18
S_ATT = 20
S_FAR = 54
S_PLAIN = 62
S_LATER = 70
S_SIDE = 78
S_COUNT = 80


def device_at(x, y, core):
    return x * 8 + y * 2 + core


def kernel(
    q_hbm, k_hbm, v_hbm, w_hbm, out_ref,
    q_ref, k_ref, q_s, kv, s0, s1, p1, fade1, acc, mrow, o_send, s_send, o_recv, s_recv,
    att, w, terms, far_in, plain_in, added, added_in, side, side_in, fetched, send, recv,
):
    c, h = lax.axis_index("ctx"), lax.axis_index("head")
    x, y, core = c // 8, (c // 2) % 4, c % 2
    z, e = h // 2, h % 2
    scale = LOG2E / math.sqrt(HD)

    to_core = (device_at(x, y, 1 - core), h)
    to_up = (device_at(x, (y + 1) % 4, core), h)
    to_down = (device_at(x, (y + 3) % 4, core), h)
    to_x = (device_at(1 - x, y, core), h)
    z_ways = ((c, ((z + 1) % 4) * 2 + e), (c, ((z + 3) % 4) * 2 + e))
    to_side = (c, z * 2 + 1 - e)
    partners = (to_core, to_up, to_down, to_x, to_side) + z_ways

    def remote(src, dst, number, where):
        return pltpu.make_async_remote_copy(
            src_ref=src, dst_ref=dst, send_sem=send.at[number], recv_sem=recv.at[number],
            device_id=where, device_id_type=MESH,
        )

    q_fetch = pltpu.make_async_copy(q_hbm, q_ref, fetched.at[0])
    k_fetch = pltpu.make_async_copy(k_hbm, k_ref, fetched.at[1])
    v_fetch = [
        pltpu.make_async_copy(
            v_hbm.at[pl.ds(i * KEYS, KEYS)], kv.at[i, pl.ds(0, KEYS)], fetched.at[2 + i]
        )
        for i in range(2)
    ]
    w_copy = pltpu.make_async_copy(w_hbm, w, fetched.at[4])
    for fetch in [k_fetch, q_fetch] + v_fetch:
        fetch.start()
    barrier = pltpu.get_barrier_semaphore()
    for partner in partners:
        pl.semaphore_signal(barrier, inc=1, device_id=partner, device_id_type=MESH)

    k_fetch.wait()
    for half in range(2):
        for b in range(4):
            start = half * KEYS + b * HD
            piece = k_ref[start : start + HD].astype(jnp.float32)
            kv[half, KEYS + b * HD : KEYS + (b + 1) * HD] = piece.T.astype(jnp.bfloat16)
    q_fetch.wait()
    for r in range(2):
        for i in range(16):
            q_s[r, i * HALF : (i + 1) * HALF] = q_ref[
                r * HALF : (r + 1) * HALF, i * HD : (i + 1) * HD
            ]
    for fetch in v_fetch:
        fetch.wait()
    w_copy.start()
    pl.semaphore_wait(barrier, len(partners))

    def kv_copy(number, source, target, where):
        return remote(kv.at[source], kv.at[target], S_KV + number, where)

    own_up = [kv_copy(0 + i, i, 12 + i, to_up) for i in range(2)]
    own_down = [kv_copy(2 + i, i, 4 + i, to_down) for i in range(2)]
    own_core = [kv_copy(4 + i, i, 2 + i, to_core) for i in range(2)]
    pass_12 = kv_copy(6, 12, 14, to_core)
    pass_4 = kv_copy(7, 4, 6, to_core)
    pass_13 = kv_copy(8, 13, 15, to_core)
    pass_5 = kv_copy(9, 5, 7, to_core)
    on_up = kv_copy(10, 12, 8, to_up)
    on_down = kv_copy(11, 5, 9, to_down)
    pass_8 = kv_copy(12, 8, 10, to_core)
    pass_9 = kv_copy(13, 9, 11, to_core)
    q_copy = [remote(q_s.at[i], q_s.at[2 + i], S_Q + i, to_x) for i in range(2)]
    o_copy = [remote(o_send.at[f], o_recv.at[f], S_O + f, to_x) for f in range(2)]
    s_copy = [remote(s_send.at[f], s_recv.at[f], S_STAT + f, to_x) for f in range(2)]

    for i in range(2):
        own_core[i].start()
    q_copy[0].start()
    own_up[0].start()
    own_down[0].start()
    q_copy[1].start()
    for r in range(4):
        acc[r] = jnp.zeros((ROWS, 2 * HD), jnp.float32)
        mrow[r] = jnp.full((ROWS, HD), NEG, jnp.float32)

    def place(t):
        q = (t - 8) % 12
        early = jnp.where(q < 8, 2 + q // 2, 6 + q % 2)
        early_row = jnp.where(q < 8, q % 2, 1 - (q - 8) // 2) * 2
        pair = jnp.where(t < 8, t // 2 % 2, jnp.where(t < 20, early, 2 + q % 6))
        row = jnp.where(t < 8, t // 4 * 2 + t % 2, early_row)
        row = jnp.where(t < 20, row, (1 - q // 6) * 2 + 1)
        i = pair - 2
        middle = 12 + 2 * (i % 2) + i // 2
        one = jnp.where(pair < 2, 2 * pair, jnp.where(pair < 6, middle, 2 * pair - 4))
        two = jnp.where((pair >= 2) & (pair < 6), one - 8, one + 1)
        return one, two, row

    def score(t, s_ref):
        one, two, row = place(t)
        queries = q_s[row]
        for j, slot in enumerate((one, two)):
            keys = jnp.concatenate(
                [kv[slot, KEYS + b * HD : KEYS + (b + 1) * HD] for b in range(4)], axis=1
            )
            s_ref[:, j * KEYS : (j + 1) * KEYS] = (
                jnp.dot(queries, keys, preferred_element_type=jnp.float32) * scale
            )

    def weigh(t, s_ref):
        one, two, row = place(t)
        asker = device_at(jnp.where(row >= 2, 1 - x, x), y, core)
        token = lax.broadcasted_iota(jnp.int32, (ROWS, HD), 0) % HALF
        key_token = lax.broadcasted_iota(jnp.int32, (ROWS, HD), 1) - RUN
        pieces = []
        for j, slot in enumerate((one, two)):
            holder_core = jnp.where((slot // 2) % 2 == 1, 1 - core, core)
            holder = device_at(x, (y + slot // 4) % 4, holder_core)
            first = jnp.where(slot % 2 == 1, holder * RUN, -(1 << 20))
            limit = asker * RUN + (row % 2) * HALF - first
            end = (j + 1) * KEYS
            seen = (key_token < 0) | (key_token - token <= limit)
            pieces.append(s_ref[:, j * KEYS : end - HD])
            pieces.append(jnp.where(seen, s_ref[:, end - HD : end], NEG))
        scores = jnp.concatenate(pieces, axis=1)
        old = mrow[row]
        new = jnp.maximum(old, jnp.max(scores, axis=1, keepdims=True))
        weights = jnp.exp2(scores - jnp.concatenate([new] * (2 * KEYS // HD), axis=1))
        mrow[row] = new
        return weights.astype(jnp.bfloat16), jnp.exp2(old - new)

    def add_values(t, weights, fade):
        one, two, row = place(t)
        ones = jnp.ones((KEYS, HD), jnp.bfloat16)
        values = jnp.concatenate(
            [jnp.concatenate([kv[slot, 0:KEYS], ones], axis=1) for slot in (one, two)], axis=0
        )
        acc[row] = acc[row] * jnp.concatenate([fade, fade], axis=1) + jnp.dot(
            weights, values, preferred_element_type=jnp.float32
        )

    def normalised(row):
        total = acc[row, :, HD : 2 * HD]
        return acc[row, :, 0:HD] / total, mrow[row] + jnp.log(total) * LOG2E

    def finish_neighbour(f):
        value, level = normalised(2 + f)
        o_send[f] = value.astype(jnp.bfloat16)
        s_send[f] = level.T[0:8]
        o_copy[f].start()
        s_copy[f].start()

    def block_of(owner):
        start = owner * HALF
        return start if isinstance(start, int) else pl.multiple_of(start, HALF)

    def combine(f):
        value, level = normalised(f)
        o_copy[f].wait_recv()
        s_copy[f].wait_recv()
        other = jnp.broadcast_to(s_recv[f, 0:1], (HD, ROWS)).T
        top = jnp.maximum(level, other)
        part_a, part_b = jnp.exp2(level - top), jnp.exp2(other - top)
        done = (value * part_a + o_recv[f].astype(jnp.float32) * part_b) / (part_a + part_b)
        done = done.astype(jnp.bfloat16)
        for i in range(16):
            att[f, pl.ds(block_of(c), HALF), i * HD : (i + 1) * HD] = done[
                i * HALF : (i + 1) * HALF
            ]

    def gather_copy(f, number, dx, dy, where, part=None, from_core=None):
        owner = device_at(1 - x if dx else x, (y + dy) % 4, core if from_core is None else from_core)
        start, size = block_of(owner), HALF
        if part is not None:
            size = HALF // 2
            start = pl.multiple_of(start + part * size, size)
        block = att.at[f, pl.ds(start, size)]
        return remote(block, block, S_ATT + 17 * f + number, where)

    sent = own_up + own_down + own_core + [pass_12, pass_4, pass_13, pass_5, on_up, on_down]
    sent += [pass_8, pass_9] + q_copy + o_copy + s_copy

    def arrived(f, number, dx, dy, part=None, from_core=None):
        gather_copy(f, number, dx, dy, to_core, part, from_core).wait_recv()

    def gather_start(f, *args):
        gather_copy(f, *args).start()

    def gather_own(f):
        gather_start(f, 8, 0, 0, to_x)
        gather_start(f, 9, 0, 0, to_up)
        gather_start(f, 11, 0, 0, to_down)
        gather_start(f, 0, 0, 0, to_core)

    def gather_x(f):
        arrived(f, 8, 1, 0)
        gather_start(f, 10, 1, 0, to_up)
        gather_start(f, 12, 1, 0, to_down)
        gather_start(f, 4, 1, 0, to_core)

    def gather_y(f, plane):
        arrived(f, 9 + plane, plane, 3)
        gather_start(f, 13 + plane, plane, 3, to_up, 0)
        gather_start(f, 4 * plane + 3, plane, 3, to_core)
        arrived(f, 11 + plane, plane, 1)
        gather_start(f, 15 + plane, plane, 1, to_down, 1)
        gather_start(f, 4 * plane + 1, plane, 1, to_core)

    def gather_y2(f, plane):
        arrived(f, 13 + plane, plane, 2, 0)
        arrived(f, 15 + plane, plane, 2, 1)
        gather_start(f, 4 * plane + 2, plane, 2, to_core)

    def gather_end(f, planes=(0, 1)):
        for plane in planes:
            for dy in range(4):
                arrived(f, 4 * plane + dy, plane, dy, None, 1 - core)

    def gather_sent(f):
        copies = [gather_copy(f, 8, 0, 0, to_x)]
        for plane in range(2):
            copies += [gather_copy(f, 4 * plane + dy, plane, dy, to_core) for dy in range(4)]
            copies += [gather_copy(f, 9 + plane, plane, 0, to_up)]
            copies += [gather_copy(f, 11 + plane, plane, 0, to_down)]
            copies += [gather_copy(f, 13 + plane, plane, 3, to_up, 0)]
            copies += [gather_copy(f, 15 + plane, plane, 1, to_down, 1)]
        return copies

    cols = w.shape[1] // 2
    span = 2 * HALF

    def half(i):
        return pl.ds(i * cols, cols)

    def block(distance, g):
        side_of = e if g == 1 else 1 - e
        start = (((z + distance) % 4) * 2 + side_of) * span
        return pl.ds(pl.multiple_of(start, span), span)

    def z_copies(number, source_of, target):
        return [
            [
                [
                    remote(
                        source_of(f, g, i), target.at[f, g, i], number + 4 * f + 2 * g + i,
                        z_ways[i],
                    )
                    for i in range(2)
                ]
                for g in range(2)
            ]
            for f in range(2)
        ]

    far_copy = z_copies(S_FAR, lambda f, g, i: terms.at[f, block(2, g), half(i)], far_in)
    plain_copy = z_copies(
        S_PLAIN, lambda f, g, i: terms.at[f, block(1 + 2 * i, g), half(1 - i)], plain_in
    )
    later_copy = z_copies(S_LATER, lambda f, g, i: added.at[f, g, i], added_in)
    side_copy = [remote(side.at[f], side_in.at[f], S_SIDE + f, to_side) for f in range(2)]

    def project_plane(f, plane, i):
        size = att.shape[1] // 2
        rows = pl.ds(pl.multiple_of((1 - x if plane else x) * size, size), size)
        terms[f, rows, half(i)] = jnp.dot(
            att[f, rows], w[:, half(i)], preferred_element_type=jnp.float32
        ).astype(jnp.bfloat16)

    def project(f, i):
        terms[f, :, half(i)] = jnp.dot(
            att[f], w[:, half(i)], preferred_element_type=jnp.float32
        ).astype(jnp.bfloat16)
        send_products(f, i)

    def send_products(f, i):
        for g in range(2):
            far_copy[f][g][i].start()
        if i == 1:
            for j in range(2):
                plain_copy[f][0][j].start()

    def add_on(f, g):
        for i in range(2):
            far_copy[f][g][i].wait_recv()
            added[f, g, i] = (
                terms[f, block(1 + 2 * i, g), half(i)].astype(jnp.float32)
                + far_in[f, g, i].astype(jnp.float32)
            ).astype(jnp.bfloat16)
            later_copy[f][g][i].start()

    def reduce_added(f):
        add_on(f, 0)
        for i in range(2):
            plain_copy[f][1][i].start()
        add_on(f, 1)

    def summed(f, g, i):
        return (
            terms[f, block(0, g), half(i)].astype(jnp.float32)
            + added_in[f, g, i].astype(jnp.float32)
            + plain_in[f, g, 1 - i].astype(jnp.float32)
        )

    def wait_sums(f, g):
        for i in range(2):
            plain_copy[f][g][i].wait_recv()
            later_copy[f][g][i].wait_recv()

    def reduce_last(f):
        wait_sums(f, 0)
        for i in range(2):
            side[f, :, half(i)] = summed(f, 0, i).astype(jnp.bfloat16)
        side_copy[f].start()

    def reduce_end(f):
        wait_sums(f, 1)
        side_copy[f].wait_recv()
        for i in range(2):
            done = (summed(f, 1, i) + side_in[f, :, half(i)].astype(jnp.float32)).astype(
                jnp.bfloat16
            )
            for k in range(2):
                start = k * RUN + f * HALF
                out_ref[start : start + HALF, half(i)] = done[k * HALF : (k + 1) * HALF]

    def wait_all(*copies):
        for copy in copies:
            copy.wait_recv()

    def pass_on(arrival, *onward):
        arrival.wait_recv()
        for copy in onward:
            copy.start()

    def start_rest():
        wait_all(*own_core)
        own_up[1].start()
        own_down[1].start()

    before = [
        (0, start_rest),
        (1, lambda: wait_all(q_copy[0])),
        (2, lambda: wait_all(q_copy[1])),
        (3, lambda: pass_on(own_up[0], on_up, pass_12)),
        (3, lambda: pass_on(own_down[0], pass_4)),
        (4, lambda: wait_all(pass_12, pass_4)),
        (5, lambda: pass_on(own_down[1], on_down, pass_5)),
        (5, lambda: pass_on(own_up[1], pass_13)),
        (6, lambda: wait_all(pass_13, pass_5)),
        (7, lambda: pass_on(on_up, pass_8)),
        (7, lambda: pass_on(on_down, pass_9)),
        (8, lambda: wait_all(pass_8, pass_9)),
    ]
    after = [
        (9, lambda: finish_neighbour(0)),
        (11, lambda: combine(0)),
        (11, lambda: gather_own(0)),
        (12, lambda: gather_x(0)),
        (13, lambda: finish_neighbour(1)),
        (13, lambda: gather_y(0, 0)),
        (14, lambda: gather_y(0, 1)),
        (15, lambda: gather_y2(0, 0)),
    ]

    def run(events, u):
        for k in sorted({step for step, _ in events}):

            @pl.when(u == k)
            def _():
                for step, action in events:
                    if step == k:
                        action()

    def unit(u, carry):
        run(before, u)
        t = 2 * u
        score(t + 1, s1)
        weights, fade = weigh(t, s0)
        add_values(jnp.maximum(t - 1, 0), p1[...], fade1[...])
        score(jnp.minimum(t + 2, 31), s0)
        weights_1, fade_1 = weigh(t + 1, s1)
        add_values(t, weights, fade)
        p1[...] = weights_1
        fade1[...] = fade_1
        run(after, u)
        return carry

    p1[...] = jnp.zeros_like(p1)
    fade1[...] = jnp.ones_like(fade1)
    score(0, s0)
    lax.fori_loop(0, 16, unit, 0)
    add_values(31, p1[...], fade1[...])
    combine(1)
    gather_own(1)
    gather_y2(0, 1)
    w_copy.wait()
    gather_end(0)
    project(0, 0)
    gather_x(1)
    gather_y(1, 0)
    project(0, 1)
    gather_y(1, 1)
    gather_y2(1, 0)
    reduce_added(0)
    gather_end(1, (0,))
    project_plane(1, 0, 0)
    gather_y2(1, 1)
    project_plane(1, 0, 1)
    gather_end(1, (1,))
    for i in range(2):
        project_plane(1, 1, i)
        send_products(1, i)
    reduce_last(0)
    reduce_added(1)
    reduce_end(0)
    reduce_last(1)
    reduce_end(1)

    sent += side_copy
    for f in range(2):
        sent += gather_sent(f)
        for copies in far_copy[f] + plain_copy[f] + later_copy[f]:
            sent += copies
    for copy in sent:
        copy.wait_send()


def body(queries, key_cache, value_cache, out_weight):
    tokens, width = queries.shape
    cols = out_weight.shape[1]
    all_rows = tokens // 2 * lax.axis_size("ctx")
    vmem, anywhere = pl.BlockSpec(memory_space=pltpu.VMEM), pl.BlockSpec(memory_space=pl.ANY)
    bf16, f32 = jnp.bfloat16, jnp.float32
    piece = pltpu.VMEM((2, 2, 2, tokens, cols // 2), bf16)
    return pl.pallas_call(
        kernel,
        out_shape=jax.ShapeDtypeStruct((2 * tokens, cols), bf16),
        in_specs=[anywhere] * 4,
        out_specs=vmem,
        scratch_shapes=[
            pltpu.VMEM(queries.shape, bf16),
            pltpu.VMEM(key_cache.shape, bf16),
            pltpu.VMEM((4, ROWS, HD), bf16),
            pltpu.VMEM((16, 2 * KEYS, HD), bf16),
            pltpu.VMEM((ROWS, 2 * KEYS), f32),
            pltpu.VMEM((ROWS, 2 * KEYS), f32),
            pltpu.VMEM((ROWS, 2 * KEYS), bf16),
            pltpu.VMEM((ROWS, HD), f32),
            pltpu.VMEM((4, ROWS, 2 * HD), f32),
            pltpu.VMEM((4, ROWS, HD), f32),
            pltpu.VMEM((2, ROWS, HD), bf16),
            pltpu.VMEM((2, 8, ROWS), f32),
            pltpu.VMEM((2, ROWS, HD), bf16),
            pltpu.VMEM((2, 8, ROWS), f32),
            pltpu.VMEM((2, all_rows, width), bf16),
            pltpu.VMEM(out_weight.shape, bf16),
            pltpu.VMEM((2, all_rows, cols), bf16),
            piece,
            piece,
            piece,
            piece,
            pltpu.VMEM((2, tokens, cols), bf16),
            pltpu.VMEM((2, tokens, cols), bf16),
            pltpu.SemaphoreType.DMA((5,)),
            pltpu.SemaphoreType.DMA((S_COUNT,)),
            pltpu.SemaphoreType.DMA((S_COUNT,)),
        ],
        compiler_params=pltpu.CompilerParams(
            collective_id=0, has_side_effects=True, vmem_limit_bytes=56 * 1024 * 1024
        ),
        cost_estimate=pl.CostEstimate(
            flops=13_000_000_000, bytes_accessed=5_000_000, transcendentals=17_000_000
        ),
    )(queries, key_cache, value_cache, out_weight)


def solution(mesh):
    in_specs = (P("ctx", "head"), P("ctx", "head"), P("ctx", "head"), P("head", "ctx"))
    out_specs = P("head", "ctx")
    return jax.shard_map(body, mesh=mesh, in_specs=in_specs, out_specs=out_specs, check_vma=False)
```

```python
import math

import jax
import jax.numpy as jnp
from jax import lax
from jax.experimental import pallas as pl
from jax.experimental.pallas import tpu as pltpu
from jax.sharding import PartitionSpec as P

HD = 128
RUN = 64
NEG = -1e30
ROWS = 512
HALF = 32
KEYS = 512
LOG2E = math.log2(math.e)
MESH = pl.DeviceIdType.MESH

S_KV = 0
S_Q = 14
S_O = 16
S_STAT = 18
S_ATT = 20
S_FAR = 54
S_PLAIN = 62
S_LATER = 70
S_SIDE = 78
S_COUNT = 80


def device_at(x, y, core):
    return x * 8 + y * 2 + core


def kernel(
    q_hbm, k_hbm, v_hbm, w_hbm, out_ref,
    q_ref, k_ref, q_s, kv, s0, s1, p1, fade1, acc, mrow, o_send, s_send, o_recv, s_recv,
    att, w, terms, far_in, plain_in, added, added_in, side, side_in, fetched, send, recv,
):
    c, h = lax.axis_index("ctx"), lax.axis_index("head")
    x, y, core = c // 8, (c // 2) % 4, c % 2
    z, e = h // 2, h % 2
    scale = LOG2E / math.sqrt(HD)

    to_core = (device_at(x, y, 1 - core), h)
    to_up = (device_at(x, (y + 1) % 4, core), h)
    to_down = (device_at(x, (y + 3) % 4, core), h)
    to_x = (device_at(1 - x, y, core), h)
    z_ways = ((c, ((z + 1) % 4) * 2 + e), (c, ((z + 3) % 4) * 2 + e))
    to_side = (c, z * 2 + 1 - e)
    partners = (to_core, to_up, to_down, to_x, to_side) + z_ways

    def remote(src, dst, number, where):
        return pltpu.make_async_remote_copy(
            src_ref=src, dst_ref=dst, send_sem=send.at[number], recv_sem=recv.at[number],
            device_id=where, device_id_type=MESH,
        )

    q_fetch = pltpu.make_async_copy(q_hbm, q_ref, fetched.at[0])
    k_fetch = pltpu.make_async_copy(k_hbm, k_ref, fetched.at[1])
    v_fetch = [
        pltpu.make_async_copy(
            v_hbm.at[pl.ds(i * KEYS, KEYS)], kv.at[i, pl.ds(0, KEYS)], fetched.at[2 + i]
        )
        for i in range(2)
    ]
    w_copy = pltpu.make_async_copy(w_hbm, w, fetched.at[4])
    for fetch in [k_fetch, q_fetch] + v_fetch:
        fetch.start()
    barrier = pltpu.get_barrier_semaphore()
    for partner in partners:
        pl.semaphore_signal(barrier, inc=1, device_id=partner, device_id_type=MESH)

    k_fetch.wait()
    for half in range(2):
        for b in range(4):
            start = half * KEYS + b * HD
            piece = k_ref[start : start + HD].astype(jnp.float32)
            kv[half, KEYS + b * HD : KEYS + (b + 1) * HD] = piece.T.astype(jnp.bfloat16)
    q_fetch.wait()
    for r in range(2):
        for i in range(16):
            q_s[r, i * HALF : (i + 1) * HALF] = q_ref[
                r * HALF : (r + 1) * HALF, i * HD : (i + 1) * HD
            ]
    for fetch in v_fetch:
        fetch.wait()
    w_copy.start()
    pl.semaphore_wait(barrier, len(partners))

    def kv_copy(number, source, target, where):
        return remote(kv.at[source], kv.at[target], S_KV + number, where)

    own_up = [kv_copy(0 + i, i, 12 + i, to_up) for i in range(2)]
    own_down = [kv_copy(2 + i, i, 4 + i, to_down) for i in range(2)]
    own_core = [kv_copy(4 + i, i, 2 + i, to_core) for i in range(2)]
    pass_12 = kv_copy(6, 12, 14, to_core)
    pass_4 = kv_copy(7, 4, 6, to_core)
    pass_13 = kv_copy(8, 13, 15, to_core)
    pass_5 = kv_copy(9, 5, 7, to_core)
    on_up = kv_copy(10, 12, 8, to_up)
    on_down = kv_copy(11, 5, 9, to_down)
    pass_8 = kv_copy(12, 8, 10, to_core)
    pass_9 = kv_copy(13, 9, 11, to_core)
    q_copy = [remote(q_s.at[i], q_s.at[2 + i], S_Q + i, to_x) for i in range(2)]
    o_copy = [remote(o_send.at[f], o_recv.at[f], S_O + f, to_x) for f in range(2)]
    s_copy = [remote(s_send.at[f], s_recv.at[f], S_STAT + f, to_x) for f in range(2)]

    own_up[0].start()
    own_down[0].start()
    q_copy[0].start()
    for i in range(2):
        own_core[i].start()
    q_copy[1].start()
    own_up[1].start()
    own_down[1].start()
    for r in range(4):
        acc[r] = jnp.zeros((ROWS, 2 * HD), jnp.float32)
        mrow[r] = jnp.full((ROWS, HD), NEG, jnp.float32)

    def place(t):
        q = (t - 8) % 12
        early = jnp.where(q < 8, 2 + q // 2, 6 + q % 2)
        early_row = jnp.where(q < 8, q % 2, 1 - (q - 8) // 2) * 2
        pair = jnp.where(t < 8, t // 2 % 2, jnp.where(t < 20, early, 2 + q % 6))
        row = jnp.where(t < 8, t // 4 * 2 + t % 2, early_row)
        row = jnp.where(t < 20, row, (1 - q // 6) * 2 + 1)
        i = pair - 2
        middle = 12 + 2 * (i % 2) + i // 2
        one = jnp.where(pair < 2, 2 * pair, jnp.where(pair < 6, middle, 2 * pair - 4))
        two = jnp.where((pair >= 2) & (pair < 6), one - 8, one + 1)
        return one, two, row

    def score(t, s_ref):
        one, two, row = place(t)
        queries = q_s[row]
        for j, slot in enumerate((one, two)):
            keys = jnp.concatenate(
                [kv[slot, KEYS + b * HD : KEYS + (b + 1) * HD] for b in range(4)], axis=1
            )
            s_ref[:, j * KEYS : (j + 1) * KEYS] = (
                jnp.dot(queries, keys, preferred_element_type=jnp.float32) * scale
            )

    def weigh(t, s_ref):
        one, two, row = place(t)
        asker = device_at(jnp.where(row >= 2, 1 - x, x), y, core)
        token = lax.broadcasted_iota(jnp.int32, (ROWS, HD), 0) % HALF
        key_token = lax.broadcasted_iota(jnp.int32, (ROWS, HD), 1) - RUN
        pieces = []
        for j, slot in enumerate((one, two)):
            holder_core = jnp.where((slot // 2) % 2 == 1, 1 - core, core)
            holder = device_at(x, (y + slot // 4) % 4, holder_core)
            first = jnp.where(slot % 2 == 1, holder * RUN, -(1 << 20))
            limit = asker * RUN + (row % 2) * HALF - first
            end = (j + 1) * KEYS
            seen = (key_token < 0) | (key_token - token <= limit)
            pieces.append(s_ref[:, j * KEYS : end - HD])
            pieces.append(jnp.where(seen, s_ref[:, end - HD : end], NEG))
        scores = jnp.concatenate(pieces, axis=1)
        old = mrow[row]
        new = jnp.maximum(old, jnp.max(scores, axis=1, keepdims=True))
        weights = jnp.exp2(scores - jnp.concatenate([new] * (2 * KEYS // HD), axis=1))
        mrow[row] = new
        return weights.astype(jnp.bfloat16), jnp.exp2(old - new)

    def add_values(t, weights, fade):
        one, two, row = place(t)
        ones = jnp.ones((KEYS, HD), jnp.bfloat16)
        values = jnp.concatenate(
            [jnp.concatenate([kv[slot, 0:KEYS], ones], axis=1) for slot in (one, two)], axis=0
        )
        acc[row] = acc[row] * jnp.concatenate([fade, fade], axis=1) + jnp.dot(
            weights, values, preferred_element_type=jnp.float32
        )

    def normalised(row):
        total = acc[row, :, HD : 2 * HD]
        return acc[row, :, 0:HD] / total, mrow[row] + jnp.log(total) * LOG2E

    def finish_neighbour(f):
        value, level = normalised(2 + f)
        o_send[f] = value.astype(jnp.bfloat16)
        s_send[f] = level.T[0:8]
        o_copy[f].start()
        s_copy[f].start()

    def block_of(owner):
        start = owner * HALF
        return start if isinstance(start, int) else pl.multiple_of(start, HALF)

    def combine(f):
        value, level = normalised(f)
        o_copy[f].wait_recv()
        s_copy[f].wait_recv()
        other = jnp.broadcast_to(s_recv[f, 0:1], (HD, ROWS)).T
        top = jnp.maximum(level, other)
        part_a, part_b = jnp.exp2(level - top), jnp.exp2(other - top)
        done = (value * part_a + o_recv[f].astype(jnp.float32) * part_b) / (part_a + part_b)
        done = done.astype(jnp.bfloat16)
        for i in range(16):
            att[f, pl.ds(block_of(c), HALF), i * HD : (i + 1) * HD] = done[
                i * HALF : (i + 1) * HALF
            ]

    def gather_copy(f, number, dx, dy, where, part=None, from_core=None):
        owner = device_at(1 - x if dx else x, (y + dy) % 4, core if from_core is None else from_core)
        start, size = block_of(owner), HALF
        if part is not None:
            size = HALF // 2
            start = pl.multiple_of(start + part * size, size)
        block = att.at[f, pl.ds(start, size)]
        return remote(block, block, S_ATT + 17 * f + number, where)

    sent = own_up + own_down + own_core + [pass_12, pass_4, pass_13, pass_5, on_up, on_down]
    sent += [pass_8, pass_9] + q_copy + o_copy + s_copy

    def arrived(f, number, dx, dy, part=None, from_core=None):
        gather_copy(f, number, dx, dy, to_core, part, from_core).wait_recv()

    def gather_start(f, *args):
        gather_copy(f, *args).start()

    def gather_own(f):
        gather_start(f, 8, 0, 0, to_x)
        gather_start(f, 9, 0, 0, to_up)
        gather_start(f, 11, 0, 0, to_down)
        gather_start(f, 0, 0, 0, to_core)

    def gather_x(f):
        arrived(f, 8, 1, 0)
        gather_start(f, 10, 1, 0, to_up)
        gather_start(f, 12, 1, 0, to_down)
        gather_start(f, 4, 1, 0, to_core)

    def gather_y(f, plane):
        arrived(f, 9 + plane, plane, 3)
        gather_start(f, 13 + plane, plane, 3, to_up, 0)
        gather_start(f, 4 * plane + 3, plane, 3, to_core)
        arrived(f, 11 + plane, plane, 1)
        gather_start(f, 15 + plane, plane, 1, to_down, 1)
        gather_start(f, 4 * plane + 1, plane, 1, to_core)

    def gather_y2(f, plane):
        arrived(f, 13 + plane, plane, 2, 0)
        arrived(f, 15 + plane, plane, 2, 1)
        gather_start(f, 4 * plane + 2, plane, 2, to_core)

    def gather_end(f, planes=(0, 1)):
        for plane in planes:
            for dy in range(4):
                arrived(f, 4 * plane + dy, plane, dy, None, 1 - core)

    def gather_sent(f):
        copies = [gather_copy(f, 8, 0, 0, to_x)]
        for plane in range(2):
            copies += [gather_copy(f, 4 * plane + dy, plane, dy, to_core) for dy in range(4)]
            copies += [gather_copy(f, 9 + plane, plane, 0, to_up)]
            copies += [gather_copy(f, 11 + plane, plane, 0, to_down)]
            copies += [gather_copy(f, 13 + plane, plane, 3, to_up, 0)]
            copies += [gather_copy(f, 15 + plane, plane, 1, to_down, 1)]
        return copies

    cols = w.shape[1] // 2
    span = 2 * HALF

    def half(i):
        return pl.ds(i * cols, cols)

    def block(distance, g):
        side_of = e if g == 1 else 1 - e
        start = (((z + distance) % 4) * 2 + side_of) * span
        return pl.ds(pl.multiple_of(start, span), span)

    def z_copies(number, source_of, target):
        return [
            [
                [
                    remote(
                        source_of(f, g, i), target.at[f, g, i], number + 4 * f + 2 * g + i,
                        z_ways[i],
                    )
                    for i in range(2)
                ]
                for g in range(2)
            ]
            for f in range(2)
        ]

    far_copy = z_copies(S_FAR, lambda f, g, i: terms.at[f, block(2, g), half(i)], far_in)
    plain_copy = z_copies(
        S_PLAIN, lambda f, g, i: terms.at[f, block(1 + 2 * i, g), half(1 - i)], plain_in
    )
    later_copy = z_copies(S_LATER, lambda f, g, i: added.at[f, g, i], added_in)
    side_copy = [remote(side.at[f], side_in.at[f], S_SIDE + f, to_side) for f in range(2)]

    def project_plane(f, plane, i):
        size = att.shape[1] // 2
        rows = pl.ds(pl.multiple_of((1 - x if plane else x) * size, size), size)
        terms[f, rows, half(i)] = jnp.dot(
            att[f, rows], w[:, half(i)], preferred_element_type=jnp.float32
        ).astype(jnp.bfloat16)

    def project(f, i):
        terms[f, :, half(i)] = jnp.dot(
            att[f], w[:, half(i)], preferred_element_type=jnp.float32
        ).astype(jnp.bfloat16)
        send_products(f, i)

    def send_products(f, i):
        for g in range(2):
            far_copy[f][g][i].start()
        if i == 1:
            for j in range(2):
                plain_copy[f][0][j].start()

    def add_on(f, g):
        for i in range(2):
            far_copy[f][g][i].wait_recv()
            added[f, g, i] = (
                terms[f, block(1 + 2 * i, g), half(i)].astype(jnp.float32)
                + far_in[f, g, i].astype(jnp.float32)
            ).astype(jnp.bfloat16)
            later_copy[f][g][i].start()

    def reduce_added(f):
        add_on(f, 0)
        for i in range(2):
            plain_copy[f][1][i].start()
        add_on(f, 1)

    def summed(f, g, i):
        return (
            terms[f, block(0, g), half(i)].astype(jnp.float32)
            + added_in[f, g, i].astype(jnp.float32)
            + plain_in[f, g, 1 - i].astype(jnp.float32)
        )

    def wait_sums(f, g):
        for i in range(2):
            plain_copy[f][g][i].wait_recv()
            later_copy[f][g][i].wait_recv()

    def reduce_last(f):
        wait_sums(f, 0)
        for i in range(2):
            side[f, :, half(i)] = summed(f, 0, i).astype(jnp.bfloat16)
        side_copy[f].start()

    def reduce_end(f):
        wait_sums(f, 1)
        side_copy[f].wait_recv()
        for i in range(2):
            done = (summed(f, 1, i) + side_in[f, :, half(i)].astype(jnp.float32)).astype(
                jnp.bfloat16
            )
            for k in range(2):
                start = k * RUN + f * HALF
                out_ref[start : start + HALF, half(i)] = done[k * HALF : (k + 1) * HALF]

    def wait_all(*copies):
        for copy in copies:
            copy.wait_recv()

    def pass_on(arrival, *onward):
        arrival.wait_recv()
        for copy in onward:
            copy.start()

    def start_rest():
        wait_all(*own_core)

    before = [
        (0, start_rest),
        (1, lambda: wait_all(q_copy[0])),
        (2, lambda: wait_all(q_copy[1])),
        (3, lambda: pass_on(own_up[0], on_up, pass_12)),
        (3, lambda: pass_on(own_down[0], pass_4)),
        (4, lambda: wait_all(pass_12, pass_4)),
        (5, lambda: pass_on(own_down[1], on_down, pass_5)),
        (5, lambda: pass_on(own_up[1], pass_13)),
        (6, lambda: wait_all(pass_13, pass_5)),
        (7, lambda: pass_on(on_up, pass_8)),
        (7, lambda: pass_on(on_down, pass_9)),
        (8, lambda: wait_all(pass_8, pass_9)),
    ]
    after = [
        (9, lambda: finish_neighbour(0)),
        (11, lambda: combine(0)),
        (11, lambda: gather_own(0)),
        (12, lambda: gather_x(0)),
        (13, lambda: finish_neighbour(1)),
        (13, lambda: gather_y(0, 0)),
        (14, lambda: gather_y(0, 1)),
        (15, lambda: gather_y2(0, 0)),
    ]

    def run(events, u):
        for k in sorted({step for step, _ in events}):

            @pl.when(u == k)
            def _():
                for step, action in events:
                    if step == k:
                        action()

    def unit(u, carry):
        run(before, u)
        t = 2 * u
        score(t + 1, s1)
        weights, fade = weigh(t, s0)
        add_values(jnp.maximum(t - 1, 0), p1[...], fade1[...])
        score(jnp.minimum(t + 2, 31), s0)
        weights_1, fade_1 = weigh(t + 1, s1)
        add_values(t, weights, fade)
        p1[...] = weights_1
        fade1[...] = fade_1
        run(after, u)
        return carry

    p1[...] = jnp.zeros_like(p1)
    fade1[...] = jnp.ones_like(fade1)
    score(0, s0)
    lax.fori_loop(0, 16, unit, 0)
    add_values(31, p1[...], fade1[...])
    combine(1)
    gather_own(1)
    gather_y2(0, 1)
    w_copy.wait()
    gather_end(0)
    project(0, 0)
    gather_x(1)
    gather_y(1, 0)
    project(0, 1)
    gather_y(1, 1)
    gather_y2(1, 0)
    reduce_added(0)
    gather_end(1, (0,))
    project_plane(1, 0, 0)
    gather_y2(1, 1)
    project_plane(1, 0, 1)
    gather_end(1, (1,))
    for i in range(2):
        project_plane(1, 1, i)
        send_products(1, i)
    reduce_last(0)
    reduce_added(1)
    reduce_end(0)
    reduce_last(1)
    reduce_end(1)

    sent += side_copy
    for f in range(2):
        sent += gather_sent(f)
        for copies in far_copy[f] + plain_copy[f] + later_copy[f]:
            sent += copies
    for copy in sent:
        copy.wait_send()


def body(queries, key_cache, value_cache, out_weight):
    tokens, width = queries.shape
    cols = out_weight.shape[1]
    all_rows = tokens // 2 * lax.axis_size("ctx")
    vmem, anywhere = pl.BlockSpec(memory_space=pltpu.VMEM), pl.BlockSpec(memory_space=pl.ANY)
    bf16, f32 = jnp.bfloat16, jnp.float32
    piece = pltpu.VMEM((2, 2, 2, tokens, cols // 2), bf16)
    return pl.pallas_call(
        kernel,
        out_shape=jax.ShapeDtypeStruct((2 * tokens, cols), bf16),
        in_specs=[anywhere] * 4,
        out_specs=vmem,
        scratch_shapes=[
            pltpu.VMEM(queries.shape, bf16),
            pltpu.VMEM(key_cache.shape, bf16),
            pltpu.VMEM((4, ROWS, HD), bf16),
            pltpu.VMEM((16, 2 * KEYS, HD), bf16),
            pltpu.VMEM((ROWS, 2 * KEYS), f32),
            pltpu.VMEM((ROWS, 2 * KEYS), f32),
            pltpu.VMEM((ROWS, 2 * KEYS), bf16),
            pltpu.VMEM((ROWS, HD), f32),
            pltpu.VMEM((4, ROWS, 2 * HD), f32),
            pltpu.VMEM((4, ROWS, HD), f32),
            pltpu.VMEM((2, ROWS, HD), bf16),
            pltpu.VMEM((2, 8, ROWS), f32),
            pltpu.VMEM((2, ROWS, HD), bf16),
            pltpu.VMEM((2, 8, ROWS), f32),
            pltpu.VMEM((2, all_rows, width), bf16),
            pltpu.VMEM(out_weight.shape, bf16),
            pltpu.VMEM((2, all_rows, cols), bf16),
            piece,
            piece,
            piece,
            piece,
            pltpu.VMEM((2, tokens, cols), bf16),
            pltpu.VMEM((2, tokens, cols), bf16),
            pltpu.SemaphoreType.DMA((5,)),
            pltpu.SemaphoreType.DMA((S_COUNT,)),
            pltpu.SemaphoreType.DMA((S_COUNT,)),
        ],
        compiler_params=pltpu.CompilerParams(
            collective_id=0, has_side_effects=True, vmem_limit_bytes=56 * 1024 * 1024
        ),
        cost_estimate=pl.CostEstimate(
            flops=13_000_000_000, bytes_accessed=5_000_000, transcendentals=17_000_000
        ),
    )(queries, key_cache, value_cache, out_weight)


def solution(mesh):
    in_specs = (P("ctx", "head"), P("ctx", "head"), P("ctx", "head"), P("head", "ctx"))
    out_specs = P("head", "ctx")
    return jax.shard_map(body, mesh=mesh, in_specs=in_specs, out_specs=out_specs, check_vma=False)
```
